32 devices in a mesh: dp: 4 (over z), fsdp: 8 (over y, x, core).
Axes of the slice: x: 2, y: 2, z: 4, core: 2. Of those that a mesh axis runs over, the one named last changes fastest.
Arguments:
- inputs: bfloat16 [2048, 8192], P('dp', 'fsdp'), may hold values from -6 to 6
- cotangent: bfloat16 [2, 2048, 1024], P(None, 'dp', 'fsdp'), may hold values from -0.29882812 to 0.29882812
- feedback: float32 [2, 4, 8192, 1024], P(None, 'dp', 'fsdp'), may hold values from -6 to 6
- q_init: float32 [2, 1024, 128], replicated, may hold values from -0.1875 to 0.1875
- factor_ranks: int32 [2], replicated, may hold values from 8 to 128, as said below
Outputs:
- factor_p: float32 [2, 8192, 128], P(None, 'fsdp')
- factor_q: float32 [2, 1024, 128], replicated
- new_error: float32 [2, 4, 8192, 1024], P(None, 'dp', 'fsdp')
The draws below stay inside these ranges and needn't reach their ends.
Inputs may be any that keep to these rules, and one draw needn't show every extreme that they name: `factor_ranks`: some projection has rank 128.
All inputs are finite; a program needn't handle non-finite values.
Results may differ from the reference program's by a relative error of at most 0.0003.
Values may be sent and summed in bfloat16 or wider, within the bound.
No kernel may reach another device: no remote copies, remote signals or barrier semaphores. Data moves between devices by JAX's collectives and lax.ppermute only.
A program may use at most 64 MiB of HBM per device.

```python
import jax
import jax.numpy as jnp
from jax import lax

D = 8192
KV = 1024
RMAX = 128
TOK_DEV = 512
REPLICAS = 4
TOKENS = 2048
N_DP = 4


def draw_factor_ranks(key, part):
    subkeys = jax.random.split(jax.random.fold_in(key, 11), 2)
    other_ranks = jax.random.randint(subkeys[0], (2,), 8, RMAX + 1)
    chosen = jax.random.randint(subkeys[1], (), 0, 2)
    return jnp.where(jnp.arange(2) == chosen, RMAX, other_ranks).astype(jnp.int32)


def level_of(own_key, shape, pieces, least, top_value):
    level = 1.0
    for position, shards_of in pieces:
        heights = jax.random.uniform(jax.random.fold_in(jax.random.fold_in(own_key, 6), position), (shards_of,), jnp.float32, least / len(pieces), top_value / len(pieces))
        level = level * jnp.repeat(jnp.exp(heights), shape[position] // shards_of).reshape((-1,) + (1,) * (len(shape) - 1 - position))
    return level


def noise(key, shape, scale, reach, cuts=(), held_as=jnp.bfloat16):
    factor_of = level_of(key, shape, cuts, -0.22, 0.18) if cuts else 1.0
    drawn = jax.random.normal(key, shape, jnp.float32) * scale * factor_of
    return jnp.minimum(jnp.maximum(drawn, -reach), reach).astype(held_as)


def setup_inputs(seed: int = 0) -> dict:
    splits = jax.random.split(jax.random.key(seed), 6)
    return {
        "inputs": noise(splits[0], (TOKENS, D), 1.0, 6.0, ((0, 4), (1, 8))),
        "cotangent": noise(splits[1], (2, TOKENS, KV), 0.05, 0.29882812, ((1, 4), (2, 8))),
        "feedback": noise(splits[2], (2, REPLICAS, D, KV), 1.0, 6.0, ((1, 4), (2, 8)), jnp.float32),
        "q_init": noise(splits[3], (2, KV, RMAX), KV ** -0.5, 0.1875, (), jnp.float32),
        "factor_ranks": draw_factor_ranks(jax.random.fold_in(splits[5], 71), 0),
    }


PRECISE = lax.Precision.HIGHEST

def triangle_solve(lower_factor, right_side):
    return jax.scipy.linalg.solve_triangular(lower_factor, right_side, lower=True)

def reference(inputs, cotangent, feedback, q_init, factor_ranks):
    input_split = inputs.astype(jnp.float32).reshape(N_DP, TOK_DEV, D)
    cotan_split = cotangent.astype(jnp.float32).reshape(2, N_DP, TOK_DEV, KV)
    rank_mask = (jnp.arange(RMAX)[None, :] < factor_ranks[:, None]).astype(jnp.float32)
    masked_q = q_init * rank_mask[:, None, :]

    def full_of(replica):
        input_rows = lax.dynamic_index_in_dim(input_split, replica, 0, keepdims=False)
        cotan_rows = lax.dynamic_index_in_dim(cotan_split, replica, 1, keepdims=False)
        feedback_rows = lax.dynamic_index_in_dim(feedback, replica, 1, keepdims=False)
        return feedback_rows + jnp.einsum('td,mtk->mdk', input_rows, cotan_rows, precision=PRECISE)

    def add_left(running, replica):
        return (running + jnp.einsum('mdk,mkr->mdr', full_of(replica), masked_q, precision=PRECISE), None)
    left_sum, _ = lax.scan(add_left, jnp.zeros((2, D, RMAX), jnp.float32), jnp.arange(N_DP))
    gram_matrix = jnp.einsum('mdr,mds->mrs', left_sum, left_sum, precision=PRECISE)
    gram_matrix = gram_matrix + jax.vmap(jnp.diag)(1.0 - rank_mask)
    chol_lower = jnp.linalg.cholesky(gram_matrix)
    solved = jax.vmap(triangle_solve)(chol_lower, jnp.swapaxes(left_sum, 1, 2))
    factor_p = jnp.swapaxes(solved, 1, 2)

    def add_right(running, replica):
        return (running + jnp.einsum('mdk,mdr->mkr', full_of(replica), factor_p, precision=PRECISE), None)
    factor_q, _ = lax.scan(add_right, jnp.zeros((2, KV, RMAX), jnp.float32), jnp.arange(N_DP))
    low_rank = jnp.einsum('mdr,mkr->mdk', factor_p, factor_q, precision=PRECISE)
    per_replica = lax.map(lambda replica: full_of(replica) - low_rank, jnp.arange(N_DP))
    new_error = jnp.swapaxes(per_replica, 0, 1)
    return (factor_p, factor_q, new_error)
```

```python
import functools

import jax
import jax.numpy as jnp
from jax import lax
from jax.experimental import pallas as pl
from jax.experimental.pallas import tpu as pltpu
from jax.sharding import PartitionSpec as P

F32 = jnp.float32
BF16 = jnp.bfloat16
VMEM = pl.BlockSpec(memory_space=pltpu.VMEM)
SMEM = pl.BlockSpec(memory_space=pltpu.SMEM)
MIB = 1024 * 1024


def halves(x):
    high = x.astype(BF16)
    return high, (x - high.astype(F32)).astype(BF16)


def mm(a, b):
    return jnp.dot(a, b, preferred_element_type=F32)


def mm_nt(a, b):
    return lax.dot_general(a, b, (((1,), (1,)), ((), ())), preferred_element_type=F32)


def params(size, steps=1):
    return pltpu.CompilerParams(
        vmem_limit_bytes=size * MIB, dimension_semantics=("arbitrary",) * steps
    )


def tile_of(rows):
    return min(rows, 256)


def feedback_q_kernel(ranks_ref, fb_ref, q_ref, out_ref, q2_ref):
    m = pl.program_id(0)

    @pl.when(pl.program_id(1) == 0)
    def _():
        width = q_ref.shape[2]
        column = lax.broadcasted_iota(jnp.int32, q_ref.shape[1:], 1)
        q_high, q_low = halves(jnp.where(column < ranks_ref[m], q_ref[0], 0.0))
        q2_ref[:, :width] = q_high
        q2_ref[:, width:] = q_low

    width = q_ref.shape[2]
    high, low = halves(fb_ref[0, 0])
    both = mm(high, q2_ref[...])
    out_ref[0] = both[:, :width] + both[:, width:] + mm(low, q2_ref[:, :width])


def feedback_q(feedback, q_init, ranks):
    count, _, rows, columns = feedback.shape
    width = q_init.shape[2]
    tile = tile_of(rows)
    return pl.pallas_call(
        feedback_q_kernel,
        grid_spec=pltpu.PrefetchScalarGridSpec(
            num_scalar_prefetch=1,
            grid=(count, rows // tile),
            in_specs=[
                pl.BlockSpec((1, 1, tile, columns), lambda m, i, r: (m, 0, i, 0)),
                pl.BlockSpec((1, columns, width), lambda m, i, r: (m, 0, 0)),
            ],
            out_specs=pl.BlockSpec((1, tile, width), lambda m, i, r: (m, i, 0)),
            scratch_shapes=[pltpu.VMEM((columns, 2 * width), BF16)],
        ),
        out_shape=jax.ShapeDtypeStruct((count, rows, width), F32),
        compiler_params=params(24, 2),
        name="feedback_q",
    )(ranks, feedback, q_init)


def fill_cotangent(order_ref, cot_ref, whole_ref):
    blocks, width = cot_ref.shape[0], cot_ref.shape[3]
    for a in range(blocks):
        whole_ref[:, a * width : (a + 1) * width] = cot_ref[order_ref[a], 0]


def left_kernel(ranks_ref, order_ref, cot_ref, q_ref, in_ref, fbq_ref, out_ref, whole_ref):
    m = pl.program_id(0)
    width = q_ref.shape[2]
    fill_cotangent(order_ref, cot_ref, whole_ref)
    column = lax.broadcasted_iota(jnp.int32, q_ref.shape[1:], 1)
    q_high, q_low = halves(jnp.where(column < ranks_ref[m], q_ref[0], 0.0))
    both = mm(whole_ref[...], jnp.concatenate([q_high, q_low], axis=1))
    c_high, c_low = halves(both[:, :width] + both[:, width:])
    both = mm(in_ref[...], jnp.concatenate([c_high, c_low], axis=1))
    out_ref[0] = fbq_ref[0] + (both[:, :width] + both[:, width:])


def left(cot, order, q_init, inputs_t, fbq, ranks):
    count, rows, width = fbq.shape
    blocks, _, tokens, block = cot.shape
    columns = q_init.shape[1]
    return pl.pallas_call(
        left_kernel,
        grid_spec=pltpu.PrefetchScalarGridSpec(
            num_scalar_prefetch=2,
            grid=(count,),
            in_specs=[
                pl.BlockSpec((blocks, 1, tokens, block), lambda m, r, o: (0, m, 0, 0)),
                pl.BlockSpec((1, columns, width), lambda m, r, o: (m, 0, 0)),
                pl.BlockSpec((rows, tokens), lambda m, r, o: (0, 0)),
                pl.BlockSpec((1, rows, width), lambda m, r, o: (m, 0, 0)),
            ],
            out_specs=pl.BlockSpec((1, rows, width), lambda m, r, o: (m, 0, 0)),
            scratch_shapes=[pltpu.VMEM((tokens, columns), BF16)],
        ),
        out_shape=jax.ShapeDtypeStruct((count, rows, width), F32),
        compiler_params=params(24),
        name="left",
    )(ranks, order, cot, q_init, inputs_t, fbq)


def full_kernel(order_ref, cot_ref, in_ref, fb_ref, out_ref, whole_ref):
    @pl.when(pl.program_id(1) == 0)
    def _():
        fill_cotangent(order_ref, cot_ref, whole_ref)

    out_ref[0, 0] = fb_ref[0, 0] + mm(in_ref[...], whole_ref[...])


def full(cot, order, inputs_t, feedback):
    count, _, rows, columns = feedback.shape
    blocks, _, tokens, block = cot.shape
    tile = tile_of(rows)
    return pl.pallas_call(
        full_kernel,
        grid_spec=pltpu.PrefetchScalarGridSpec(
            num_scalar_prefetch=1,
            grid=(count, rows // tile),
            in_specs=[
                pl.BlockSpec((blocks, 1, tokens, block), lambda m, i, o: (0, m, 0, 0)),
                pl.BlockSpec((tile, tokens), lambda m, i, o: (i, 0)),
                pl.BlockSpec((1, 1, tile, columns), lambda m, i, o: (m, 0, i, 0)),
            ],
            out_specs=pl.BlockSpec((1, 1, tile, columns), lambda m, i, o: (m, 0, i, 0)),
            scratch_shapes=[pltpu.VMEM((tokens, columns), BF16)],
        ),
        out_shape=jax.ShapeDtypeStruct(feedback.shape, F32),
        compiler_params=params(24, 2),
        name="full",
    )(order, cot, inputs_t, feedback)


def right_kernel(full_ref, p_ref, out_ref):
    width = p_ref.shape[2]
    p_high, p_low = halves(p_ref[0].T)
    g_high, g_low = halves(full_ref[0, 0])
    both = mm(jnp.concatenate([p_high, p_low], axis=0), g_high)
    part = both[:width] + both[width:] + mm(p_high, g_low)

    @pl.when(pl.program_id(1) == 0)
    def _():
        out_ref[0] = part

    @pl.when(pl.program_id(1) > 0)
    def _():
        out_ref[0] += part


def right(full_grad, p):
    count, _, rows, columns = full_grad.shape
    width = p.shape[2]
    tile = tile_of(rows)
    return pl.pallas_call(
        right_kernel,
        grid=(count, rows // tile),
        in_specs=[
            pl.BlockSpec((1, 1, tile, columns), lambda m, i: (m, 0, i, 0)),
            pl.BlockSpec((1, tile, width), lambda m, i: (m, i, 0)),
        ],
        out_specs=pl.BlockSpec((1, width, columns), lambda m, i: (m, 0, 0)),
        out_shape=jax.ShapeDtypeStruct((count, width, columns), F32),
        compiler_params=params(24, 2),
        name="right",
    )(full_grad, p)


def gram_kernel(p_ref, out_ref):
    width = p_ref.shape[2]
    high, low = halves(p_ref[0])
    high_t, low_t = halves(p_ref[0].T)
    both = mm(high_t, jnp.concatenate([high, low], axis=1))
    out_ref[0] = both[:, :width] + both[:, width:] + mm(low_t, high)


def gram(p):
    count, rows, width = p.shape
    return pl.pallas_call(
        gram_kernel,
        grid=(count,),
        in_specs=[pl.BlockSpec((1, rows, width), lambda m: (m, 0, 0))],
        out_specs=pl.BlockSpec((1, width, width), lambda m: (m, 0, 0)),
        out_shape=jax.ShapeDtypeStruct((count, width, width), F32),
        compiler_params=params(24),
        name="gram",
    )(p)


def factor_kernel(ranks_ref, g_ref, p_ref, inv_ref, out_ref):
    count, n, _ = g_ref.shape
    lane = lax.broadcasted_iota(jnp.int32, (8, n), 1)
    sub = lax.broadcasted_iota(jnp.int32, (8, n), 0)
    work = []
    for m in range(count):
        free = jnp.where(lane < ranks_ref[m], 0.0, 1.0)
        blocks = []
        for b in range(n // 8):
            g = g_ref[m, 8 * b : 8 * b + 8, :]
            blocks.append(jnp.where(lane == sub + 8 * b, g + free, g))
        work.append(blocks)
    for k in range(n):
        top, s = divmod(k, 8)
        for blocks in work:
            row = jnp.broadcast_to(blocks[top][s : s + 1, :], (8, n))
            scale = lax.rsqrt(jnp.broadcast_to(row[:, k : k + 1], (8, n)))
            row = jnp.where(lane == k, scale, row * scale)
            for b in range(top, n // 8):
                x = blocks[b]
                times = jnp.broadcast_to(x[:, k : k + 1], (8, n)) * scale
                y = jnp.where(lane == k, 0.0, x) - times * row
                if b == top:
                    y = jnp.where(sub > s, y, jnp.where(sub == s, row, x))
                blocks[b] = y
    for m in range(count):
        for b in range(n // 8):
            inv_ref[m, 8 * b : 8 * b + 8, :] = jnp.where(lane <= sub + 8 * b, work[m][b], 0.0)
        i_high, i_low = halves(inv_ref[m])
        p_high, p_low = halves(p_ref[m])
        both = mm_nt(p_high, jnp.concatenate([i_high, i_low], axis=0))
        out_ref[m] = both[:, :n] + both[:, n:] + mm_nt(p_low, i_high)


def factor(gram_sum, p, ranks):
    return pl.pallas_call(
        factor_kernel,
        in_specs=[SMEM, VMEM, VMEM],
        out_specs=[VMEM, VMEM],
        out_shape=[
            jax.ShapeDtypeStruct(gram_sum.shape, F32),
            jax.ShapeDtypeStruct(p.shape, F32),
        ],
        compiler_params=pltpu.CompilerParams(vmem_limit_bytes=24 * MIB),
        name="factor",
    )(ranks, gram_sum, p)


def error_kernel(full_ref, fp_ref, inv_ref, rt_ref, err_ref, fq_ref, q3_ref):
    width = inv_ref.shape[1]

    @pl.when(pl.program_id(1) == 0)
    def _():
        i_high, i_low = halves(inv_ref[0])
        r_high, r_low = halves(rt_ref[0])
        both = mm(jnp.concatenate([i_high, i_low], axis=0), r_high)
        fq_t = both[:width] + both[width:] + mm(i_high, r_low)
        fq_ref[0] = fq_t.T
        q_high, q_low = halves(fq_t)
        q3_ref[:width] = q_high
        q3_ref[width : 2 * width] = q_high
        q3_ref[2 * width :] = q_low

    p_high, p_low = halves(fp_ref[0])
    low_rank = mm(jnp.concatenate([p_high, p_low, p_high], axis=1), q3_ref[...])
    err_ref[0, 0] = full_ref[0, 0] - low_rank


def error(full_grad, factor_p, inverse, rt):
    count, _, rows, columns = full_grad.shape
    width = rt.shape[1]
    tile = tile_of(rows)
    return pl.pallas_call(
        error_kernel,
        grid=(count, rows // tile),
        in_specs=[
            pl.BlockSpec((1, 1, tile, columns), lambda m, i: (m, 0, i, 0)),
            pl.BlockSpec((1, tile, width), lambda m, i: (m, i, 0)),
            pl.BlockSpec((1, width, width), lambda m, i: (m, 0, 0)),
            pl.BlockSpec((1, width, columns), lambda m, i: (m, 0, 0)),
        ],
        out_specs=[
            pl.BlockSpec((1, 1, tile, columns), lambda m, i: (m, 0, i, 0)),
            pl.BlockSpec((1, columns, width), lambda m, i: (m, 0, 0)),
        ],
        out_shape=[
            jax.ShapeDtypeStruct(full_grad.shape, F32),
            jax.ShapeDtypeStruct((count, columns, width), F32),
        ],
        scratch_shapes=[pltpu.VMEM((3 * width, columns), BF16)],
        compiler_params=params(24, 2),
        name="error",
    )(full_grad, factor_p, inverse, rt)


def power_of_two(n):
    return n & (n - 1) == 0


def across(x, axis, bit):
    size = lax.axis_size(axis)
    return lax.ppermute(x, axis, [(i, i ^ bit) for i in range(size)])


def bits_of(axis):
    size = lax.axis_size(axis)
    return [1 << b for b in range(size.bit_length() - 1)]


def gather_blocks(x, axis, split_axis):
    bits = bits_of(axis)
    held = {0: x}
    slow = bits[1:][::-1]
    while slow:
        if len(slow) >= 2:
            one, two = slow[:2]
            slow = slow[2:]
            keys = list(held)
            by_one = {r: across(held[r], axis, one) for r in keys}
            by_two = {r: across(held[r], axis, two) for r in keys}
            for r in keys:
                held[r ^ one] = by_one[r]
                held[r ^ two] = by_two[r]
                first, _ = jnp.split(by_two[r], 2, axis=split_axis)
                _, second = jnp.split(by_one[r], 2, axis=split_axis)
                held[r ^ one ^ two] = jnp.concatenate(
                    [across(first, axis, one), across(second, axis, two)], axis=split_axis
                )
        else:
            one = slow.pop()
            held.update({r ^ one: across(held[r], axis, one) for r in list(held)})
    held.update({r ^ 1: across(held[r], axis, 1) for r in list(held)})
    return [held[r] for r in range(len(held))]


def gather_cotangent(cotangent):
    size = lax.axis_size("fsdp")
    width = cotangent.shape[2]
    if power_of_two(size) and size > 1 and width % 128 == 0:
        blocks = gather_blocks(cotangent, "fsdp", 1)
        order = jnp.arange(size, dtype=jnp.int32) ^ lax.axis_index("fsdp")
        return jnp.stack(blocks), order
    whole = lax.all_gather(cotangent, "fsdp", axis=2, tiled=True)
    return whole[None], jnp.zeros((1,), jnp.int32)


def sum_dp(x):
    size = lax.axis_size("dp")
    if not (power_of_two(size) and size > 1):
        return lax.psum(x, "dp")
    bits = bits_of("dp")
    low = lax.axis_index("dp") & 1
    half = x.shape[1] // 2
    mine = lax.dynamic_slice_in_dim(x, low * half, half, 1)
    other = lax.dynamic_slice_in_dim(x, (1 - low) * half, half, 1)
    mine = mine + across(other, "dp", 1)
    for bit in bits[1:]:
        mine = mine + across(mine, "dp", bit)
    theirs = across(mine, "dp", 1)
    first = jnp.where(low == 0, mine, theirs)
    second = jnp.where(low == 0, theirs, mine)
    return jnp.concatenate([first, second], axis=1)


def sum_fsdp(x):
    size = lax.axis_size("fsdp")
    if not (power_of_two(size) and size > 1):
        return lax.psum(x, "fsdp")
    for bit in bits_of("fsdp"):
        x = x + across(x, "fsdp", bit)
    return x


def sum_all(x):
    size = lax.axis_size("fsdp")
    if not (power_of_two(size) and size > 1):
        rows = lax.psum_scatter(x, "fsdp", scatter_dimension=1, tiled=True)
        rows = lax.psum(rows, "dp")
        return lax.all_gather(rows, "fsdp", axis=1, tiled=True)
    me = lax.axis_index("fsdp")
    bits = bits_of("fsdp")
    for bit in bits:
        half = x.shape[1] // 2
        side = (me & bit) // bit
        mine = lax.dynamic_slice_in_dim(x, side * half, half, 1)
        other = lax.dynamic_slice_in_dim(x, (1 - side) * half, half, 1)
        x = mine + across(other, "fsdp", bit)
    if power_of_two(lax.axis_size("dp")):
        for bit in bits_of("dp"):
            x = x + across(x, "dp", bit)
    else:
        x = lax.psum(x, "dp")
    for bit in bits[::-1]:
        side = (me & bit) // bit
        theirs = across(x, "fsdp", bit)
        first = jnp.where(side == 0, x, theirs)
        second = jnp.where(side == 0, theirs, x)
        x = jnp.concatenate([first, second], axis=1)
    return x


def local(inputs, cotangent, feedback, q_init, factor_ranks):
    cot, order = gather_cotangent(cotangent)
    inputs_t = inputs.T
    fbq = feedback_q(feedback, q_init, factor_ranks)
    p = sum_dp(left(cot, order, q_init, inputs_t, fbq, factor_ranks))
    full_grad = full(cot, order, inputs_t, feedback)
    gram_sum = sum_fsdp(gram(p))
    rt = sum_all(right(full_grad, p))
    inverse, factor_p = factor(gram_sum, p, factor_ranks)
    new_error, factor_q = error(full_grad, factor_p, inverse, rt)
    return (factor_p, factor_q, new_error)


def solution(mesh):
    placed = (P("dp", "fsdp"), P(None, "dp", "fsdp"), P(None, "dp", "fsdp", None), P(), P())
    return jax.shard_map(
        local,
        mesh=mesh,
        in_specs=placed,
        out_specs=(P(None, "fsdp", None), P(), P(None, "dp", "fsdp", None)),
        check_vma=False,
    )
```

```python
import functools

import jax
import jax.numpy as jnp
from jax import lax
from jax.experimental import pallas as pl
from jax.experimental.pallas import tpu as pltpu
from jax.sharding import PartitionSpec as P

F32 = jnp.float32
BF16 = jnp.bfloat16
VMEM = pl.BlockSpec(memory_space=pltpu.VMEM)
SMEM = pl.BlockSpec(memory_space=pltpu.SMEM)
MIB = 1024 * 1024


def halves(x):
    high = x.astype(BF16)
    return high, (x - high.astype(F32)).astype(BF16)


def mm(a, b):
    return jnp.dot(a, b, preferred_element_type=F32)


def mm_nt(a, b):
    return lax.dot_general(a, b, (((1,), (1,)), ((), ())), preferred_element_type=F32)


def params(size, steps=1):
    return pltpu.CompilerParams(
        vmem_limit_bytes=size * MIB, dimension_semantics=("arbitrary",) * steps
    )


def tile_of(rows):
    return min(rows, 256)


def feedback_q_kernel(ranks_ref, fb_ref, q_ref, out_ref, q2_ref):
    m = pl.program_id(0)

    @pl.when(pl.program_id(1) == 0)
    def _():
        width = q_ref.shape[2]
        column = lax.broadcasted_iota(jnp.int32, q_ref.shape[1:], 1)
        q_high, q_low = halves(jnp.where(column < ranks_ref[m], q_ref[0], 0.0))
        q2_ref[:, :width] = q_high
        q2_ref[:, width:] = q_low

    width = q_ref.shape[2]
    high, low = halves(fb_ref[0, 0])
    both = mm(high, q2_ref[...])
    out_ref[0] = both[:, :width] + both[:, width:] + mm(low, q2_ref[:, :width])


def feedback_q(feedback, q_init, ranks):
    count, _, rows, columns = feedback.shape
    width = q_init.shape[2]
    tile = tile_of(rows)
    return pl.pallas_call(
        feedback_q_kernel,
        grid_spec=pltpu.PrefetchScalarGridSpec(
            num_scalar_prefetch=1,
            grid=(count, rows // tile),
            in_specs=[
                pl.BlockSpec((1, 1, tile, columns), lambda m, i, r: (m, 0, i, 0)),
                pl.BlockSpec((1, columns, width), lambda m, i, r: (m, 0, 0)),
            ],
            out_specs=pl.BlockSpec((1, tile, width), lambda m, i, r: (m, i, 0)),
            scratch_shapes=[pltpu.VMEM((columns, 2 * width), BF16)],
        ),
        out_shape=jax.ShapeDtypeStruct((count, rows, width), F32),
        compiler_params=params(56, 2),
        name="feedback_q",
    )(ranks, feedback, q_init)


def fill_cotangent(order_ref, cot_ref, whole_ref):
    blocks, width = cot_ref.shape[0], cot_ref.shape[3]
    for a in range(blocks):
        whole_ref[:, a * width : (a + 1) * width] = cot_ref[order_ref[a], 0]


def left_kernel(ranks_ref, order_ref, cot_ref, q_ref, in_ref, fbq_ref, out_ref, whole_ref):
    m = pl.program_id(0)
    width = q_ref.shape[2]
    fill_cotangent(order_ref, cot_ref, whole_ref)
    column = lax.broadcasted_iota(jnp.int32, q_ref.shape[1:], 1)
    q_high, q_low = halves(jnp.where(column < ranks_ref[m], q_ref[0], 0.0))
    both = mm(whole_ref[...], jnp.concatenate([q_high, q_low], axis=1))
    c_high, c_low = halves(both[:, :width] + both[:, width:])
    both = mm(in_ref[...], jnp.concatenate([c_high, c_low], axis=1))
    out_ref[0] = fbq_ref[0] + (both[:, :width] + both[:, width:])


def left(cot, order, q_init, inputs_t, fbq, ranks):
    count, rows, width = fbq.shape
    blocks, _, tokens, block = cot.shape
    columns = q_init.shape[1]
    return pl.pallas_call(
        left_kernel,
        grid_spec=pltpu.PrefetchScalarGridSpec(
            num_scalar_prefetch=2,
            grid=(count,),
            in_specs=[
                pl.BlockSpec((blocks, 1, tokens, block), lambda m, r, o: (0, m, 0, 0)),
                pl.BlockSpec((1, columns, width), lambda m, r, o: (m, 0, 0)),
                pl.BlockSpec((rows, tokens), lambda m, r, o: (0, 0)),
                pl.BlockSpec((1, rows, width), lambda m, r, o: (m, 0, 0)),
            ],
            out_specs=pl.BlockSpec((1, rows, width), lambda m, r, o: (m, 0, 0)),
            scratch_shapes=[pltpu.VMEM((tokens, columns), BF16)],
        ),
        out_shape=jax.ShapeDtypeStruct((count, rows, width), F32),
        compiler_params=params(32),
        name="left",
    )(ranks, order, cot, q_init, inputs_t, fbq)


GROUPS = 16


def encode(x, out_ref):
    rows, width = x.shape
    grouped = x.reshape(GROUPS, rows // GROUPS, width)
    top = jnp.max(jnp.abs(grouped), axis=1)
    level = jnp.ceil(jnp.log(jnp.maximum(top, 1e-30)) * 32.0) + 1.0
    up = jnp.exp(level * (-1.0 / 32.0)) * 32767.0
    code = jnp.round(grouped * up[:, None, :]).reshape(rows, width)
    out_ref[:rows] = code.astype(jnp.int32).astype(jnp.int16)
    out_ref[rows:] = level.astype(jnp.int32).astype(jnp.int16)


def decode(ref):
    rows = ref.shape[0] - GROUPS
    width = ref.shape[1]
    level = ref[rows:].astype(jnp.int32).astype(F32)
    down = jnp.exp(level * (1.0 / 32.0)) * (1.0 / 32767.0)
    code = ref[:rows].astype(jnp.int32).astype(F32).reshape(GROUPS, rows // GROUPS, width)
    return (code * down[:, None, :]).reshape(rows, width)


def left_code_kernel(
    m, ranks_ref, order_ref, low_ref, cot_ref, q_ref, in_ref, fbq_ref, mine_ref, code_ref, whole_ref, p_ref
):
    width = q_ref.shape[2]
    fill_cotangent(order_ref, cot_ref, whole_ref)
    column = lax.broadcasted_iota(jnp.int32, q_ref.shape[1:], 1)
    q_high, q_low = halves(jnp.where(column < ranks_ref[m], q_ref[0], 0.0))
    both = mm(whole_ref[...], jnp.concatenate([q_high, q_low], axis=1))
    c_high, c_low = halves(both[:, :width] + both[:, width:])
    both = mm(in_ref[...], jnp.concatenate([c_high, c_low], axis=1))
    p_ref[...] = (fbq_ref[0] + (both[:, :width] + both[:, width:])).reshape(p_ref.shape)
    mine_ref[...] = p_ref[low_ref[0]]
    encode(p_ref[1 - low_ref[0]], code_ref)


def left_code(m, cot, order, low, q_init, inputs_t, fbq, ranks):
    count, rows, width = fbq.shape
    blocks, _, tokens, block = cot.shape
    columns = q_init.shape[1]
    half = rows // 2
    return pl.pallas_call(
        functools.partial(left_code_kernel, m),
        grid_spec=pltpu.PrefetchScalarGridSpec(
            num_scalar_prefetch=3,
            grid=(1,),
            in_specs=[
                pl.BlockSpec((blocks, 1, tokens, block), lambda i, *_: (0, m, 0, 0)),
                pl.BlockSpec((1, columns, width), lambda i, *_: (m, 0, 0)),
                pl.BlockSpec((rows, tokens), lambda i, *_: (0, 0)),
                pl.BlockSpec((1, rows, width), lambda i, *_: (m, 0, 0)),
            ],
            out_specs=[
                pl.BlockSpec((half, width), lambda i, *_: (0, 0)),
                pl.BlockSpec((half + GROUPS, width), lambda i, *_: (0, 0)),
            ],
            scratch_shapes=[
                pltpu.VMEM((tokens, columns), BF16),
                pltpu.VMEM((2, half, width), F32),
            ],
        ),
        out_shape=[
            jax.ShapeDtypeStruct((half, width), F32),
            jax.ShapeDtypeStruct((half + GROUPS, width), jnp.int16),
        ],
        compiler_params=params(32),
        name=f"left_code_{m}",
    )(ranks, order, low, cot, q_init, inputs_t, fbq)


def add_kernel(mine_ref, theirs_ref, out_ref):
    mine = mine_ref[...] if mine_ref.dtype == F32 else decode(mine_ref)
    encode(mine + decode(theirs_ref), out_ref)


def add_code(mine, theirs):
    return pl.pallas_call(
        add_kernel,
        in_specs=[VMEM, VMEM],
        out_specs=VMEM,
        out_shape=jax.ShapeDtypeStruct(theirs.shape, jnp.int16),
        compiler_params=pltpu.CompilerParams(vmem_limit_bytes=32 * MIB),
        name="add_code",
    )(mine, theirs)


def whole_left_kernel(low_ref, mine_ref, theirs_ref, p_ref, gram_ref):
    half, width = mine_ref.shape[0] - GROUPS, mine_ref.shape[1]
    low = low_ref[0]
    p_ref[pl.ds(pl.multiple_of(low * half, half), half)] = decode(mine_ref)
    p_ref[pl.ds(pl.multiple_of((1 - low) * half, half), half)] = decode(theirs_ref)
    gram_ref[...] = gram_of(p_ref[...])


def whole_left(low, mine, theirs):
    half, width = mine.shape[0] - GROUPS, mine.shape[1]
    return pl.pallas_call(
        whole_left_kernel,
        in_specs=[SMEM, VMEM, VMEM],
        out_specs=[VMEM, VMEM],
        out_shape=[
            jax.ShapeDtypeStruct((2 * half, width), F32),
            jax.ShapeDtypeStruct((width, width), F32),
        ],
        compiler_params=pltpu.CompilerParams(vmem_limit_bytes=32 * MIB),
        name="whole_left",
    )(low, mine, theirs)


def full_kernel(order_ref, cot_ref, in_ref, fb_ref, out_ref, whole_ref):
    @pl.when(pl.program_id(1) == 0)
    def _():
        fill_cotangent(order_ref, cot_ref, whole_ref)

    out_ref[0, 0] = fb_ref[0, 0] + mm(in_ref[...], whole_ref[...])


def full(cot, order, inputs_t, feedback):
    count, _, rows, columns = feedback.shape
    blocks, _, tokens, block = cot.shape
    tile = tile_of(rows)
    return pl.pallas_call(
        full_kernel,
        grid_spec=pltpu.PrefetchScalarGridSpec(
            num_scalar_prefetch=1,
            grid=(count, rows // tile),
            in_specs=[
                pl.BlockSpec((blocks, 1, tokens, block), lambda m, i, o: (0, m, 0, 0)),
                pl.BlockSpec((tile, tokens), lambda m, i, o: (i, 0)),
                pl.BlockSpec((1, 1, tile, columns), lambda m, i, o: (m, 0, i, 0)),
            ],
            out_specs=pl.BlockSpec((1, 1, tile, columns), lambda m, i, o: (m, 0, i, 0)),
            scratch_shapes=[pltpu.VMEM((tokens, columns), BF16)],
        ),
        out_shape=jax.ShapeDtypeStruct(feedback.shape, F32),
        compiler_params=params(56, 2),
        name="full",
    )(order, cot, inputs_t, feedback)


def right_kernel(full_ref, p_ref, out_ref):
    width = p_ref.shape[1]
    p_high, p_low = halves(p_ref[...].T)
    g_high, g_low = halves(full_ref[0, 0])
    both = mm(jnp.concatenate([p_high, p_low], axis=0), g_high)
    part = both[:width] + both[width:] + mm(p_high, g_low)

    @pl.when(pl.program_id(0) == 0)
    def _():
        out_ref[...] = part

    @pl.when(pl.program_id(0) > 0)
    def _():
        out_ref[...] += part


def right(m, full_grad, p):
    _, _, rows, columns = full_grad.shape
    width = p.shape[1]
    tile = tile_of(rows)
    return pl.pallas_call(
        right_kernel,
        grid=(rows // tile,),
        in_specs=[
            pl.BlockSpec((1, 1, tile, columns), lambda i: (m, 0, i, 0)),
            pl.BlockSpec((tile, width), lambda i: (i, 0)),
        ],
        out_specs=pl.BlockSpec((width, columns), lambda i: (0, 0)),
        out_shape=jax.ShapeDtypeStruct((width, columns), F32),
        compiler_params=params(56),
        name=f"right_{m}",
    )(full_grad, p)


def gram_of(p):
    width = p.shape[1]
    high, low = halves(p)
    high_t, low_t = halves(p.T)
    both = mm(high_t, jnp.concatenate([high, low], axis=1))
    return both[:, :width] + both[:, width:] + mm(low_t, high)


def gram_kernel(p_ref, out_ref):
    out_ref[0] = gram_of(p_ref[0])


def gram(p):
    count, rows, width = p.shape
    return pl.pallas_call(
        gram_kernel,
        grid=(count,),
        in_specs=[pl.BlockSpec((1, rows, width), lambda m: (m, 0, 0))],
        out_specs=pl.BlockSpec((1, width, width), lambda m: (m, 0, 0)),
        out_shape=jax.ShapeDtypeStruct((count, width, width), F32),
        compiler_params=params(32),
        name="gram",
    )(p)


def factor_kernel(ranks_ref, g_ref, p_ref, inv_ref, out_ref):
    count, n, _ = g_ref.shape
    lane = lax.broadcasted_iota(jnp.int32, (8, n), 1)
    sub = lax.broadcasted_iota(jnp.int32, (8, n), 0)
    work = []
    for m in range(count):
        free = jnp.where(lane < ranks_ref[m], 0.0, 1.0)
        blocks = []
        for b in range(n // 8):
            g = g_ref[m, 8 * b : 8 * b + 8, :]
            blocks.append(jnp.where(lane == sub + 8 * b, g + free, g))
        work.append(blocks)
    for k in range(n):
        top, s = divmod(k, 8)
        for blocks in work:
            row = jnp.broadcast_to(blocks[top][s : s + 1, :], (8, n))
            scale = lax.rsqrt(jnp.broadcast_to(row[:, k : k + 1], (8, n)))
            row = jnp.where(lane == k, scale, row * scale)
            for b in range(top, n // 8):
                x = blocks[b]
                times = jnp.broadcast_to(x[:, k : k + 1], (8, n)) * scale
                y = jnp.where(lane == k, 0.0, x) - times * row
                if b == top:
                    y = jnp.where(sub > s, y, jnp.where(sub == s, row, x))
                blocks[b] = y
    for m in range(count):
        for b in range(n // 8):
            inv_ref[m, 8 * b : 8 * b + 8, :] = jnp.where(lane <= sub + 8 * b, work[m][b], 0.0)
        i_high, i_low = halves(inv_ref[m])
        p_high, p_low = halves(p_ref[m])
        both = mm_nt(p_high, jnp.concatenate([i_high, i_low], axis=0))
        out_ref[m] = both[:, :n] + both[:, n:] + mm_nt(p_low, i_high)


def factor(gram_sum, p, ranks):
    return pl.pallas_call(
        factor_kernel,
        in_specs=[SMEM, VMEM, VMEM],
        out_specs=[VMEM, VMEM],
        out_shape=[
            jax.ShapeDtypeStruct(gram_sum.shape, F32),
            jax.ShapeDtypeStruct(p.shape, F32),
        ],
        compiler_params=pltpu.CompilerParams(vmem_limit_bytes=24 * MIB),
        name="factor",
    )(ranks, gram_sum, p)


def error_kernel(full_ref, fp_ref, inv_ref, rt_ref, err_ref, fq_ref, q3_ref):
    width = inv_ref.shape[1]

    @pl.when(pl.program_id(1) == 0)
    def _():
        i_high, i_low = halves(inv_ref[0])
        r_high, r_low = halves(rt_ref[0])
        both = mm(jnp.concatenate([i_high, i_low], axis=0), r_high)
        fq_t = both[:width] + both[width:] + mm(i_high, r_low)
        fq_ref[0] = fq_t.T
        q_high, q_low = halves(fq_t)
        q3_ref[:width] = q_high
        q3_ref[width : 2 * width] = q_high
        q3_ref[2 * width :] = q_low

    p_high, p_low = halves(fp_ref[0])
    low_rank = mm(jnp.concatenate([p_high, p_low, p_high], axis=1), q3_ref[...])
    err_ref[0, 0] = full_ref[0, 0] - low_rank


def error(full_grad, factor_p, inverse, rt):
    count, _, rows, columns = full_grad.shape
    width = rt.shape[1]
    tile = tile_of(rows)
    return pl.pallas_call(
        error_kernel,
        grid=(count, rows // tile),
        in_specs=[
            pl.BlockSpec((1, 1, tile, columns), lambda m, i: (m, 0, i, 0)),
            pl.BlockSpec((1, tile, width), lambda m, i: (m, i, 0)),
            pl.BlockSpec((1, width, width), lambda m, i: (m, 0, 0)),
            pl.BlockSpec((1, width, columns), lambda m, i: (m, 0, 0)),
        ],
        out_specs=[
            pl.BlockSpec((1, 1, tile, columns), lambda m, i: (m, 0, i, 0)),
            pl.BlockSpec((1, columns, width), lambda m, i: (m, 0, 0)),
        ],
        out_shape=[
            jax.ShapeDtypeStruct(full_grad.shape, F32),
            jax.ShapeDtypeStruct((count, columns, width), F32),
        ],
        scratch_shapes=[pltpu.VMEM((3 * width, columns), BF16)],
        compiler_params=params(56, 2),
        name="error",
    )(full_grad, factor_p, inverse, rt)


def power_of_two(n):
    return n & (n - 1) == 0


def across(x, axis, bit):
    size = lax.axis_size(axis)
    return lax.ppermute(x, axis, [(i, i ^ bit) for i in range(size)])


def bits_of(axis):
    size = lax.axis_size(axis)
    return [1 << b for b in range(size.bit_length() - 1)]


def gather_blocks(x, axis, split_axis):
    bits = bits_of(axis)
    held = {0: x}
    slow = bits[1:][::-1]
    while slow:
        if len(slow) >= 2:
            one, two = slow[:2]
            slow = slow[2:]
            keys = list(held)
            by_one = {r: across(held[r], axis, one) for r in keys}
            by_two = {r: across(held[r], axis, two) for r in keys}
            for r in keys:
                held[r ^ one] = by_one[r]
                held[r ^ two] = by_two[r]
                first, _ = jnp.split(by_two[r], 2, axis=split_axis)
                _, second = jnp.split(by_one[r], 2, axis=split_axis)
                held[r ^ one ^ two] = jnp.concatenate(
                    [across(first, axis, one), across(second, axis, two)], axis=split_axis
                )
        else:
            one = slow.pop()
            held.update({r ^ one: across(held[r], axis, one) for r in list(held)})
    held.update({r ^ 1: across(held[r], axis, 1) for r in list(held)})
    return [held[r] for r in range(len(held))]


def gather_cotangent(cotangent):
    size = lax.axis_size("fsdp")
    width = cotangent.shape[2]
    if power_of_two(size) and size > 1 and width % 128 == 0:
        blocks = gather_blocks(cotangent, "fsdp", 1)
        order = jnp.arange(size, dtype=jnp.int32) ^ lax.axis_index("fsdp")
        return jnp.stack(blocks), order
    whole = lax.all_gather(cotangent, "fsdp", axis=2, tiled=True)
    return whole[None], jnp.zeros((1,), jnp.int32)


def cut(x, side, bit, axis):
    half = x.shape[axis] // 2
    mine = lax.dynamic_slice_in_dim(x, side * half, half, axis)
    other = lax.dynamic_slice_in_dim(x, (1 - side) * half, half, axis)
    return mine, other


def side_of(bit):
    return (lax.axis_index("fsdp") & bit) // bit


def halve(x, bit):
    mine, other = cut(x, side_of(bit), bit, 1)
    return mine + across(other, "fsdp", bit)


def unhalve(x, bit):
    theirs = across(x, "fsdp", bit)
    side = side_of(bit)
    first = jnp.where(side == 0, x, theirs)
    second = jnp.where(side == 0, theirs, x)
    return jnp.concatenate([first, second], axis=1)


def scatter_sum(x, bits):
    if not bits:
        return x
    if len(bits) == 1 or x.shape[1] < 8:
        return scatter_sum(halve(x, bits[0]), bits[1:])
    one, two = bits[:2]
    a, b = jnp.split(x, 2, axis=1)
    a, b = halve(a, one), halve(b, two)
    a, b = halve(a, two), halve(b, one)
    return scatter_sum(jnp.concatenate([a, b], axis=1), bits[2:])


def gather_sum(x, bits, rows):
    if not bits:
        return x
    if len(bits) == 1 or rows < 8:
        return unhalve(gather_sum(x, bits[1:], rows // 2), bits[0])
    one, two = bits[:2]
    a, b = jnp.split(gather_sum(x, bits[2:], rows // 4), 2, axis=1)
    a, b = unhalve(a, two), unhalve(b, one)
    a, b = unhalve(a, one), unhalve(b, two)
    return jnp.concatenate([a, b], axis=1)


def tie(*values):
    return lax.optimization_barrier(values)


def sums(gram_part, rt_parts, p, ranks):
    size = lax.axis_size("fsdp")
    replicas = lax.axis_size("dp")
    if not (power_of_two(size) and size > 1):
        gram_sum = lax.psum(gram_part, "fsdp")
        inverse, factor_p = factor(gram_sum, p, ranks)
        rows = lax.psum_scatter(jnp.stack(rt_parts), "fsdp", scatter_dimension=1, tiled=True)
        rows = lax.psum(rows, "dp")
        return inverse, factor_p, lax.all_gather(rows, "fsdp", axis=1, tiled=True)
    bits = bits_of("fsdp")
    rt = jnp.concatenate([halve(part[None], 1) for part in rt_parts], axis=0)
    rows = rt.shape[1]
    gram_sum = gram_part
    for bit in bits:
        gram_sum = gram_sum + across(gram_sum, "fsdp", bit)
    rt = scatter_sum(rt, bits[1:])
    if power_of_two(replicas):
        steps = bits_of("dp")
        for bit in steps[:-1]:
            rt = rt + across(rt, "dp", bit)
        gram_sum, rt = tie(gram_sum, rt)
        theirs = across(rt, "dp", steps[-1]) if steps else 0.0
        inverse, factor_p = factor(gram_sum, p, ranks)
        theirs, inverse, factor_p = tie(theirs, inverse, factor_p)
        rt = rt + theirs
    else:
        rt = lax.psum(rt, "dp")
        inverse, factor_p = factor(gram_sum, p, ranks)
    return inverse, factor_p, unhalve(gather_sum(rt, bits[1:], rows), 1)


def left_sums(cot, order, q_init, inputs_t, fbq, ranks):
    replicas = lax.axis_size("dp")
    count = fbq.shape[0]
    if not (power_of_two(replicas) and replicas > 1):
        p = lax.psum(left(cot, order, q_init, inputs_t, fbq, ranks), "dp")
        return [p[m] for m in range(count)], gram(p)
    low = (lax.axis_index("dp") & 1).reshape(1)
    whole = []
    for m in range(count):
        mine, other = left_code(m, cot, order, low, q_init, inputs_t, fbq, ranks)
        mine = add_code(mine, across(other, "dp", 1))
        for bit in bits_of("dp")[1:]:
            mine = add_code(mine, across(mine, "dp", bit))
        whole.append(whole_left(low, mine, across(mine, "dp", 1)))
    return [p for p, _ in whole], jnp.stack([part for _, part in whole])


def local(inputs, cotangent, feedback, q_init, factor_ranks):
    cot, order = gather_cotangent(cotangent)
    inputs_t = inputs.T
    fbq = feedback_q(feedback, q_init, factor_ranks)
    p, gram_part = left_sums(cot, order, q_init, inputs_t, fbq, factor_ranks)
    full_grad = full(cot, order, inputs_t, feedback)
    rt_parts = [right(m, full_grad, p[m]) for m in range(len(p))]
    inverse, factor_p, rt = sums(gram_part, rt_parts, jnp.stack(p), factor_ranks)
    new_error, factor_q = error(full_grad, factor_p, inverse, rt)
    return (factor_p, factor_q, new_error)


def solution(mesh):
    placed = (P("dp", "fsdp"), P(None, "dp", "fsdp"), P(None, "dp", "fsdp", None), P(), P())
    return jax.shard_map(
        local,
        mesh=mesh,
        in_specs=placed,
        out_specs=(P(None, "fsdp", None), P(), P(None, "dp", "fsdp", None)),
        check_vma=False,
    )
```

```python
import functools

import jax
import jax.numpy as jnp
from jax import lax
from jax.experimental import pallas as pl
from jax.experimental.pallas import tpu as pltpu
from jax.sharding import PartitionSpec as P

F32 = jnp.float32
BF16 = jnp.bfloat16
VMEM = pl.BlockSpec(memory_space=pltpu.VMEM)
SMEM = pl.BlockSpec(memory_space=pltpu.SMEM)
MIB = 1024 * 1024


def halves(x):
    high = x.astype(BF16)
    return high, (x - high.astype(F32)).astype(BF16)


def mm(a, b):
    return jnp.dot(a, b, preferred_element_type=F32)


def mm_nt(a, b):
    return lax.dot_general(a, b, (((1,), (1,)), ((), ())), preferred_element_type=F32)


def params(size, steps=1):
    return pltpu.CompilerParams(
        vmem_limit_bytes=size * MIB, dimension_semantics=("arbitrary",) * steps
    )


def tile_of(rows):
    return min(rows, 256)


def in_vmem(shape, dtype):
    return pltpu.VMEM(shape, dtype)


def stay(x):
    return pltpu.with_memory_space_constraint(x, pltpu.VMEM)


def masked_halves(q, rank):
    column = lax.broadcasted_iota(jnp.int32, q.shape, 1)
    return halves(jnp.where(column < rank, q, 0.0))


def feedback_q_kernel(ranks_ref, fb_ref, q_ref, in_ref, held_ref, out_ref, in_t_ref, q2_ref, sems):
    count, rows, _ = held_ref.shape
    width = q_ref.shape[2]
    tile = tile_of(rows)
    copies = []
    for m in range(count):
        for i in range(rows // tile):
            part = pl.ds(i * tile, tile)
            copies.append(
                pltpu.make_async_copy(fb_ref.at[m, 0, part], held_ref.at[m, part], sems.at[len(copies)])
            )
            copies[-1].start()
    in_t_ref[...] = in_ref[...].T
    for m in range(count):
        q_high, q_low = masked_halves(q_ref[m], ranks_ref[m])
        q2_ref[m, :, :width] = q_high
        q2_ref[m, :, width:] = q_low
    for m in range(count):
        for i in range(rows // tile):
            part = pl.ds(i * tile, tile)
            copies[m * (rows // tile) + i].wait()
            high, low = halves(held_ref[m, part])
            both = mm(high, q2_ref[m])
            out_ref[m, part] = both[:, :width] + both[:, width:] + mm(low, q2_ref[m, :, :width])


def feedback_q(feedback, q_init, inputs, ranks):
    count, _, rows, columns = feedback.shape
    width = q_init.shape[2]
    return pl.pallas_call(
        feedback_q_kernel,
        in_specs=[SMEM, pl.BlockSpec(memory_space=pltpu.HBM), VMEM, VMEM],
        out_specs=[VMEM, VMEM, VMEM],
        out_shape=[
            in_vmem((count, rows, columns), F32),
            jax.ShapeDtypeStruct((count, rows, width), F32),
            jax.ShapeDtypeStruct(inputs.shape[::-1], inputs.dtype),
        ],
        scratch_shapes=[
            pltpu.VMEM((count, columns, 2 * width), BF16),
            pltpu.SemaphoreType.DMA((count * (rows // tile_of(rows)),)),
        ],
        compiler_params=pltpu.CompilerParams(vmem_limit_bytes=16 * MIB),
        name="feedback_q",
    )(ranks, pltpu.with_memory_space_constraint(feedback, pltpu.HBM), q_init, inputs)


def fill_cotangent(blocks, whole_ref):
    if len(blocks) == 1:
        whole_ref[...] = blocks[0][0]
        return
    me = lax.axis_index("fsdp")
    for r, block in enumerate(blocks):
        width = block.shape[2]
        start = pl.multiple_of((me ^ r) * width, width)
        whole_ref[:, pl.ds(start, width)] = block[0]


def gradient_q(whole, q, rank, inputs_t):
    width = q.shape[1]
    q_high, q_low = masked_halves(q, rank)
    both = mm(whole, jnp.concatenate([q_high, q_low], axis=1))
    c_high, c_low = halves(both[:, :width] + both[:, width:])
    both = mm(inputs_t, jnp.concatenate([c_high, c_low], axis=1))
    return both[:, :width] + both[:, width:]


def at_block(shape, m):
    return pl.BlockSpec((1, *shape[1:]), lambda *_: (m,) + (0,) * (len(shape) - 1))


def block_of(pieces, m):
    for piece in pieces:
        if m < piece.shape[0]:
            return piece, m
        m -= piece.shape[0]
    raise ValueError(m)


def left_kernel(m, ranks_ref, q_ref, in_ref, fbq_ref, *refs):
    *blocks, out_ref, whole_ref = refs
    fill_cotangent(blocks, whole_ref)
    out_ref[...] = fbq_ref[0] + gradient_q(whole_ref[...], q_ref[0], ranks_ref[m], in_ref[...])


def left(m, blocks, q_init, inputs_t, fbq, ranks):
    _, rows, width = fbq.shape
    arrays, indices = zip(*(block_of(pieces, m) for pieces in blocks))
    shape = (arrays[0].shape[1], q_init.shape[1])
    return pl.pallas_call(
        functools.partial(left_kernel, m),
        grid=(1,),
        in_specs=[SMEM, at_block(q_init.shape, m), VMEM, at_block(fbq.shape, m)]
        + [at_block(a.shape, i) for a, i in zip(arrays, indices)],
        out_specs=[
            pl.BlockSpec((rows, width), lambda i: (0, 0)),
            pl.BlockSpec(shape, lambda i: (0, 0)),
        ],
        out_shape=[
            jax.ShapeDtypeStruct((rows, width), F32),
            jax.ShapeDtypeStruct(shape, BF16),
        ],
        compiler_params=params(16),
        name=f"left_{m}",
    )(ranks, q_init, inputs_t, fbq, *arrays)


GROUPS = 16
LANES = 128


def encode(x, out_ref):
    rows, width = x.shape
    grouped = x.reshape(GROUPS, rows // GROUPS, width)
    top = jnp.max(jnp.abs(grouped), axis=1)
    level = jnp.ceil(jnp.log(jnp.maximum(top, 1e-30)) * 32.0) + 1.0
    up = jnp.exp(level * (-1.0 / 32.0)) * 32767.0
    code = jnp.round(grouped * up[:, None, :]).reshape(rows, width)
    out_ref[:rows] = code.astype(jnp.int32).astype(jnp.int16)
    out_ref[rows:] = level.astype(jnp.int32).astype(jnp.int16)


def decode(ref):
    rows = ref.shape[0] - GROUPS
    width = ref.shape[1]
    level = ref[rows:].astype(jnp.int32).astype(F32)
    down = jnp.exp(level * (1.0 / 32.0)) * (1.0 / 32767.0)
    code = ref[:rows].astype(jnp.int32).astype(F32).reshape(GROUPS, rows // GROUPS, width)
    return (code * down[:, None, :]).reshape(rows, width)


def left_code_kernel(m, ranks_ref, q_ref, in_ref, fbq_ref, *refs):
    *blocks, mine_ref, code_ref, whole_ref, p_ref = refs
    fill_cotangent(blocks, whole_ref)
    p = fbq_ref[0] + gradient_q(whole_ref[...], q_ref[0], ranks_ref[m], in_ref[...])
    p_ref[...] = p.reshape(p_ref.shape)
    low = lax.axis_index("dp") & 1
    mine_ref[...] = p_ref[low]
    encode(p_ref[1 - low], code_ref)


def left_code(m, blocks, q_init, inputs_t, fbq, ranks):
    _, rows, width = fbq.shape
    arrays, indices = zip(*(block_of(pieces, m) for pieces in blocks))
    shape = (arrays[0].shape[1], q_init.shape[1])
    half = rows // 2
    return pl.pallas_call(
        functools.partial(left_code_kernel, m),
        grid=(1,),
        in_specs=[SMEM, at_block(q_init.shape, m), VMEM, at_block(fbq.shape, m)]
        + [at_block(a.shape, i) for a, i in zip(arrays, indices)],
        out_specs=[
            pl.BlockSpec((half, width), lambda i: (0, 0)),
            pl.BlockSpec((half + GROUPS, width), lambda i: (0, 0)),
            pl.BlockSpec(shape, lambda i: (0, 0)),
        ],
        out_shape=[
            jax.ShapeDtypeStruct((half, width), F32),
            jax.ShapeDtypeStruct((half + GROUPS, width), jnp.int16),
            jax.ShapeDtypeStruct(shape, BF16),
        ],
        scratch_shapes=[pltpu.VMEM((2, half, width), F32)],
        compiler_params=params(16),
        name=f"left_code_{m}",
    )(ranks, q_init, inputs_t, fbq, *arrays)


def add_kernel(mine_ref, theirs_ref, out_ref):
    mine = mine_ref[...] if mine_ref.dtype == F32 else decode(mine_ref)
    encode(mine + decode(theirs_ref), out_ref)


def add_code(mine, theirs):
    return pl.pallas_call(
        add_kernel,
        in_specs=[VMEM, VMEM],
        out_specs=VMEM,
        out_shape=jax.ShapeDtypeStruct(theirs.shape, jnp.int16),
        compiler_params=pltpu.CompilerParams(vmem_limit_bytes=16 * MIB),
        name="add_code",
    )(mine, theirs)


def whole_left_kernel(mine_ref, theirs_ref, p_ref, gram_ref):
    half, width = mine_ref.shape[0] - GROUPS, mine_ref.shape[1]
    low = lax.axis_index("dp") & 1
    p_ref[pl.ds(pl.multiple_of(low * half, half), half)] = decode(mine_ref)
    p_ref[pl.ds(pl.multiple_of((1 - low) * half, half), half)] = decode(theirs_ref)
    gram_ref[...] = gram_of(p_ref[...])


def whole_left(mine, theirs):
    half, width = mine.shape[0] - GROUPS, mine.shape[1]
    return pl.pallas_call(
        whole_left_kernel,
        in_specs=[VMEM, VMEM],
        out_specs=[VMEM, VMEM],
        out_shape=[
            jax.ShapeDtypeStruct((2 * half, width), F32),
            jax.ShapeDtypeStruct((width, width), F32),
        ],
        compiler_params=pltpu.CompilerParams(vmem_limit_bytes=16 * MIB),
        name="whole_left",
    )(mine, theirs)


def full_kernel(m, held_ref, in_ref, whole_ref, out_ref):
    rows = out_ref.shape[0]
    tile = tile_of(rows)
    for i in range(rows // tile):
        part = pl.ds(i * tile, tile)
        out_ref[part] = held_ref[m, part] + mm(in_ref[part], whole_ref[...])


def full(m, held, inputs_t, whole):
    _, rows, columns = held.shape
    return pl.pallas_call(
        functools.partial(full_kernel, m),
        in_specs=[VMEM, VMEM, VMEM],
        out_specs=VMEM,
        out_shape=in_vmem((rows, columns), F32),
        compiler_params=pltpu.CompilerParams(vmem_limit_bytes=16 * MIB),
        name=f"full_{m}",
    )(stay(held), inputs_t, whole)


def right_kernel(full_ref, p_ref, mine_ref, other_ref, both_ref):
    rows, width = p_ref.shape
    tile = tile_of(rows)
    total = None
    for i in range(rows // tile):
        part = pl.ds(i * tile, tile)
        p_high, p_low = halves(p_ref[part].T)
        g_high, g_low = halves(full_ref[part])
        both = mm(jnp.concatenate([p_high, p_low], axis=0), g_high)
        term = both[:width] + both[width:] + mm(p_high, g_low)
        total = term if total is None else total + term
    lanes = both_ref.shape[2]
    tiles = total.shape[1] // lanes
    stacked = [total[:, t * lanes : (t + 1) * lanes] for t in range(tiles)]
    both_ref[...] = jnp.concatenate(stacked, axis=0).reshape(both_ref.shape)
    side = lax.axis_index("fsdp") & 1
    mine_ref[...] = both_ref[side]
    other_ref[...] = both_ref[1 - side]


def right(m, full_grad, p):
    width = p.shape[1]
    half = full_grad.shape[1] * width // LANES // 2
    return pl.pallas_call(
        right_kernel,
        in_specs=[VMEM, VMEM],
        out_specs=[VMEM, VMEM],
        out_shape=[jax.ShapeDtypeStruct((half, LANES), F32)] * 2,
        scratch_shapes=[pltpu.VMEM((2, half, LANES), F32)],
        compiler_params=pltpu.CompilerParams(vmem_limit_bytes=16 * MIB),
        name=f"right_{m}",
    )(stay(full_grad), p)


def tree(values):
    while len(values) > 1:
        values = [sum(values[i : i + 2][1:], values[i]) for i in range(0, len(values), 2)]
    return values[0]


def merge_kernel(count, plain, coded, parts, bit, *refs):
    terms, refs = refs[: plain * count], refs[plain * count :]
    codes, refs = refs[:coded], refs[coded:]
    decoded = [decode(code) for code in codes]
    rows = (decoded[0] if decoded else terms[0]).shape[0] // (count if decoded else 1)
    sums = []
    for m in range(count):
        values = [terms[t * count + m][...] for t in range(plain)]
        values += [value[m * rows : (m + 1) * rows] for value in decoded]
        sums.append(tree(values))
    if parts == 1:
        encode(jnp.concatenate(sums, axis=0), refs[0])
        return
    *outs, cut_ref = refs
    own = (lax.axis_index("fsdp") >> (bit.bit_length() - 1)) & (parts - 1)
    for m in range(count):
        cut_ref[m] = sums[m].reshape(cut_ref.shape[1:])
        outs[m][...] = cut_ref[m, own]
    for r in range(1, parts):
        encode(jnp.concatenate([cut_ref[m, own ^ r] for m in range(count)], axis=0), outs[count + r - 1])


def merge(terms, codes, name, parts=1, bit=1):
    count = len(terms[0]) if terms else 1
    if terms:
        rows = terms[0][0].shape[0]
        lanes = terms[0][0].shape[1]
    else:
        rows = codes[0].shape[0] - GROUPS
        lanes = codes[0].shape[1]
    share = rows // parts
    code = jax.ShapeDtypeStruct((count * share + GROUPS, lanes), jnp.int16)
    plain = [jax.ShapeDtypeStruct((share, lanes), F32)] * count if parts > 1 else []
    outs = plain + [code] * max(parts - 1, 1)
    flat = [x for term in terms for x in term]
    results = pl.pallas_call(
        functools.partial(merge_kernel, count, len(terms), len(codes), parts, bit),
        in_specs=[VMEM] * (len(flat) + len(codes)),
        out_specs=[VMEM] * len(outs),
        out_shape=outs,
        scratch_shapes=[pltpu.VMEM((count, parts, share, lanes), F32)] if parts > 1 else [],
        compiler_params=pltpu.CompilerParams(vmem_limit_bytes=16 * MIB),
        name=name,
    )(*flat, *codes)
    return (results[:count], results[count:]) if parts > 1 else results[0]


def gram_of(p):
    width = p.shape[1]
    high, low = halves(p)
    high_t, low_t = halves(p.T)
    both = mm(high_t, jnp.concatenate([high, low], axis=1))
    return both[:, :width] + both[:, width:] + mm(low_t, high)


def gram_kernel(p_ref, out_ref):
    out_ref[0] = gram_of(p_ref[0])


def gram(p):
    count, rows, width = p.shape
    return pl.pallas_call(
        gram_kernel,
        grid=(count,),
        in_specs=[pl.BlockSpec((1, rows, width), lambda m: (m, 0, 0))],
        out_specs=pl.BlockSpec((1, width, width), lambda m: (m, 0, 0)),
        out_shape=jax.ShapeDtypeStruct((count, width, width), F32),
        compiler_params=params(16),
        name="gram",
    )(p)


def cholesky_inverse(work, n):
    lane = lax.broadcasted_iota(jnp.int32, (8, n), 1)
    sub = lax.broadcasted_iota(jnp.int32, (8, n), 0)

    def wide(x):
        return jnp.broadcast_to(x, (8, n))

    for b in range(n // 8):
        at = 8 * b
        panels = []
        for blocks in work:
            head = blocks[b]
            columns = [wide(head[:, at + j : at + j + 1]) for j in range(8)]
            scales, lows, tops = [], [], []
            for s in range(8):
                scale = lax.rsqrt(wide(columns[s][s : s + 1, :]))
                low = columns[s] * scale
                for j in range(s + 1, 8):
                    columns[j] = columns[j] - low * wide(low[j : j + 1, :])
                row = jnp.where(lane == at + s, scale, wide(head[s : s + 1, :]) * scale)
                below = jnp.where(lane == at + s, 0.0, head) - low * row
                head = jnp.where(sub > s, below, jnp.where(sub == s, row, head))
                scales.append(scale)
                lows.append(low)
                tops.append(jnp.where((lane > at + s) & (lane < at + 8), 0.0, row))
            blocks[b] = head
            panels.append((scales, lows, tops))
        for c in range(b + 1, n // 8):
            for blocks, (scales, lows, tops) in zip(work, panels):
                x = blocks[c]
                columns = [wide(x[:, at + j : at + j + 1]) for j in range(8)]
                y = jnp.where((lane >= at) & (lane < at + 8), 0.0, x)
                for s in range(8):
                    low = columns[s] * scales[s]
                    for j in range(s + 1, 8):
                        columns[j] = columns[j] - low * wide(lows[s][j : j + 1, :])
                    y = y - low * tops[s]
                blocks[c] = y


def factor_kernel(terms, ranks_ref, *refs):
    gram_refs, refs = refs[:terms], refs[terms:]
    inv_ref, out_ref = refs[-2:]
    p_refs = refs[:-2]
    count, n, _ = inv_ref.shape
    lane = lax.broadcasted_iota(jnp.int32, (8, n), 1)
    sub = lax.broadcasted_iota(jnp.int32, (8, n), 0)
    work = []
    for m in range(count):
        free = jnp.where(lane < ranks_ref[m], 0.0, 1.0)
        blocks = []
        for b in range(n // 8):
            g = tree([ref[m, 8 * b : 8 * b + 8, :] for ref in gram_refs])
            blocks.append(jnp.where(lane == sub + 8 * b, g + free, g))
        work.append(blocks)
    cholesky_inverse(work, n)
    for m in range(count):
        for b in range(n // 8):
            inv_ref[m, 8 * b : 8 * b + 8, :] = jnp.where(lane <= sub + 8 * b, work[m][b], 0.0)
        i_high, i_low = halves(inv_ref[m])
        p_high, p_low = halves(p_refs[m][...])
        both = mm_nt(p_high, jnp.concatenate([i_high, i_low], axis=0))
        out_ref[m] = both[:, :n] + both[:, n:] + mm_nt(p_low, i_high)


def factor(grams, p, ranks):
    count = len(p)
    return pl.pallas_call(
        functools.partial(factor_kernel, len(grams)),
        in_specs=[SMEM] + [VMEM] * (len(grams) + count),
        out_specs=[VMEM, VMEM],
        out_shape=[
            jax.ShapeDtypeStruct(grams[0].shape, F32),
            jax.ShapeDtypeStruct((count, *p[0].shape), F32),
        ],
        compiler_params=pltpu.CompilerParams(vmem_limit_bytes=16 * MIB),
        name="factor",
    )(ranks, *grams, *p)


def error_kernel(count, pieces, groups, fp_ref, inv_ref, *refs):
    codes, refs = refs[:pieces], refs[pieces:]
    full_refs, (err_ref, fq_ref, right_ref, q_ref, buf_ref, sems) = refs[:count], refs[count:]
    rows, width = fp_ref.shape[1:]
    tile = tile_of(rows)
    share = right_ref.shape[1] // pieces
    me = lax.axis_index("fsdp") if pieces > 1 else 0
    for r, code in enumerate(codes):
        value = decode(code)
        place = (me ^ r) & 1 if pieces > 1 else 0
        for bit, members in groups:
            place = place * members + (((me ^ r) >> (bit.bit_length() - 1)) & (members - 1))
        at = pl.ds(pl.multiple_of(place * share, share), share)
        for m in range(count):
            right_ref[m, at] = value[m * share : (m + 1) * share]
    copies = []
    for m in range(count):
        i_high, i_low = halves(inv_ref[m])
        tiles = [right_ref[m, t : t + width] for t in range(0, right_ref.shape[1], width)]
        r_high, r_low = halves(jnp.concatenate(tiles, axis=1))
        both = mm(jnp.concatenate([i_high, i_low], axis=0), r_high)
        fq_t = both[:width] + both[width:] + mm(i_high, r_low)
        q_high, q_low = halves(fq_t)
        q3 = jnp.concatenate([q_high, q_high, q_low], axis=0)
        for i in range(rows // tile):
            part = pl.ds(i * tile, tile)
            p_high, p_low = halves(fp_ref[m, part])
            low_rank = mm(jnp.concatenate([p_high, p_low, p_high], axis=1), q3)
            buf_ref[m, part] = full_refs[m][part] - low_rank
            copies.append(
                pltpu.make_async_copy(buf_ref.at[m, part], err_ref.at[m, 0, part], sems.at[len(copies)])
            )
            copies[-1].start()
        q_ref[m] = fq_t.T
        copies.append(pltpu.make_async_copy(q_ref.at[m], fq_ref.at[m], sems.at[len(copies)]))
        copies[-1].start()
    for copy in copies:
        copy.wait()


def error(full_grad, factor_p, inverse, codes):
    count, rows, width = factor_p.shape
    columns = full_grad[0].shape[1]
    out = pl.BlockSpec(memory_space=pltpu.HBM)
    groups = groups_of("fsdp") if len(codes) > 1 else []
    return pl.pallas_call(
        functools.partial(error_kernel, count, len(codes), groups),
        in_specs=[VMEM] * (2 + len(codes) + count),
        out_specs=[out, out],
        out_shape=[
            jax.ShapeDtypeStruct((count, 1, rows, columns), F32),
            jax.ShapeDtypeStruct((count, columns, width), F32),
        ],
        scratch_shapes=[
            pltpu.VMEM((count, columns * width // LANES, LANES), F32),
            pltpu.VMEM((count, columns, width), F32),
            pltpu.VMEM((count, rows, columns), F32),
            pltpu.SemaphoreType.DMA((count * (rows // tile_of(rows) + 1),)),
        ],
        compiler_params=pltpu.CompilerParams(vmem_limit_bytes=24 * MIB),
        name="error",
    )(factor_p, inverse, *codes, *[stay(x) for x in full_grad])


def power_of_two(n):
    return n & (n - 1) == 0


def across(x, axis, bit):
    size = lax.axis_size(axis)
    return lax.ppermute(x, axis, [(i, i ^ bit) for i in range(size)])


def bits_of(axis):
    size = lax.axis_size(axis)
    return [1 << b for b in range(size.bit_length() - 1)]


def groups_of(axis):
    bits = bits_of(axis)[1:]
    return [(bits[i], 1 << len(bits[i : i + 2])) for i in range(0, len(bits), 2)]


def gather_blocks(x, axis, beside=()):
    held = {0: x}
    for bit, members in groups_of(axis)[::-1]:
        for r in list(held):
            for k in range(1, members):
                held[r ^ (k * bit)] = across(held[r], axis, k * bit)
    order = list(held)
    values = tie(*[held[r] for r in order], *beside)
    held, beside = dict(zip(order, values)), values[len(order) :]
    held.update({r ^ 1: across(held[r], axis, 1) for r in order})
    return [held[r] for r in range(len(held))], beside


def gather_cotangent(cotangent, beside):
    size = lax.axis_size("fsdp")
    count, _, width = cotangent.shape
    if power_of_two(size) and size > 1 and width % 128 == 0 and count > 1:
        lists = []
        for m in range(count):
            blocks, beside = gather_blocks(cotangent[m : m + 1], "fsdp", beside)
            lists.append(blocks)
        blocks = [list(pieces) for pieces in zip(*lists)]
        return blocks, beside
    whole = lax.all_gather(cotangent, "fsdp", axis=2, tiled=True)
    return [[whole]], beside


def tie(*values):
    return lax.optimization_barrier(values)


def sums(gram_part, full_grad, p, ranks):
    size = lax.axis_size("fsdp")
    replicas = lax.axis_size("dp")
    count = len(p)
    if not (power_of_two(size) and size > 1):
        inverse, factor_p = factor([lax.psum(gram_part, "fsdp")], p, ranks)
        pairs = [right(m, full_grad[m], p[m]) for m in range(count)]
        ordered = [jnp.stack(pair) for pair in pairs]
        odd = (lax.axis_index("fsdp") & 1) == 1
        whole = jnp.stack([jnp.where(odd, x[::-1], x).reshape(-1, x.shape[2]) for x in ordered])
        return inverse, factor_p, [merge([list(lax.psum(whole, ("fsdp", "dp")))], [], "code")]
    groups = groups_of("fsdp")

    gram_part = gram_part + across(gram_part, "fsdp", 1)
    for bit, members in groups[:-1]:
        gram_part = tree([gram_part] + [across(gram_part, "fsdp", k * bit) for k in range(1, members)])
    grams = [gram_part]
    for bit, members in groups[-1:]:
        grams += [across(gram_part, "fsdp", k * bit) for k in range(1, members)]

    pairs = [right(m, full_grad[m], p[m]) for m in range(count)]
    terms = [[mine for mine, _ in pairs], [across(other, "fsdp", 1) for _, other in pairs]]
    codes = []
    for bit, members in groups:
        keep, others = merge(terms, codes, f"part_{bit}", members, bit)
        codes = [across(others[k - 1], "fsdp", k * bit) for k in range(1, members)]
        terms = [keep]
    code = merge(terms, codes, "code")
    if power_of_two(replicas) and replicas > 1:
        *grams, code = tie(*grams, code)
        theirs = [across(code, "dp", k) for k in range(1, replicas)]
        inverse, factor_p = factor(grams, p, ranks)
        *theirs, inverse, factor_p = tie(*theirs, inverse, factor_p)
        code = merge([], [code] + theirs, "code_sum")
    else:
        inverse, factor_p = factor(grams, p, ranks)
        code = merge([[lax.psum(plain(code), "dp")]], [], "code_sum")
    return inverse, factor_p, gather_blocks(code, "fsdp")[0]


def plain_kernel(code_ref, out_ref):
    out_ref[...] = decode(code_ref)


def plain(code):
    return pl.pallas_call(
        plain_kernel,
        in_specs=[VMEM],
        out_specs=VMEM,
        out_shape=jax.ShapeDtypeStruct((code.shape[0] - GROUPS, code.shape[1]), F32),
        name="plain",
    )(code)


def left_sums(blocks, q_init, inputs_t, held, fbq, ranks):
    replicas = lax.axis_size("dp")
    count = fbq.shape[0]
    if not (power_of_two(replicas) and replicas > 1):
        parts = [left(m, blocks, q_init, inputs_t, fbq, ranks) for m in range(count)]
        p = lax.psum(jnp.stack([part for part, _ in parts]), "dp")
        full_grad = [full(m, held, inputs_t, parts[m][1]) for m in range(count)]
        return [p[m] for m in range(count)], full_grad, gram(p)
    whole, full_grad = [], []
    for m in range(count):
        mine, other, cot = left_code(m, blocks, q_init, inputs_t, fbq, ranks)
        mine = add_code(mine, across(other, "dp", 1))
        for step, bit in enumerate(bits_of("dp")[1:]):
            if step == 0:
                mine, cot = tie(mine, cot)
                theirs, grad = tie(across(mine, "dp", bit), full(m, held, inputs_t, cot))
                full_grad.append(grad)
            else:
                theirs = across(mine, "dp", bit)
            mine = add_code(mine, theirs)
        if len(full_grad) == m:
            full_grad.append(full(m, held, inputs_t, cot))
        whole.append(whole_left(mine, across(mine, "dp", 1)))
    return [p for p, _ in whole], full_grad, jnp.stack([part for _, part in whole])


def local(inputs, cotangent, feedback, q_init, factor_ranks):
    beside = feedback_q(feedback, q_init, inputs, factor_ranks)
    blocks, (held, fbq, inputs_t) = gather_cotangent(cotangent, beside)
    p, full_grad, gram_part = left_sums(blocks, q_init, inputs_t, held, fbq, factor_ranks)
    inverse, factor_p, codes = sums(gram_part, full_grad, p, factor_ranks)
    new_error, factor_q = error(full_grad, factor_p, inverse, codes)
    return (factor_p, factor_q, new_error)


def solution(mesh):
    placed = (P("dp", "fsdp"), P(None, "dp", "fsdp"), P(None, "dp", "fsdp", None), P(), P())
    return jax.shard_map(
        local,
        mesh=mesh,
        in_specs=placed,
        out_specs=(P(None, "fsdp", None), P(), P(None, "dp", "fsdp", None)),
        check_vma=False,
    )
```

```python
import functools

import jax
import jax.numpy as jnp
from jax import lax
from jax.experimental import pallas as pl
from jax.experimental.pallas import tpu as pltpu
from jax.sharding import PartitionSpec as P

F32 = jnp.float32
BF16 = jnp.bfloat16
VMEM = pl.BlockSpec(memory_space=pltpu.VMEM)
SMEM = pl.BlockSpec(memory_space=pltpu.SMEM)
MIB = 1024 * 1024


def halves(x):
    high = x.astype(BF16)
    return high, (x - high.astype(F32)).astype(BF16)


def mm(a, b):
    return jnp.dot(a, b, preferred_element_type=F32)


def mm_nt(a, b):
    return lax.dot_general(a, b, (((1,), (1,)), ((), ())), preferred_element_type=F32)


def params(size, steps=1):
    return pltpu.CompilerParams(
        vmem_limit_bytes=size * MIB, dimension_semantics=("arbitrary",) * steps
    )


def tile_of(rows):
    return min(rows, 256)


def in_vmem(shape, dtype):
    return pltpu.VMEM(shape, dtype)


def stay(x):
    return pltpu.with_memory_space_constraint(x, pltpu.VMEM)


def masked_halves(q, rank):
    column = lax.broadcasted_iota(jnp.int32, q.shape, 1)
    return halves(jnp.where(column < rank, q, 0.0))


def feedback_q_kernel(
    ranks_ref, fb_ref, q_ref, in_ref, held_ref, out_ref, q2_ref, in_t_ref, ranks_own, q_own, in_own, sems, sem_q
):
    count, rows, _ = held_ref.shape
    width = q_ref.shape[2]
    tile = tile_of(rows)
    small = [
        pltpu.make_async_copy(ranks_ref, ranks_own, sem_q.at[0]),
        pltpu.make_async_copy(q_ref, q_own, sem_q.at[1]),
        pltpu.make_async_copy(in_ref, in_own, sem_q.at[2]),
    ]
    copies = []
    small[2].start()
    small[0].start()
    small[1].start()
    for m in range(count):
        for i in range(rows // tile):
            part = pl.ds(i * tile, tile)
            copies.append(
                pltpu.make_async_copy(fb_ref.at[m, 0, part], held_ref.at[m, part], sems.at[len(copies)])
            )
            copies[-1].start()
    small[2].wait()
    in_t_ref[...] = in_own[...].T
    small[0].wait()
    small[1].wait()
    for m in range(count):
        q_high, q_low = masked_halves(q_own[m], ranks_own[m])
        q2_ref[m, :, :width] = q_high
        q2_ref[m, :, width:] = q_low
    for m in range(count):
        for i in range(rows // tile):
            part = pl.ds(i * tile, tile)
            copies[m * (rows // tile) + i].wait()
            high, low = halves(held_ref[m, part])
            both = mm(high, q2_ref[m])
            out_ref[m, part] = both[:, :width] + both[:, width:] + mm(low, q2_ref[m, :, :width])


def feedback_q(feedback, q_init, inputs, ranks):
    count, _, rows, columns = feedback.shape
    width = q_init.shape[2]
    far = pl.BlockSpec(memory_space=pltpu.HBM)
    return pl.pallas_call(
        feedback_q_kernel,
        in_specs=[far] * 4,
        out_specs=[VMEM] * 4,
        out_shape=[
            in_vmem((count, rows, columns), F32),
            in_vmem((count, rows, width), F32),
            in_vmem((count, columns, 2 * width), BF16),
            in_vmem(inputs.shape[::-1], inputs.dtype),
        ],
        scratch_shapes=[
            pltpu.SMEM(ranks.shape, ranks.dtype),
            pltpu.VMEM(q_init.shape, q_init.dtype),
            pltpu.VMEM(inputs.shape, inputs.dtype),
            pltpu.SemaphoreType.DMA((count * (rows // tile_of(rows)),)),
            pltpu.SemaphoreType.DMA((3,)),
        ],
        compiler_params=pltpu.CompilerParams(vmem_limit_bytes=16 * MIB),
        name="feedback_q",
    )(*[pltpu.with_memory_space_constraint(x, pltpu.HBM) for x in (ranks, feedback, q_init, inputs)])


def fill_cotangent(blocks, at, whole_ref):
    if len(blocks) == 1:
        whole_ref[...] = blocks[0][at]
        return
    me = lax.axis_index("fsdp")
    for r, block in enumerate(blocks):
        width = block.shape[2]
        start = pl.multiple_of((me ^ r) * width, width)
        whole_ref[:, pl.ds(start, width)] = block[at]


def gradient_q(whole, q2, inputs_t):
    width = q2.shape[1] // 2
    both = mm(whole, q2)
    c_high, c_low = halves(both[:, :width] + both[:, width:])
    both = mm(inputs_t, jnp.concatenate([c_high, c_low], axis=1))
    return both[:, :width] + both[:, width:]


def left_kernel(m, at, q2_ref, in_ref, fbq_ref, *refs):
    *blocks, out_ref, whole_ref = refs
    fill_cotangent(blocks, at, whole_ref)
    out_ref[...] = fbq_ref[m] + gradient_q(whole_ref[...], q2_ref[m], in_ref[...])


def left(m, blocks, at, q2, inputs_t, fbq):
    _, rows, width = fbq.shape
    return pl.pallas_call(
        functools.partial(left_kernel, m, at),
        in_specs=[VMEM] * (3 + len(blocks)),
        out_specs=[VMEM, VMEM],
        out_shape=[
            jax.ShapeDtypeStruct((rows, width), F32),
            jax.ShapeDtypeStruct((blocks[0].shape[1], q2.shape[1]), BF16),
        ],
        compiler_params=pltpu.CompilerParams(vmem_limit_bytes=16 * MIB),
        name=f"left_{m}",
    )(q2, inputs_t, fbq, *blocks)


GROUPS = 16
LANES = 128


def encode(x, out_ref):
    rows, width = x.shape
    grouped = x.reshape(GROUPS, rows // GROUPS, width)
    top = jnp.max(jnp.abs(grouped), axis=1)
    level = jnp.ceil(jnp.log(jnp.maximum(top, 1e-30)) * 32.0) + 1.0
    up = jnp.exp(level * (-1.0 / 32.0)) * 32767.0
    code = jnp.round(grouped * up[:, None, :]).reshape(rows, width)
    out_ref[:rows] = code.astype(jnp.int32).astype(jnp.int16)
    out_ref[rows:] = level.astype(jnp.int32).astype(jnp.int16)


def decode(ref):
    rows = ref.shape[0] - GROUPS
    width = ref.shape[1]
    level = ref[rows:].astype(jnp.int32).astype(F32)
    down = jnp.exp(level * (1.0 / 32.0)) * (1.0 / 32767.0)
    code = ref[:rows].astype(jnp.int32).astype(F32).reshape(GROUPS, rows // GROUPS, width)
    return (code * down[:, None, :]).reshape(rows, width)


def left_code_kernel(m, at, q2_ref, in_ref, fbq_ref, *refs):
    *blocks, mine_ref, code_ref, whole_ref, p_ref = refs
    fill_cotangent(blocks, at, whole_ref)
    p = fbq_ref[m] + gradient_q(whole_ref[...], q2_ref[m], in_ref[...])
    p_ref[...] = p.reshape(p_ref.shape)
    low = lax.axis_index("dp") & 1
    mine_ref[...] = p_ref[low]
    encode(p_ref[1 - low], code_ref)


def left_code(m, blocks, at, q2, inputs_t, fbq):
    _, rows, width = fbq.shape
    half = rows // 2
    return pl.pallas_call(
        functools.partial(left_code_kernel, m, at),
        in_specs=[VMEM] * (3 + len(blocks)),
        out_specs=[VMEM] * 3,
        out_shape=[
            jax.ShapeDtypeStruct((half, width), F32),
            jax.ShapeDtypeStruct((half + GROUPS, width), jnp.int16),
            jax.ShapeDtypeStruct((blocks[0].shape[1], q2.shape[1]), BF16),
        ],
        scratch_shapes=[pltpu.VMEM((2, half, width), F32)],
        compiler_params=pltpu.CompilerParams(vmem_limit_bytes=16 * MIB),
        name=f"left_code_{m}",
    )(q2, inputs_t, fbq, *blocks)


def add_kernel(mine_ref, theirs_ref, out_ref):
    mine = mine_ref[...] if mine_ref.dtype == F32 else decode(mine_ref)
    encode(mine + decode(theirs_ref), out_ref)


def add_code(mine, theirs):
    return pl.pallas_call(
        add_kernel,
        in_specs=[VMEM, VMEM],
        out_specs=VMEM,
        out_shape=jax.ShapeDtypeStruct(theirs.shape, jnp.int16),
        compiler_params=pltpu.CompilerParams(vmem_limit_bytes=16 * MIB),
        name="add_code",
    )(mine, theirs)


def whole_left_kernel(mine_ref, theirs_ref, p_ref, gram_ref):
    half, width = mine_ref.shape[0] - GROUPS, mine_ref.shape[1]
    low = lax.axis_index("dp") & 1
    p_ref[pl.ds(pl.multiple_of(low * half, half), half)] = decode(mine_ref)
    p_ref[pl.ds(pl.multiple_of((1 - low) * half, half), half)] = decode(theirs_ref)
    gram_ref[...] = gram_of(p_ref[...])


def whole_left(mine, theirs):
    half, width = mine.shape[0] - GROUPS, mine.shape[1]
    return pl.pallas_call(
        whole_left_kernel,
        in_specs=[VMEM, VMEM],
        out_specs=[VMEM, VMEM],
        out_shape=[
            jax.ShapeDtypeStruct((2 * half, width), F32),
            jax.ShapeDtypeStruct((width, width), F32),
        ],
        compiler_params=pltpu.CompilerParams(vmem_limit_bytes=16 * MIB),
        name="whole_left",
    )(mine, theirs)


def full_kernel(m, held_ref, in_ref, whole_ref, out_ref):
    rows = out_ref.shape[0]
    tile = tile_of(rows)
    for i in range(rows // tile):
        part = pl.ds(i * tile, tile)
        out_ref[part] = held_ref[m, part] + mm(in_ref[part], whole_ref[...])


def full(m, held, inputs_t, whole):
    _, rows, columns = held.shape
    return pl.pallas_call(
        functools.partial(full_kernel, m),
        in_specs=[VMEM, VMEM, VMEM],
        out_specs=VMEM,
        out_shape=in_vmem((rows, columns), F32),
        compiler_params=pltpu.CompilerParams(vmem_limit_bytes=16 * MIB),
        name=f"full_{m}",
    )(stay(held), inputs_t, whole)


def right_kernel(full_ref, p_ref, mine_ref, other_ref, both_ref):
    rows, width = p_ref.shape
    tile = tile_of(rows)
    total = None
    for i in range(rows // tile):
        part = pl.ds(i * tile, tile)
        p_high, p_low = halves(p_ref[part].T)
        g_high, g_low = halves(full_ref[part])
        both = mm(jnp.concatenate([p_high, p_low], axis=0), g_high)
        term = both[:width] + both[width:] + mm(p_high, g_low)
        total = term if total is None else total + term
    lanes = both_ref.shape[2]
    tiles = total.shape[1] // lanes
    stacked = [total[:, t * lanes : (t + 1) * lanes] for t in range(tiles)]
    both_ref[...] = jnp.concatenate(stacked, axis=0).reshape(both_ref.shape)
    side = lax.axis_index("fsdp") & 1
    mine_ref[...] = both_ref[side]
    other_ref[...] = both_ref[1 - side]


def right(m, full_grad, p):
    width = p.shape[1]
    half = full_grad.shape[1] * width // LANES // 2
    return pl.pallas_call(
        right_kernel,
        in_specs=[VMEM, VMEM],
        out_specs=[VMEM, VMEM],
        out_shape=[jax.ShapeDtypeStruct((half, LANES), F32)] * 2,
        scratch_shapes=[pltpu.VMEM((2, half, LANES), F32)],
        compiler_params=pltpu.CompilerParams(vmem_limit_bytes=16 * MIB),
        name=f"right_{m}",
    )(stay(full_grad), p)


def tree(values):
    while len(values) > 1:
        values = [sum(values[i : i + 2][1:], values[i]) for i in range(0, len(values), 2)]
    return values[0]


def merge_kernel(count, plain, coded, parts, bit, *refs):
    terms, refs = refs[: plain * count], refs[plain * count :]
    codes, refs = refs[:coded], refs[coded:]
    decoded = [decode(code) for code in codes]
    rows = (decoded[0] if decoded else terms[0]).shape[0] // (count if decoded else 1)
    sums = []
    for m in range(count):
        values = [terms[t * count + m][...] for t in range(plain)]
        values += [value[m * rows : (m + 1) * rows] for value in decoded]
        sums.append(tree(values))
    if parts == 1:
        encode(jnp.concatenate(sums, axis=0), refs[0])
        return
    *outs, cut_ref = refs
    own = (lax.axis_index("fsdp") >> (bit.bit_length() - 1)) & (parts - 1)
    for m in range(count):
        cut_ref[m] = sums[m].reshape(cut_ref.shape[1:])
        outs[m][...] = cut_ref[m, own]
    for r in range(1, parts):
        encode(jnp.concatenate([cut_ref[m, own ^ r] for m in range(count)], axis=0), outs[count + r - 1])


def merge(terms, codes, name, parts=1, bit=1):
    count = len(terms[0]) if terms else 1
    if terms:
        rows = terms[0][0].shape[0]
        lanes = terms[0][0].shape[1]
    else:
        rows = codes[0].shape[0] - GROUPS
        lanes = codes[0].shape[1]
    share = rows // parts
    code = jax.ShapeDtypeStruct((count * share + GROUPS, lanes), jnp.int16)
    plain = [jax.ShapeDtypeStruct((share, lanes), F32)] * count if parts > 1 else []
    outs = plain + [code] * max(parts - 1, 1)
    flat = [x for term in terms for x in term]
    results = pl.pallas_call(
        functools.partial(merge_kernel, count, len(terms), len(codes), parts, bit),
        in_specs=[VMEM] * (len(flat) + len(codes)),
        out_specs=[VMEM] * len(outs),
        out_shape=outs,
        scratch_shapes=[pltpu.VMEM((count, parts, share, lanes), F32)] if parts > 1 else [],
        compiler_params=pltpu.CompilerParams(vmem_limit_bytes=16 * MIB),
        name=name,
    )(*flat, *codes)
    return (results[:count], results[count:]) if parts > 1 else results[0]


def gram_of(p):
    width = p.shape[1]
    high, low = halves(p)
    high_t, low_t = halves(p.T)
    both = mm(high_t, jnp.concatenate([high, low], axis=1))
    return both[:, :width] + both[:, width:] + mm(low_t, high)


def gram_kernel(p_ref, out_ref):
    out_ref[0] = gram_of(p_ref[0])


def gram(p):
    count, rows, width = p.shape
    return pl.pallas_call(
        gram_kernel,
        grid=(count,),
        in_specs=[pl.BlockSpec((1, rows, width), lambda m: (m, 0, 0))],
        out_specs=pl.BlockSpec((1, width, width), lambda m: (m, 0, 0)),
        out_shape=jax.ShapeDtypeStruct((count, width, width), F32),
        compiler_params=params(16),
        name="gram",
    )(p)


def cholesky_inverse(work, n):
    lane = lax.broadcasted_iota(jnp.int32, (8, n), 1)
    sub = lax.broadcasted_iota(jnp.int32, (8, n), 0)

    def wide(x):
        return jnp.broadcast_to(x, (8, n))

    for b in range(n // 8):
        at = 8 * b
        panels = []
        for blocks in work:
            head = blocks[b]
            columns = [wide(head[:, at + j : at + j + 1]) for j in range(8)]
            scales, lows, tops = [], [], []
            for s in range(8):
                scale = lax.rsqrt(wide(columns[s][s : s + 1, :]))
                low = columns[s] * scale
                for j in range(s + 1, 8):
                    columns[j] = columns[j] - low * wide(low[j : j + 1, :])
                row = jnp.where(lane == at + s, scale, wide(head[s : s + 1, :]) * scale)
                below = jnp.where(lane == at + s, 0.0, head) - low * row
                head = jnp.where(sub > s, below, jnp.where(sub == s, row, head))
                scales.append(scale)
                lows.append(low)
                tops.append(jnp.where((lane > at + s) & (lane < at + 8), 0.0, row))
            blocks[b] = head
            panels.append((scales, lows, tops))
        for c in range(b + 1, n // 8):
            for blocks, (scales, lows, tops) in zip(work, panels):
                x = blocks[c]
                columns = [wide(x[:, at + j : at + j + 1]) for j in range(8)]
                y = jnp.where((lane >= at) & (lane < at + 8), 0.0, x)
                for s in range(8):
                    low = columns[s] * scales[s]
                    for j in range(s + 1, 8):
                        columns[j] = columns[j] - low * wide(lows[s][j : j + 1, :])
                    y = y - low * tops[s]
                blocks[c] = y


def factor_kernel(ranks_ref, gram_ref, inv_ref):
    count, n, _ = inv_ref.shape
    lane = lax.broadcasted_iota(jnp.int32, (8, n), 1)
    sub = lax.broadcasted_iota(jnp.int32, (8, n), 0)
    work = []
    for m in range(count):
        free = jnp.where(lane < ranks_ref[m], 0.0, 1.0)
        blocks = []
        for b in range(n // 8):
            g = gram_ref[m, 8 * b : 8 * b + 8, :]
            blocks.append(jnp.where(lane == sub + 8 * b, g + free, g))
        work.append(blocks)
    cholesky_inverse(work, n)
    for m in range(count):
        for b in range(n // 8):
            inv_ref[m, 8 * b : 8 * b + 8, :] = jnp.where(lane <= sub + 8 * b, work[m][b], 0.0)


def factor(grams, ranks):
    return pl.pallas_call(
        factor_kernel,
        in_specs=[SMEM, VMEM],
        out_specs=VMEM,
        out_shape=jax.ShapeDtypeStruct(grams.shape, F32),
        compiler_params=pltpu.CompilerParams(vmem_limit_bytes=16 * MIB),
        name="factor",
    )(ranks, grams)


def factor_p_kernel(inv_ref, *refs):
    *p_refs, out_ref, p3_ref, buf_ref, sems = refs
    n = inv_ref.shape[1]
    copies = []
    for m, p_ref in enumerate(p_refs):
        i_high, i_low = halves(inv_ref[m])
        p_high, p_low = halves(p_ref[...])
        both = mm_nt(p_high, jnp.concatenate([i_high, i_low], axis=0))
        result = both[:, :n] + both[:, n:] + mm_nt(p_low, i_high)
        buf_ref[m] = result
        copies.append(pltpu.make_async_copy(buf_ref.at[m], out_ref.at[m], sems.at[m]))
        copies[-1].start()
        high, low = halves(result)
        p3_ref[m] = jnp.concatenate([high, low, high], axis=1)
    for copy in copies:
        copy.wait()


def factor_p_of(inverse, p):
    count, (rows, width) = len(p), p[0].shape
    return pl.pallas_call(
        factor_p_kernel,
        in_specs=[VMEM] * (1 + count),
        out_specs=[pl.BlockSpec(memory_space=pltpu.HBM), VMEM],
        out_shape=[
            jax.ShapeDtypeStruct((count, rows, width), F32),
            in_vmem((count, rows, 3 * width), BF16),
        ],
        scratch_shapes=[pltpu.VMEM((count, rows, width), F32), pltpu.SemaphoreType.DMA((count,))],
        compiler_params=pltpu.CompilerParams(vmem_limit_bytes=16 * MIB),
        name="factor_p",
    )(inverse, *p)


def error_kernel(count, pieces, groups, p3_ref, inv_ref, *refs):
    codes, refs = refs[:pieces], refs[pieces:]
    full_refs, (err_ref, fq_ref, right_ref, q_ref, buf_ref, sems) = refs[:count], refs[count:]
    rows, width = p3_ref.shape[1], inv_ref.shape[1]
    tile = tile_of(rows)
    share = right_ref.shape[1] // pieces
    me = lax.axis_index("fsdp") if pieces > 1 else 0
    for r, code in enumerate(codes):
        value = decode(code)
        place = (me ^ r) & 1 if pieces > 1 else 0
        for bit, members in groups:
            place = place * members + (((me ^ r) >> (bit.bit_length() - 1)) & (members - 1))
        at = pl.ds(pl.multiple_of(place * share, share), share)
        for m in range(count):
            right_ref[m, at] = value[m * share : (m + 1) * share]
    copies = []
    for m in range(count):
        i_high, i_low = halves(inv_ref[m])
        tiles = [right_ref[m, t : t + width] for t in range(0, right_ref.shape[1], width)]
        r_high, r_low = halves(jnp.concatenate(tiles, axis=1))
        both = mm(jnp.concatenate([i_high, i_low], axis=0), r_high)
        fq_t = both[:width] + both[width:] + mm(i_high, r_low)
        q_high, q_low = halves(fq_t)
        q3 = jnp.concatenate([q_high, q_high, q_low], axis=0)
        for i in range(rows // tile):
            part = pl.ds(i * tile, tile)
            buf_ref[m, part] = full_refs[m][part] - mm(p3_ref[m, part], q3)
            copies.append(
                pltpu.make_async_copy(buf_ref.at[m, part], err_ref.at[m, 0, part], sems.at[len(copies)])
            )
            copies[-1].start()
        q_ref[m] = fq_t.T
        copies.append(pltpu.make_async_copy(q_ref.at[m], fq_ref.at[m], sems.at[len(copies)]))
        copies[-1].start()
    for copy in copies:
        copy.wait()


def error(full_grad, p3, inverse, codes):
    count, rows, _ = p3.shape
    width = inverse.shape[1]
    columns = full_grad[0].shape[1]
    out = pl.BlockSpec(memory_space=pltpu.HBM)
    groups = groups_of("fsdp") if len(codes) > 1 else []
    return pl.pallas_call(
        functools.partial(error_kernel, count, len(codes), groups),
        in_specs=[VMEM] * (2 + len(codes) + count),
        out_specs=[out, out],
        out_shape=[
            jax.ShapeDtypeStruct((count, 1, rows, columns), F32),
            jax.ShapeDtypeStruct((count, columns, width), F32),
        ],
        scratch_shapes=[
            pltpu.VMEM((count, columns * width // LANES, LANES), F32),
            pltpu.VMEM((count, columns, width), F32),
            pltpu.VMEM((count, rows, columns), F32),
            pltpu.SemaphoreType.DMA((count * (rows // tile_of(rows) + 1),)),
        ],
        compiler_params=pltpu.CompilerParams(vmem_limit_bytes=24 * MIB),
        name="error",
    )(stay(p3), inverse, *codes, *[stay(x) for x in full_grad])


def power_of_two(n):
    return n & (n - 1) == 0


def across(x, axis, bit):
    size = lax.axis_size(axis)
    return lax.ppermute(x, axis, [(i, i ^ bit) for i in range(size)])


def bits_of(axis):
    size = lax.axis_size(axis)
    return [1 << b for b in range(size.bit_length() - 1)]


def groups_of(axis):
    bits = bits_of(axis)[1:]
    return [(bits[i], 1 << len(bits[i : i + 2])) for i in range(0, len(bits), 2)]


def gather_blocks(x, axis, beside=()):
    held = {0: x}
    for bit, members in groups_of(axis)[::-1]:
        for r in list(held):
            for k in range(1, members):
                held[r ^ (k * bit)] = across(held[r], axis, k * bit)
    order = list(held)
    held[order[-1]], *beside = tie(held[order[-1]], *beside)
    held.update({r ^ 1: across(held[r], axis, 1) for r in order})
    return [held[r] for r in range(len(held))], beside


def gather_cotangent(cotangent, beside):
    size = lax.axis_size("fsdp")
    count, _, width = cotangent.shape
    if power_of_two(size) and size > 1 and width % 128 == 0:
        blocks, beside = gather_blocks(cotangent, "fsdp", beside)
        return [(blocks, m) for m in range(count)], beside
    whole = lax.all_gather(cotangent, "fsdp", axis=2, tiled=True)
    return [([whole], m) for m in range(count)], beside


def tie(*values):
    return lax.optimization_barrier(values)


def sums(gram_parts, full_grad, p, ranks):
    size = lax.axis_size("fsdp")
    replicas = lax.axis_size("dp")
    count = len(p)
    if not (power_of_two(size) and size > 1):
        inverse = factor(lax.psum(jnp.stack(gram_parts), "fsdp"), ranks)
        pairs = [right(m, full_grad[m], p[m]) for m in range(count)]
        ordered = [jnp.stack(pair) for pair in pairs]
        odd = (lax.axis_index("fsdp") & 1) == 1
        whole = jnp.stack([jnp.where(odd, x[::-1], x).reshape(-1, x.shape[2]) for x in ordered])
        codes = [merge([list(lax.psum(whole, ("fsdp", "dp")))], [], "code")]
        return inverse, factor_p_of(inverse, p), codes
    groups = groups_of("fsdp")

    grams = jnp.stack(gram_parts)
    for bit in bits_of("fsdp"):
        grams = grams + across(grams, "fsdp", bit)

    pairs = [right(m, full_grad[m], p[m]) for m in range(count)]
    terms = [[mine for mine, _ in pairs], [across(other, "fsdp", 1) for _, other in pairs]]
    codes = []
    for bit, members in groups:
        keep, others = merge(terms, codes, f"part_{bit}", members, bit)
        codes = [across(others[k - 1], "fsdp", k * bit) for k in range(1, members)]
        terms = [keep]
    code = merge(terms, codes, "code")
    if power_of_two(replicas) and replicas > 1:
        theirs = [across(code, "dp", k) for k in range(1, replicas)]
        inverse = factor(grams, ranks)
        *theirs, inverse = tie(*theirs, inverse)
        code = merge([], [code] + theirs, "code_sum")
    else:
        inverse = factor(grams, ranks)
        code = merge([[lax.psum(plain(code), "dp")]], [], "code_sum")
    code, inverse = tie(code, inverse)
    codes, made = gather_blocks(code, "fsdp", factor_p_of(inverse, p))
    return inverse, made, codes


def plain_kernel(code_ref, out_ref):
    out_ref[...] = decode(code_ref)


def plain(code):
    return pl.pallas_call(
        plain_kernel,
        in_specs=[VMEM],
        out_specs=VMEM,
        out_shape=jax.ShapeDtypeStruct((code.shape[0] - GROUPS, code.shape[1]), F32),
        name="plain",
    )(code)


def left_sums(blocks, q2, inputs_t, held, fbq):
    replicas = lax.axis_size("dp")
    count = fbq.shape[0]
    if not (power_of_two(replicas) and replicas > 1):
        parts = [left(m, *blocks[m], q2, inputs_t, fbq) for m in range(count)]
        p = lax.psum(jnp.stack([part for part, _ in parts]), "dp")
        full_grad = [full(m, held, inputs_t, parts[m][1]) for m in range(count)]
        grams = gram(p)
        return [p[m] for m in range(count)], full_grad, [grams[m] for m in range(count)]
    whole, full_grad = [], []
    for m in range(count):
        mine, other, cot = left_code(m, *blocks[m], q2, inputs_t, fbq)
        mine = add_code(mine, across(other, "dp", 1))
        for step, bit in enumerate(bits_of("dp")[1:]):
            if step == 0:
                mine, cot = tie(mine, cot)
                theirs, grad = tie(across(mine, "dp", bit), full(m, held, inputs_t, cot))
                full_grad.append(grad)
            else:
                theirs = across(mine, "dp", bit)
            mine = add_code(mine, theirs)
        if len(full_grad) == m:
            full_grad.append(full(m, held, inputs_t, cot))
        whole.append(whole_left(mine, across(mine, "dp", 1)))
    return [p for p, _ in whole], full_grad, [part for _, part in whole]


def local(inputs, cotangent, feedback, q_init, factor_ranks):
    beside = feedback_q(feedback, q_init, inputs, factor_ranks)
    blocks, (held, fbq, q2, inputs_t) = gather_cotangent(cotangent, beside)
    p, full_grad, gram_parts = left_sums(blocks, q2, inputs_t, held, fbq)
    inverse, (factor_p, p3), codes = sums(gram_parts, full_grad, p, factor_ranks)
    new_error, factor_q = error(full_grad, p3, inverse, codes)
    return (factor_p, factor_q, new_error)


def solution(mesh):
    placed = (P("dp", "fsdp"), P(None, "dp", "fsdp"), P(None, "dp", "fsdp", None), P(), P())
    return jax.shard_map(
        local,
        mesh=mesh,
        in_specs=placed,
        out_specs=(P(None, "fsdp", None), P(), P(None, "dp", "fsdp", None)),
        check_vma=False,
    )
```

```python
import functools

import jax
import jax.numpy as jnp
from jax import lax
from jax.experimental import pallas as pl
from jax.experimental.pallas import tpu as pltpu
from jax.sharding import PartitionSpec as P

F32 = jnp.float32
BF16 = jnp.bfloat16
VMEM = pl.BlockSpec(memory_space=pltpu.VMEM)
SMEM = pl.BlockSpec(memory_space=pltpu.SMEM)
MIB = 1024 * 1024


def halves(x):
    high = x.astype(BF16)
    return high, (x - high.astype(F32)).astype(BF16)


def mm(a, b):
    return jnp.dot(a, b, preferred_element_type=F32)


def mm_nt(a, b):
    return lax.dot_general(a, b, (((1,), (1,)), ((), ())), preferred_element_type=F32)


def params(size, steps=1):
    return pltpu.CompilerParams(
        vmem_limit_bytes=size * MIB, dimension_semantics=("arbitrary",) * steps
    )


def tile_of(rows):
    return min(rows, 256)


def in_vmem(shape, dtype):
    return pltpu.VMEM(shape, dtype)


def stay(x):
    return pltpu.with_memory_space_constraint(x, pltpu.VMEM)


def masked_halves(q, rank):
    column = lax.broadcasted_iota(jnp.int32, q.shape, 1)
    return halves(jnp.where(column < rank, q, 0.0))


def feedback_q_kernel(
    ranks_ref, fb_ref, q_ref, in_ref, held_ref, out_ref, q2_ref, in_t_ref, ranks_own, q_own, in_own, sems, sem_q
):
    count, rows, _ = held_ref.shape
    width = q_ref.shape[2]
    tile = tile_of(rows)
    small = [
        pltpu.make_async_copy(ranks_ref, ranks_own, sem_q.at[0]),
        pltpu.make_async_copy(q_ref, q_own, sem_q.at[1]),
        pltpu.make_async_copy(in_ref, in_own, sem_q.at[2]),
    ]
    copies = []
    small[2].start()
    small[0].start()
    small[1].start()
    for m in range(count):
        for i in range(rows // tile):
            part = pl.ds(i * tile, tile)
            copies.append(
                pltpu.make_async_copy(fb_ref.at[m, 0, part], held_ref.at[m, part], sems.at[len(copies)])
            )
            copies[-1].start()
    small[2].wait()
    in_t_ref[...] = in_own[...].T
    small[0].wait()
    small[1].wait()
    for m in range(count):
        q_high, q_low = masked_halves(q_own[m], ranks_own[m])
        q2_ref[m, :, :width] = q_high
        q2_ref[m, :, width:] = q_low
    for m in range(count):
        for i in range(rows // tile):
            part = pl.ds(i * tile, tile)
            copies[m * (rows // tile) + i].wait()
            high, low = halves(held_ref[m, part])
            both = mm(high, q2_ref[m])
            out_ref[m, part] = both[:, :width] + both[:, width:] + mm(low, q2_ref[m, :, :width])


def feedback_q(feedback, q_init, inputs, ranks):
    count, _, rows, columns = feedback.shape
    width = q_init.shape[2]
    far = pl.BlockSpec(memory_space=pltpu.HBM)
    return pl.pallas_call(
        feedback_q_kernel,
        in_specs=[far] * 4,
        out_specs=[VMEM] * 4,
        out_shape=[
            in_vmem((count, rows, columns), F32),
            in_vmem((count, rows, width), F32),
            in_vmem((count, columns, 2 * width), BF16),
            in_vmem(inputs.shape[::-1], inputs.dtype),
        ],
        scratch_shapes=[
            pltpu.SMEM(ranks.shape, ranks.dtype),
            pltpu.VMEM(q_init.shape, q_init.dtype),
            pltpu.VMEM(inputs.shape, inputs.dtype),
            pltpu.SemaphoreType.DMA((count * (rows // tile_of(rows)),)),
            pltpu.SemaphoreType.DMA((3,)),
        ],
        compiler_params=pltpu.CompilerParams(vmem_limit_bytes=16 * MIB),
        name="feedback_q",
    )(*[pltpu.with_memory_space_constraint(x, pltpu.HBM) for x in (ranks, feedback, q_init, inputs)])


def fill_cotangent(blocks, at, whole_ref):
    if len(blocks) == 1:
        whole_ref[...] = blocks[0][at]
        return
    me = lax.axis_index("fsdp")
    for r, block in enumerate(blocks):
        width = block.shape[2]
        start = pl.multiple_of((me ^ r) * width, width)
        whole_ref[:, pl.ds(start, width)] = block[at]


def cotangent_q(q2_ref, m, pairs, at):
    terms = []
    for r, blocks in pairs:
        if r is None:
            terms.append(mm(blocks[0][at], q2_ref[m]))
            continue
        me = lax.axis_index("fsdp") ^ r
        width = blocks[0].shape[2]
        rows = [q2_ref[m, pl.ds(pl.multiple_of((me ^ k) * width, width), width)] for k in range(2)]
        pair = jnp.concatenate([block[at] for block in blocks], axis=1)
        terms.append(mm(pair, jnp.concatenate(rows, axis=0)))
    return sum(terms[1:], terms[0])


def paired(keys, refs):
    if keys == [None]:
        return [(None, refs)]
    return [(r, refs[2 * i : 2 * i + 2]) for i, r in enumerate(keys)]


def begin_kernel(keys, q2_ref, *refs):
    *blocks, out_ref = refs
    for m in range(out_ref.shape[0]):
        out_ref[m] = cotangent_q(q2_ref, m, paired(keys, blocks), m)


def begin(held, keys, q2):
    blocks = [held[r ^ k] for r in keys for k in range(2)]
    count, tokens, _ = blocks[0].shape
    return pl.pallas_call(
        functools.partial(begin_kernel, keys),
        in_specs=[VMEM] * (1 + len(blocks)),
        out_specs=VMEM,
        out_shape=jax.ShapeDtypeStruct((count, tokens, q2.shape[2]), F32),
        compiler_params=pltpu.CompilerParams(vmem_limit_bytes=16 * MIB),
        name="begin",
    )(q2, *blocks)


def gradient_q(both, inputs_t):
    width = both.shape[1] // 2
    c_high, c_low = halves(both[:, :width] + both[:, width:])
    both = mm(inputs_t, jnp.concatenate([c_high, c_low], axis=1))
    return both[:, :width] + both[:, width:]


def left_kernel(m, keys, q2_ref, in_ref, fbq_ref, *refs):
    *blocks, out_ref = refs
    out_ref[...] = fbq_ref[m] + gradient_q(cotangent_q(q2_ref, m, paired(keys, blocks), m), in_ref[...])


def left(m, keys, blocks, q2, inputs_t, fbq):
    _, rows, width = fbq.shape
    return pl.pallas_call(
        functools.partial(left_kernel, m, keys),
        in_specs=[VMEM] * (3 + len(blocks)),
        out_specs=VMEM,
        out_shape=jax.ShapeDtypeStruct((rows, width), F32),
        compiler_params=pltpu.CompilerParams(vmem_limit_bytes=16 * MIB),
        name=f"left_{m}",
    )(q2, inputs_t, fbq, *blocks)


GROUPS = 16
LANES = 128


def encode(x, out_ref):
    rows, width = x.shape
    grouped = x.reshape(GROUPS, rows // GROUPS, width)
    top = jnp.max(jnp.abs(grouped), axis=1)
    level = jnp.ceil(jnp.log(jnp.maximum(top, 1e-30)) * 32.0) + 1.0
    up = jnp.exp(level * (-1.0 / 32.0)) * 32767.0
    code = jnp.round(grouped * up[:, None, :]).reshape(rows, width)
    out_ref[:rows] = code.astype(jnp.int32).astype(jnp.int16)
    out_ref[rows:] = level.astype(jnp.int32).astype(jnp.int16)


def decode(ref):
    rows = ref.shape[0] - GROUPS
    width = ref.shape[1]
    level = ref[rows:].astype(jnp.int32).astype(F32)
    down = jnp.exp(level * (1.0 / 32.0)) * (1.0 / 32767.0)
    code = ref[:rows].astype(jnp.int32).astype(F32).reshape(GROUPS, rows // GROUPS, width)
    return (code * down[:, None, :]).reshape(rows, width)


def decode_part(ref, part, count):
    rows, width = ref.shape[0] - GROUPS, ref.shape[1]
    own, groups = rows // count, GROUPS // count
    level = ref[rows:].astype(jnp.int32).astype(F32)[part * groups : (part + 1) * groups]
    down = jnp.exp(level * (1.0 / 32.0)) * (1.0 / 32767.0)
    code = ref[part * own : (part + 1) * own].astype(jnp.int32).astype(F32)
    return (code.reshape(groups, own // groups, width) * down[:, None, :]).reshape(own, width)


def left_code_kernel(m, keys, q2_ref, in_ref, fbq_ref, *refs):
    *refs, mine_ref, code_ref, p_ref = refs
    if keys == [None]:
        both = cotangent_q(q2_ref, m, paired(keys, refs), m)
    else:
        both = refs[0][m] + cotangent_q(q2_ref, m, paired(keys, refs[1:]), m)
    p = fbq_ref[m] + gradient_q(both, in_ref[...])
    p_ref[...] = p.reshape(p_ref.shape)
    low = lax.axis_index("dp") & 1
    mine_ref[...] = p_ref[low]
    encode(p_ref[1 - low], code_ref)


def left_code(m, keys, begun, blocks, q2, inputs_t, fbq):
    _, rows, width = fbq.shape
    half = rows // 2
    return pl.pallas_call(
        functools.partial(left_code_kernel, m, keys),
        in_specs=[VMEM] * (3 + len(begun) + len(blocks)),
        out_specs=[VMEM] * 2,
        out_shape=[
            jax.ShapeDtypeStruct((half, width), F32),
            jax.ShapeDtypeStruct((half + GROUPS, width), jnp.int16),
        ],
        scratch_shapes=[pltpu.VMEM((2, half, width), F32)],
        compiler_params=pltpu.CompilerParams(vmem_limit_bytes=16 * MIB),
        name=f"left_code_{m}",
    )(q2, inputs_t, fbq, *begun, *blocks)


def add_kernel(mine_ref, theirs_ref, out_ref):
    mine = mine_ref[...] if mine_ref.dtype == F32 else decode(mine_ref)
    encode(mine + decode(theirs_ref), out_ref)


def add_code(mine, theirs):
    return pl.pallas_call(
        add_kernel,
        in_specs=[VMEM, VMEM],
        out_specs=VMEM,
        out_shape=jax.ShapeDtypeStruct(theirs.shape, jnp.int16),
        compiler_params=pltpu.CompilerParams(vmem_limit_bytes=16 * MIB),
        name="add_code",
    )(mine, theirs)


def halves_code_kernel(p_ref, first_ref, second_ref):
    half = p_ref.shape[0] // 2
    encode(p_ref[:half], first_ref)
    encode(p_ref[half:], second_ref)


def halves_code(p):
    code = jax.ShapeDtypeStruct((p.shape[0] // 2 + GROUPS, p.shape[1]), jnp.int16)
    return pl.pallas_call(
        halves_code_kernel,
        in_specs=[VMEM],
        out_specs=[VMEM, VMEM],
        out_shape=[code, code],
        compiler_params=pltpu.CompilerParams(vmem_limit_bytes=16 * MIB),
        name="halves_code",
    )(p)


def full_kernel(m, held_ref, in_ref, *refs):
    *blocks, out_ref, whole_ref = refs
    fill_cotangent(blocks, m, whole_ref)
    rows = out_ref.shape[0]
    tile = tile_of(rows)
    for i in range(rows // tile):
        part = pl.ds(i * tile, tile)
        out_ref[part] = held_ref[m, part] + mm(in_ref[part], whole_ref[...])


def full(m, held, inputs_t, blocks):
    _, rows, columns = held.shape
    return pl.pallas_call(
        functools.partial(full_kernel, m),
        in_specs=[VMEM] * (2 + len(blocks)),
        out_specs=VMEM,
        out_shape=in_vmem((rows, columns), F32),
        scratch_shapes=[pltpu.VMEM((inputs_t.shape[1], columns), BF16)],
        compiler_params=pltpu.CompilerParams(vmem_limit_bytes=16 * MIB),
        name=f"full_{m}",
    )(stay(held), inputs_t, *blocks)


def half_of(halved):
    return lax.axis_index("dp") & 1 if halved else 0


def half_products(full_ref, code_ref, which):
    half, width = code_ref.shape[0] - GROUPS, code_ref.shape[1]
    tile = tile_of(half)
    p = decode(code_ref)
    total = None
    for i in range(half // tile):
        p_high, p_low = halves(p[i * tile : (i + 1) * tile].T)
        start = pl.multiple_of(which * half + i * tile, tile)
        g_high, g_low = halves(full_ref[pl.ds(start, tile)])
        both = mm(jnp.concatenate([p_high, p_low], axis=0), g_high)
        term = both[:width] + both[width:] + mm(p_high, g_low)
        total = term if total is None else total + term
    return total, gram_of(p)


def own_half_kernel(halved, full_ref, code_ref, total_ref, gram_ref):
    total_ref[...], gram_ref[...] = half_products(full_ref, code_ref, half_of(halved))


def own_half(m, halved, full_grad, code):
    width = code.shape[1]
    return pl.pallas_call(
        functools.partial(own_half_kernel, halved),
        in_specs=[VMEM, VMEM],
        out_specs=[VMEM, VMEM],
        out_shape=[
            jax.ShapeDtypeStruct((width, full_grad.shape[1]), F32),
            jax.ShapeDtypeStruct((width, width), F32),
        ],
        compiler_params=pltpu.CompilerParams(vmem_limit_bytes=16 * MIB),
        name=f"own_half_{m}",
    )(stay(full_grad), code)


def other_half_kernel(halved, full_ref, code_ref, total_ref, part_ref, mine_ref, other_ref, gram_ref, both_ref):
    total, gram = half_products(full_ref, code_ref, 1 - half_of(halved))
    gram_ref[...] = part_ref[...] + gram
    total = total_ref[...] + total
    lanes = both_ref.shape[2]
    stacked = [total[:, t : t + lanes] for t in range(0, total.shape[1], lanes)]
    both_ref[...] = jnp.concatenate(stacked, axis=0).reshape(both_ref.shape)
    side = lax.axis_index("fsdp") & 1
    mine_ref[...] = both_ref[side]
    other_ref[...] = both_ref[1 - side]


def other_half(m, halved, full_grad, code, total, part):
    half = total.size // LANES // 2
    return pl.pallas_call(
        functools.partial(other_half_kernel, halved),
        in_specs=[VMEM] * 4,
        out_specs=[VMEM] * 3,
        out_shape=[jax.ShapeDtypeStruct((half, LANES), F32)] * 2 + [jax.ShapeDtypeStruct(part.shape, F32)],
        scratch_shapes=[pltpu.VMEM((2, half, LANES), F32)],
        compiler_params=pltpu.CompilerParams(vmem_limit_bytes=16 * MIB),
        name=f"other_half_{m}",
    )(stay(full_grad), code, total, part)


def tree(values):
    while len(values) > 1:
        values = [sum(values[i : i + 2][1:], values[i]) for i in range(0, len(values), 2)]
    return values[0]


def merge_kernel(count, plain, coded, parts, bit, *refs):
    terms, refs = refs[: plain * count], refs[plain * count :]
    codes, refs = refs[:coded], refs[coded:]
    decoded = [decode(code) for code in codes]
    rows = (decoded[0] if decoded else terms[0]).shape[0] // (count if decoded else 1)
    sums = []
    for m in range(count):
        values = [terms[t * count + m][...] for t in range(plain)]
        values += [value[m * rows : (m + 1) * rows] for value in decoded]
        sums.append(tree(values))
    if parts == 1:
        encode(jnp.concatenate(sums, axis=0), refs[0])
        return
    *outs, cut_ref = refs
    own = (lax.axis_index("fsdp") >> (bit.bit_length() - 1)) & (parts - 1)
    for m in range(count):
        cut_ref[m] = sums[m].reshape(cut_ref.shape[1:])
        outs[m][...] = cut_ref[m, own]
    for r in range(1, parts):
        encode(jnp.concatenate([cut_ref[m, own ^ r] for m in range(count)], axis=0), outs[count + r - 1])


def merge(terms, codes, name, parts=1, bit=1):
    count = len(terms[0]) if terms else 1
    if terms:
        rows = terms[0][0].shape[0]
        lanes = terms[0][0].shape[1]
    else:
        rows = codes[0].shape[0] - GROUPS
        lanes = codes[0].shape[1]
    share = rows // parts
    code = jax.ShapeDtypeStruct((count * share + GROUPS, lanes), jnp.int16)
    plain = [jax.ShapeDtypeStruct((share, lanes), F32)] * count if parts > 1 else []
    outs = plain + [code] * max(parts - 1, 1)
    flat = [x for term in terms for x in term]
    results = pl.pallas_call(
        functools.partial(merge_kernel, count, len(terms), len(codes), parts, bit),
        in_specs=[VMEM] * (len(flat) + len(codes)),
        out_specs=[VMEM] * len(outs),
        out_shape=outs,
        scratch_shapes=[pltpu.VMEM((count, parts, share, lanes), F32)] if parts > 1 else [],
        compiler_params=pltpu.CompilerParams(vmem_limit_bytes=16 * MIB),
        name=name,
    )(*flat, *codes)
    return (results[:count], results[count:]) if parts > 1 else results[0]


def gram_of(p):
    width = p.shape[1]
    high, low = halves(p)
    high_t, low_t = halves(p.T)
    both = mm(high_t, jnp.concatenate([high, low], axis=1))
    return both[:, :width] + both[:, width:] + mm(low_t, high)


def cholesky_inverse(work, n):
    lane = lax.broadcasted_iota(jnp.int32, (8, n), 1)
    sub = lax.broadcasted_iota(jnp.int32, (8, n), 0)

    def wide(x):
        return jnp.broadcast_to(x, (8, n))

    for b in range(n // 8):
        at = 8 * b
        panels = []
        for blocks in work:
            head = blocks[b]
            columns = [wide(head[:, at + j : at + j + 1]) for j in range(8)]
            scales, lows, tops = [], [], []
            for s in range(8):
                scale = lax.rsqrt(wide(columns[s][s : s + 1, :]))
                low = columns[s] * scale
                for j in range(s + 1, 8):
                    columns[j] = columns[j] - low * wide(low[j : j + 1, :])
                row = jnp.where(lane == at + s, scale, wide(head[s : s + 1, :]) * scale)
                below = jnp.where(lane == at + s, 0.0, head) - low * row
                head = jnp.where(sub > s, below, jnp.where(sub == s, row, head))
                scales.append(scale)
                lows.append(low)
                tops.append(jnp.where((lane > at + s) & (lane < at + 8), 0.0, row))
            blocks[b] = head
            panels.append((scales, lows, tops))
        for c in range(b + 1, n // 8):
            for blocks, (scales, lows, tops) in zip(work, panels):
                x = blocks[c]
                columns = [wide(x[:, at + j : at + j + 1]) for j in range(8)]
                y = jnp.where((lane >= at) & (lane < at + 8), 0.0, x)
                for s in range(8):
                    low = columns[s] * scales[s]
                    for j in range(s + 1, 8):
                        columns[j] = columns[j] - low * wide(lows[s][j : j + 1, :])
                    y = y - low * tops[s]
                blocks[c] = y


def factor_kernel(ranks_ref, gram_ref, inv_ref):
    count, n, _ = inv_ref.shape
    lane = lax.broadcasted_iota(jnp.int32, (8, n), 1)
    sub = lax.broadcasted_iota(jnp.int32, (8, n), 0)
    work = []
    for m in range(count):
        free = jnp.where(lane < ranks_ref[m], 0.0, 1.0)
        blocks = []
        for b in range(n // 8):
            g = gram_ref[m, 8 * b : 8 * b + 8, :]
            blocks.append(jnp.where(lane == sub + 8 * b, g + free, g))
        work.append(blocks)
    cholesky_inverse(work, n)
    for m in range(count):
        for b in range(n // 8):
            inv_ref[m, 8 * b : 8 * b + 8, :] = jnp.where(lane <= sub + 8 * b, work[m][b], 0.0)


def factor(grams, ranks):
    return pl.pallas_call(
        factor_kernel,
        in_specs=[SMEM, VMEM],
        out_specs=VMEM,
        out_shape=jax.ShapeDtypeStruct(grams.shape, F32),
        compiler_params=pltpu.CompilerParams(vmem_limit_bytes=16 * MIB),
        name="factor",
    )(ranks, grams)


def factor_p_kernel(halved, inv_ref, *refs):
    *codes, out_ref, p3_ref, buf_ref, sems = refs
    n = inv_ref.shape[1]
    which = half_of(halved)
    copies = []
    for m in range(inv_ref.shape[0]):
        i_high, i_low = halves(inv_ref[m])
        i_both = jnp.concatenate([i_high, i_low], axis=0)
        for code, place in ((codes[2 * m], which), (codes[2 * m + 1], 1 - which)):
            p_high, p_low = halves(decode(code))
            rows = p_high.shape[0]
            part = pl.ds(pl.multiple_of(place * rows, rows), rows)
            both = mm_nt(p_high, i_both)
            result = both[:, :n] + both[:, n:] + mm_nt(p_low, i_high)
            buf_ref[m, part] = result
            high, low = halves(result)
            p3_ref[m, part] = jnp.concatenate([high, low, high], axis=1)
        copies.append(pltpu.make_async_copy(buf_ref.at[m], out_ref.at[m], sems.at[m]))
        copies[-1].start()
    for copy in copies:
        copy.wait()


def factor_p_of(halved, inverse, codes):
    count, rows, width = len(codes), 2 * (codes[0][0].shape[0] - GROUPS), codes[0][0].shape[1]
    return pl.pallas_call(
        functools.partial(factor_p_kernel, halved),
        in_specs=[VMEM] * (1 + 2 * count),
        out_specs=[pl.BlockSpec(memory_space=pltpu.HBM), VMEM],
        out_shape=[
            jax.ShapeDtypeStruct((count, rows, width), F32),
            in_vmem((count, rows, 3 * width), BF16),
        ],
        scratch_shapes=[pltpu.VMEM((count, rows, width), F32), pltpu.SemaphoreType.DMA((count,))],
        compiler_params=pltpu.CompilerParams(vmem_limit_bytes=16 * MIB),
        name="factor_p",
    )(inverse, *[code for pair in codes for code in pair])


def error_kernel(count, pieces, groups, p3_ref, inv_ref, *refs):
    codes, refs = refs[:pieces], refs[pieces:]
    full_refs, (err_ref, fq_ref, right_ref, q_ref, buf_ref, sems) = refs[:count], refs[count:]
    rows, width = p3_ref.shape[1], inv_ref.shape[1]
    tile = min(rows, LANES)
    share = right_ref.shape[1] // pieces
    me = lax.axis_index("fsdp") if pieces > 1 else 0
    copies = []
    for m in range(count):
        for r, code in enumerate(codes):
            place = (me ^ r) & 1 if pieces > 1 else 0
            for bit, members in groups:
                place = place * members + (((me ^ r) >> (bit.bit_length() - 1)) & (members - 1))
            at = pl.ds(pl.multiple_of(place * share, share), share)
            right_ref[m, at] = decode_part(code, m, count)
        i_high, i_low = halves(inv_ref[m])
        tiles = [right_ref[m, t : t + width] for t in range(0, right_ref.shape[1], width)]
        r_high, r_low = halves(jnp.concatenate(tiles, axis=1))
        both = mm(jnp.concatenate([i_high, i_low], axis=0), r_high)
        fq_t = both[:width] + both[width:] + mm(i_high, r_low)
        q_high, q_low = halves(fq_t)
        q3 = jnp.concatenate([q_high, q_high, q_low], axis=0)
        for start in range(0, rows, tile):
            part = pl.ds(start, tile)
            buf_ref[m, part] = full_refs[m][part] - mm(p3_ref[m, part], q3)
            copies.append(
                pltpu.make_async_copy(buf_ref.at[m, part], err_ref.at[m, 0, part], sems.at[len(copies)])
            )
            copies[-1].start()
        q_ref[m] = fq_t.T
        copies.append(pltpu.make_async_copy(q_ref.at[m], fq_ref.at[m], sems.at[len(copies)]))
        copies[-1].start()
    for copy in copies:
        copy.wait()


def error(full_grad, p3, inverse, codes):
    count, rows, _ = p3.shape
    width = inverse.shape[1]
    columns = full_grad[0].shape[1]
    out = pl.BlockSpec(memory_space=pltpu.HBM)
    groups = groups_of("fsdp") if len(codes) > 1 else []
    return pl.pallas_call(
        functools.partial(error_kernel, count, len(codes), groups),
        in_specs=[VMEM] * (2 + len(codes) + count),
        out_specs=[out, out],
        out_shape=[
            jax.ShapeDtypeStruct((count, 1, rows, columns), F32),
            jax.ShapeDtypeStruct((count, columns, width), F32),
        ],
        scratch_shapes=[
            pltpu.VMEM((count, columns * width // LANES, LANES), F32),
            pltpu.VMEM((count, columns, width), F32),
            pltpu.VMEM((count, rows, columns), F32),
            pltpu.SemaphoreType.DMA((count * (rows // min(rows, LANES) + 1),)),
        ],
        compiler_params=pltpu.CompilerParams(vmem_limit_bytes=24 * MIB),
        name="error",
    )(stay(p3), inverse, *codes, *[stay(x) for x in full_grad])


def power_of_two(n):
    return n & (n - 1) == 0


def across(x, axis, bit):
    size = lax.axis_size(axis)
    return lax.ppermute(x, axis, [(i, i ^ bit) for i in range(size)])


def bits_of(axis):
    size = lax.axis_size(axis)
    return [1 << b for b in range(size.bit_length() - 1)]


def groups_of(axis):
    bits = bits_of(axis)[1:]
    return [(bits[i], 1 << len(bits[i : i + 2])) for i in range(0, len(bits), 2)]


def gather_slow(x, axis):
    held = {0: x}
    for bit, members in groups_of(axis)[::-1]:
        for r in list(held):
            for k in range(1, members):
                held[r ^ (k * bit)] = across(held[r], axis, k * bit)
    return held


def gather_blocks(x, axis, beside=()):
    held = gather_slow(x, axis)
    order = list(held)
    held[order[-1]], *beside = tie(held[order[-1]], *beside)
    held.update({r ^ 1: across(held[r], axis, 1) for r in order})
    return [held[r] for r in range(len(held))], beside


def gather_cotangent(cotangent, beside):
    size = lax.axis_size("fsdp")
    width = cotangent.shape[2]
    if not (power_of_two(size) and size > 1 and width % 128 == 0):
        return [lax.all_gather(cotangent, "fsdp", axis=2, tiled=True)], [None], [], beside
    held = gather_slow(cotangent, "fsdp")
    *order, last = list(held)
    values = tie(*[held[r] for r in order], *beside)
    held.update(zip(order, values))
    beside = values[len(order) :]
    swapped = [across(held[r], "fsdp", 1) for r in order]
    held[last], *swapped = tie(held[last], *swapped)
    held.update({r ^ 1: x for r, x in zip(order, swapped)})
    begun = begin(held, order, beside[2])
    held[last ^ 1] = across(held[last], "fsdp", 1)
    return [held[r] for r in range(len(held))], [last], [begun], beside


def tie(*values):
    return lax.optimization_barrier(values)


def sums(halved, grams, pairs, p_codes, ranks):
    size = lax.axis_size("fsdp")
    replicas = lax.axis_size("dp")
    if not (power_of_two(size) and size > 1):
        inverse = factor(lax.psum(grams, "fsdp"), ranks)
        ordered = [jnp.stack(pair) for pair in pairs]
        odd = (lax.axis_index("fsdp") & 1) == 1
        whole = jnp.stack([jnp.where(odd, x[::-1], x).reshape(-1, x.shape[2]) for x in ordered])
        codes = [merge([list(lax.psum(whole, ("fsdp", "dp")))], [], "code")]
        return inverse, factor_p_of(halved, inverse, p_codes), codes
    groups = groups_of("fsdp")

    for bit in bits_of("fsdp"):
        grams = grams + across(grams, "fsdp", bit)

    terms = [[mine for mine, _ in pairs], [across(other, "fsdp", 1) for _, other in pairs]]
    codes = []
    for bit, members in groups:
        keep, others = merge(terms, codes, f"part_{bit}", members, bit)
        codes = [across(others[k - 1], "fsdp", k * bit) for k in range(1, members)]
        terms = [keep]
    code = merge(terms, codes, "code")
    if power_of_two(replicas) and replicas > 1:
        theirs = [across(code, "dp", k) for k in range(1, replicas)]
        inverse = factor(grams, ranks)
        *theirs, inverse = tie(*theirs, inverse)
        code = merge([], [code] + theirs, "code_sum")
    else:
        inverse = factor(grams, ranks)
        code = merge([[lax.psum(plain(code), "dp")]], [], "code_sum")
    code, inverse = tie(code, inverse)
    codes, made = gather_blocks(code, "fsdp", factor_p_of(halved, inverse, p_codes))
    return inverse, made, codes


def plain_kernel(code_ref, out_ref):
    out_ref[...] = decode(code_ref)


def plain(code):
    return pl.pallas_call(
        plain_kernel,
        in_specs=[VMEM],
        out_specs=VMEM,
        out_shape=jax.ShapeDtypeStruct((code.shape[0] - GROUPS, code.shape[1]), F32),
        name="plain",
    )(code)


def left_sums(halved, blocks, keys, begun, q2, inputs_t, held, fbq):
    count = fbq.shape[0]
    codes, full_grad, pairs, grams = [], [], [], []
    if not halved:
        pairs_of = [None] if keys == [None] else list(range(0, len(blocks), 2))
        p = lax.psum(jnp.stack([left(m, pairs_of, blocks, q2, inputs_t, fbq) for m in range(count)]), "dp")
        for m in range(count):
            full_grad.append(full(m, held, inputs_t, blocks))
            codes.append(halves_code(p[m]))
            total, part = own_half(m, halved, full_grad[m], codes[m][0])
            *pair, part = other_half(m, halved, full_grad[m], codes[m][1], total, part)
            pairs.append(pair)
            grams.append(part)
        return codes, full_grad, pairs, jnp.stack(grams)
    steps = bits_of("dp")[1:]
    mines = []
    late = blocks if keys == [None] else [blocks[r ^ k] for r in keys for k in range(2)]
    for m in range(count):
        mine, other = left_code(m, keys, begun, late, q2, inputs_t, fbq)
        mines.append(add_code(mine, across(other, "dp", 1)))
    own, late = {}, None
    for m in range(count)[::-1]:
        mine, in_t = tie(mines[m], inputs_t)
        grad = full(m, held, in_t, blocks)
        for bit in steps:
            theirs, grad = tie(across(mine, "dp", bit), grad)
            if late is not None:
                theirs, *own[late] = tie(theirs, *own[late])
            mine = add_code(mine, theirs)
        mines[m] = mine
        full_grad.insert(0, grad)
        own[m] = list(own_half(m, halved, grad, mine))
        late = m
    for m in range(count):
        codes.append((mines[m], across(mines[m], "dp", 1)))
        *pair, part = other_half(m, halved, full_grad[m], codes[m][1], *own[m])
        pairs.append(pair)
        grams.append(part)
    return codes, full_grad, pairs, jnp.stack(grams)


def local(inputs, cotangent, feedback, q_init, factor_ranks):
    replicas = lax.axis_size("dp")
    halved = power_of_two(replicas) and replicas > 1
    beside = feedback_q(feedback, q_init, inputs, factor_ranks)
    blocks, keys, begun, (held, fbq, q2, inputs_t) = gather_cotangent(cotangent, beside)
    p_codes, full_grad, pairs, grams = left_sums(halved, blocks, keys, begun, q2, inputs_t, held, fbq)
    inverse, (factor_p, p3), codes = sums(halved, grams, pairs, p_codes, factor_ranks)
    new_error, factor_q = error(full_grad, p3, inverse, codes)
    return (factor_p, factor_q, new_error)


def solution(mesh):
    placed = (P("dp", "fsdp"), P(None, "dp", "fsdp"), P(None, "dp", "fsdp", None), P(), P())
    return jax.shard_map(
        local,
        mesh=mesh,
        in_specs=placed,
        out_specs=(P(None, "fsdp", None), P(), P(None, "dp", "fsdp", None)),
        check_vma=False,
    )
```

```python
import functools

import jax
import jax.numpy as jnp
from jax import lax
from jax.experimental import pallas as pl
from jax.experimental.pallas import tpu as pltpu
from jax.sharding import PartitionSpec as P

F32 = jnp.float32
BF16 = jnp.bfloat16
VMEM = pl.BlockSpec(memory_space=pltpu.VMEM)
SMEM = pl.BlockSpec(memory_space=pltpu.SMEM)
MIB = 1024 * 1024


def halves(x):
    high = x.astype(BF16)
    return high, (x - high.astype(F32)).astype(BF16)


def mm(a, b):
    return jnp.dot(a, b, preferred_element_type=F32)


def mm_nt(a, b):
    return lax.dot_general(a, b, (((1,), (1,)), ((), ())), preferred_element_type=F32)


def params(size, steps=1):
    return pltpu.CompilerParams(
        vmem_limit_bytes=size * MIB, dimension_semantics=("arbitrary",) * steps
    )


def tile_of(rows):
    return min(rows, 256)


def in_vmem(shape, dtype):
    return pltpu.VMEM(shape, dtype)


def stay(x):
    return pltpu.with_memory_space_constraint(x, pltpu.VMEM)


def masked_halves(q, rank):
    column = lax.broadcasted_iota(jnp.int32, q.shape, 1)
    return halves(jnp.where(column < rank, q, 0.0))


def feedback_q_kernel(
    ranks_ref, fb_ref, q_ref, in_ref, held_ref, out_ref, q2_ref, in_t_ref, ranks_own, q_own, in_own, sems, sem_q
):
    count, rows, _ = held_ref.shape
    width = q_ref.shape[2]
    tile = tile_of(rows)
    small = [
        pltpu.make_async_copy(ranks_ref, ranks_own, sem_q.at[0]),
        pltpu.make_async_copy(q_ref, q_own, sem_q.at[1]),
        pltpu.make_async_copy(in_ref, in_own, sem_q.at[2]),
    ]
    copies = []
    small[2].start()
    small[0].start()
    small[1].start()
    for m in range(count):
        for i in range(rows // tile):
            part = pl.ds(i * tile, tile)
            copies.append(
                pltpu.make_async_copy(fb_ref.at[m, 0, part], held_ref.at[m, part], sems.at[len(copies)])
            )
            copies[-1].start()
    small[2].wait()
    in_t_ref[...] = in_own[...].T
    small[0].wait()
    small[1].wait()
    for m in range(count):
        q_high, q_low = masked_halves(q_own[m], ranks_own[m])
        q2_ref[m, :, :width] = q_high
        q2_ref[m, :, width:] = q_low
    for m in range(count):
        for i in range(rows // tile):
            part = pl.ds(i * tile, tile)
            copies[m * (rows // tile) + i].wait()
            high, low = halves(held_ref[m, part])
            both = mm(high, q2_ref[m])
            out_ref[m, part] = both[:, :width] + both[:, width:] + mm(low, q2_ref[m, :, :width])


def feedback_q(feedback, q_init, inputs, ranks):
    count, _, rows, columns = feedback.shape
    width = q_init.shape[2]
    far = pl.BlockSpec(memory_space=pltpu.HBM)
    return pl.pallas_call(
        feedback_q_kernel,
        in_specs=[far] * 4,
        out_specs=[VMEM] * 4,
        out_shape=[
            in_vmem((count, rows, columns), F32),
            in_vmem((count, rows, width), F32),
            in_vmem((count, columns, 2 * width), BF16),
            in_vmem(inputs.shape[::-1], inputs.dtype),
        ],
        scratch_shapes=[
            pltpu.SMEM(ranks.shape, ranks.dtype),
            pltpu.VMEM(q_init.shape, q_init.dtype),
            pltpu.VMEM(inputs.shape, inputs.dtype),
            pltpu.SemaphoreType.DMA((count * (rows // tile_of(rows)),)),
            pltpu.SemaphoreType.DMA((3,)),
        ],
        compiler_params=pltpu.CompilerParams(vmem_limit_bytes=16 * MIB),
        name="feedback_q",
    )(*[pltpu.with_memory_space_constraint(x, pltpu.HBM) for x in (ranks, feedback, q_init, inputs)])


def fill_cotangent(blocks, at, whole_ref):
    if len(blocks) == 1:
        whole_ref[...] = blocks[0][at]
        return
    me = lax.axis_index("fsdp")
    for r, block in enumerate(blocks):
        width = block.shape[2]
        start = pl.multiple_of((me ^ r) * width, width)
        whole_ref[:, pl.ds(start, width)] = block[at]


def cotangent_q(q2_ref, m, pairs, at):
    terms = []
    for r, blocks in pairs:
        if r is None:
            terms.append(mm(blocks[0][at], q2_ref[m]))
            continue
        me = lax.axis_index("fsdp") ^ r
        width = blocks[0].shape[2]
        rows = [q2_ref[m, pl.ds(pl.multiple_of((me ^ k) * width, width), width)] for k in range(2)]
        pair = jnp.concatenate([block[at] for block in blocks], axis=1)
        terms.append(mm(pair, jnp.concatenate(rows, axis=0)))
    return sum(terms[1:], terms[0])


def paired(keys, refs):
    if keys == [None]:
        return [(None, refs)]
    return [(r, refs[2 * i : 2 * i + 2]) for i, r in enumerate(keys)]


def begin_kernel(keys, q2_ref, *refs):
    *blocks, out_ref = refs
    for m in range(out_ref.shape[0]):
        out_ref[m] = cotangent_q(q2_ref, m, paired(keys, blocks), m)


def begin(held, keys, q2):
    blocks = [held[r ^ k] for r in keys for k in range(2)]
    count, tokens, _ = blocks[0].shape
    return pl.pallas_call(
        functools.partial(begin_kernel, keys),
        in_specs=[VMEM] * (1 + len(blocks)),
        out_specs=VMEM,
        out_shape=jax.ShapeDtypeStruct((count, tokens, q2.shape[2]), F32),
        compiler_params=pltpu.CompilerParams(vmem_limit_bytes=16 * MIB),
        name="begin",
    )(q2, *blocks)


def gradient_q(both, inputs_t):
    width = both.shape[1] // 2
    c_high, c_low = halves(both[:, :width] + both[:, width:])
    both = mm(inputs_t, jnp.concatenate([c_high, c_low], axis=1))
    return both[:, :width] + both[:, width:]


def left_kernel(m, keys, q2_ref, in_ref, fbq_ref, *refs):
    *blocks, out_ref = refs
    out_ref[...] = fbq_ref[m] + gradient_q(cotangent_q(q2_ref, m, paired(keys, blocks), m), in_ref[...])


def left(m, keys, blocks, q2, inputs_t, fbq):
    _, rows, width = fbq.shape
    return pl.pallas_call(
        functools.partial(left_kernel, m, keys),
        in_specs=[VMEM] * (3 + len(blocks)),
        out_specs=VMEM,
        out_shape=jax.ShapeDtypeStruct((rows, width), F32),
        compiler_params=pltpu.CompilerParams(vmem_limit_bytes=16 * MIB),
        name=f"left_{m}",
    )(q2, inputs_t, fbq, *blocks)


GROUPS = 16
LANES = 128


def encode(x, out_ref):
    rows, width = x.shape
    grouped = x.reshape(GROUPS, rows // GROUPS, width)
    top = jnp.max(jnp.abs(grouped), axis=1)
    level = jnp.ceil(jnp.log(jnp.maximum(top, 1e-30)) * 32.0) + 1.0
    up = jnp.exp(level * (-1.0 / 32.0)) * 32767.0
    code = jnp.round(grouped * up[:, None, :]).reshape(rows, width)
    out_ref[:rows] = code.astype(jnp.int32).astype(jnp.int16)
    out_ref[rows:] = level.astype(jnp.int32).astype(jnp.int16)


def decode(ref):
    rows = ref.shape[0] - GROUPS
    width = ref.shape[1]
    level = ref[rows:].astype(jnp.int32).astype(F32)
    down = jnp.exp(level * (1.0 / 32.0)) * (1.0 / 32767.0)
    code = ref[:rows].astype(jnp.int32).astype(F32).reshape(GROUPS, rows // GROUPS, width)
    return (code * down[:, None, :]).reshape(rows, width)


def decode_part(ref, part, count):
    rows, width = ref.shape[0] - GROUPS, ref.shape[1]
    own, groups = rows // count, GROUPS // count
    level = ref[rows:].astype(jnp.int32).astype(F32)[part * groups : (part + 1) * groups]
    down = jnp.exp(level * (1.0 / 32.0)) * (1.0 / 32767.0)
    code = ref[part * own : (part + 1) * own].astype(jnp.int32).astype(F32)
    return (code.reshape(groups, own // groups, width) * down[:, None, :]).reshape(own, width)


def left_code_kernel(m, keys, q2_ref, in_ref, fbq_ref, *refs):
    *refs, mine_ref, code_ref, p_ref = refs
    if keys == [None]:
        both = cotangent_q(q2_ref, m, paired(keys, refs), m)
    else:
        both = refs[0][m] + cotangent_q(q2_ref, m, paired(keys, refs[1:]), m)
    p = fbq_ref[m] + gradient_q(both, in_ref[...])
    p_ref[...] = p.reshape(p_ref.shape)
    low = lax.axis_index("dp") & 1
    mine_ref[...] = p_ref[low]
    encode(p_ref[1 - low], code_ref)


def left_code(m, keys, begun, blocks, q2, inputs_t, fbq):
    _, rows, width = fbq.shape
    half = rows // 2
    return pl.pallas_call(
        functools.partial(left_code_kernel, m, keys),
        in_specs=[VMEM] * (3 + len(begun) + len(blocks)),
        out_specs=[VMEM] * 2,
        out_shape=[
            jax.ShapeDtypeStruct((half, width), F32),
            jax.ShapeDtypeStruct((half + GROUPS, width), jnp.int16),
        ],
        scratch_shapes=[pltpu.VMEM((2, half, width), F32)],
        compiler_params=pltpu.CompilerParams(vmem_limit_bytes=16 * MIB),
        name=f"left_code_{m}",
    )(q2, inputs_t, fbq, *begun, *blocks)


def add_kernel(mine_ref, theirs_ref, out_ref):
    mine = mine_ref[...] if mine_ref.dtype == F32 else decode(mine_ref)
    encode(mine + decode(theirs_ref), out_ref)


def add_code(mine, theirs):
    return pl.pallas_call(
        add_kernel,
        in_specs=[VMEM, VMEM],
        out_specs=VMEM,
        out_shape=jax.ShapeDtypeStruct(theirs.shape, jnp.int16),
        compiler_params=pltpu.CompilerParams(vmem_limit_bytes=16 * MIB),
        name="add_code",
    )(mine, theirs)


def halves_code_kernel(p_ref, first_ref, second_ref):
    half = p_ref.shape[0] // 2
    encode(p_ref[:half], first_ref)
    encode(p_ref[half:], second_ref)


def halves_code(p):
    code = jax.ShapeDtypeStruct((p.shape[0] // 2 + GROUPS, p.shape[1]), jnp.int16)
    return pl.pallas_call(
        halves_code_kernel,
        in_specs=[VMEM],
        out_specs=[VMEM, VMEM],
        out_shape=[code, code],
        compiler_params=pltpu.CompilerParams(vmem_limit_bytes=16 * MIB),
        name="halves_code",
    )(p)


def full_kernel(m, held_ref, in_ref, *refs):
    *blocks, out_ref, whole_ref = refs
    fill_cotangent(blocks, m, whole_ref)
    rows = out_ref.shape[0]
    tile = tile_of(rows)
    for i in range(rows // tile):
        part = pl.ds(i * tile, tile)
        out_ref[part] = held_ref[m, part] + mm(in_ref[part], whole_ref[...])


def full(m, held, inputs_t, blocks):
    _, rows, columns = held.shape
    return pl.pallas_call(
        functools.partial(full_kernel, m),
        in_specs=[VMEM] * (2 + len(blocks)),
        out_specs=VMEM,
        out_shape=in_vmem((rows, columns), F32),
        scratch_shapes=[pltpu.VMEM((inputs_t.shape[1], columns), BF16)],
        compiler_params=pltpu.CompilerParams(vmem_limit_bytes=16 * MIB),
        name=f"full_{m}",
    )(stay(held), inputs_t, *blocks)


def half_of(halved):
    return lax.axis_index("dp") & 1 if halved else 0


def half_products(full_ref, code_ref, which):
    half, width = code_ref.shape[0] - GROUPS, code_ref.shape[1]
    tile = tile_of(half)
    p = decode(code_ref)
    total = None
    for i in range(half // tile):
        p_high, p_low = halves(p[i * tile : (i + 1) * tile].T)
        start = pl.multiple_of(which * half + i * tile, tile)
        g_high, g_low = halves(full_ref[pl.ds(start, tile)])
        both = mm(jnp.concatenate([p_high, p_low], axis=0), g_high)
        term = both[:width] + both[width:] + mm(p_high, g_low)
        total = term if total is None else total + term
    return total, gram_of(p)


def own_half_kernel(halved, full_ref, code_ref, total_ref, gram_ref):
    total_ref[...], gram_ref[...] = half_products(full_ref, code_ref, half_of(halved))


def own_half(m, halved, full_grad, code):
    width = code.shape[1]
    return pl.pallas_call(
        functools.partial(own_half_kernel, halved),
        in_specs=[VMEM, VMEM],
        out_specs=[VMEM, VMEM],
        out_shape=[
            jax.ShapeDtypeStruct((width, full_grad.shape[1]), F32),
            jax.ShapeDtypeStruct((width, width), F32),
        ],
        compiler_params=pltpu.CompilerParams(vmem_limit_bytes=16 * MIB),
        name=f"own_half_{m}",
    )(stay(full_grad), code)


def other_half_kernel(halved, full_ref, code_ref, total_ref, part_ref, mine_ref, other_ref, gram_ref, both_ref):
    total, gram = half_products(full_ref, code_ref, 1 - half_of(halved))
    gram_ref[...] = part_ref[...] + gram
    total = total_ref[...] + total
    lanes = both_ref.shape[2]
    stacked = [total[:, t : t + lanes] for t in range(0, total.shape[1], lanes)]
    both_ref[...] = jnp.concatenate(stacked, axis=0).reshape(both_ref.shape)
    side = lax.axis_index("fsdp") & 1
    mine_ref[...] = both_ref[side]
    other_ref[...] = both_ref[1 - side]


def other_half(m, halved, full_grad, code, total, part):
    half = total.size // LANES // 2
    return pl.pallas_call(
        functools.partial(other_half_kernel, halved),
        in_specs=[VMEM] * 4,
        out_specs=[VMEM] * 3,
        out_shape=[jax.ShapeDtypeStruct((half, LANES), F32)] * 2 + [jax.ShapeDtypeStruct(part.shape, F32)],
        scratch_shapes=[pltpu.VMEM((2, half, LANES), F32)],
        compiler_params=pltpu.CompilerParams(vmem_limit_bytes=16 * MIB),
        name=f"other_half_{m}",
    )(stay(full_grad), code, total, part)


def tree(values):
    while len(values) > 1:
        values = [sum(values[i : i + 2][1:], values[i]) for i in range(0, len(values), 2)]
    return values[0]


def merge_kernel(count, plain, coded, parts, bit, *refs):
    terms, refs = refs[: plain * count], refs[plain * count :]
    codes, refs = refs[:coded], refs[coded:]
    decoded = [decode(code) for code in codes]
    rows = (decoded[0] if decoded else terms[0]).shape[0] // (count if decoded else 1)
    sums = []
    for m in range(count):
        values = [terms[t * count + m][...] for t in range(plain)]
        values += [value[m * rows : (m + 1) * rows] for value in decoded]
        sums.append(tree(values))
    if parts == 1:
        encode(jnp.concatenate(sums, axis=0), refs[0])
        return
    *outs, cut_ref = refs
    own = (lax.axis_index("fsdp") >> (bit.bit_length() - 1)) & (parts - 1)
    for m in range(count):
        cut_ref[m] = sums[m].reshape(cut_ref.shape[1:])
        outs[m][...] = cut_ref[m, own]
    for r in range(1, parts):
        encode(jnp.concatenate([cut_ref[m, own ^ r] for m in range(count)], axis=0), outs[count + r - 1])


def merge(terms, codes, name, parts=1, bit=1):
    count = len(terms[0]) if terms else 1
    if terms:
        rows = terms[0][0].shape[0]
        lanes = terms[0][0].shape[1]
    else:
        rows = codes[0].shape[0] - GROUPS
        lanes = codes[0].shape[1]
    share = rows // parts
    code = jax.ShapeDtypeStruct((count * share + GROUPS, lanes), jnp.int16)
    plain = [jax.ShapeDtypeStruct((share, lanes), F32)] * count if parts > 1 else []
    outs = plain + [code] * max(parts - 1, 1)
    flat = [x for term in terms for x in term]
    results = pl.pallas_call(
        functools.partial(merge_kernel, count, len(terms), len(codes), parts, bit),
        in_specs=[VMEM] * (len(flat) + len(codes)),
        out_specs=[VMEM] * len(outs),
        out_shape=outs,
        scratch_shapes=[pltpu.VMEM((count, parts, share, lanes), F32)] if parts > 1 else [],
        compiler_params=pltpu.CompilerParams(vmem_limit_bytes=16 * MIB),
        name=name,
    )(*flat, *codes)
    return (results[:count], results[count:]) if parts > 1 else results[0]


def gram_of(p):
    width = p.shape[1]
    high, low = halves(p)
    high_t, low_t = halves(p.T)
    both = mm(high_t, jnp.concatenate([high, low], axis=1))
    return both[:, :width] + both[:, width:] + mm(low_t, high)


def cholesky_inverse(work, n):
    lane = lax.broadcasted_iota(jnp.int32, (8, n), 1)
    sub = lax.broadcasted_iota(jnp.int32, (8, n), 0)

    def wide(x):
        return jnp.broadcast_to(x, (8, n))

    for b in range(n // 8):
        at = 8 * b
        panels = []
        for blocks in work:
            head = blocks[b]
            columns = [wide(head[:, at + j : at + j + 1]) for j in range(8)]
            scales, lows, tops = [], [], []
            for s in range(8):
                scale = lax.rsqrt(wide(columns[s][s : s + 1, :]))
                low = columns[s] * scale
                for j in range(s + 1, 8):
                    columns[j] = columns[j] - low * wide(low[j : j + 1, :])
                row = jnp.where(lane == at + s, scale, wide(head[s : s + 1, :]) * scale)
                below = jnp.where(lane == at + s, 0.0, head) - low * row
                head = jnp.where(sub > s, below, jnp.where(sub == s, row, head))
                scales.append(scale)
                lows.append(low)
                tops.append(jnp.where((lane > at + s) & (lane < at + 8), 0.0, row))
            blocks[b] = head
            panels.append((scales, lows, tops))
        for c in range(b + 1, n // 8):
            for blocks, (scales, lows, tops) in zip(work, panels):
                x = blocks[c]
                columns = [wide(x[:, at + j : at + j + 1]) for j in range(8)]
                y = jnp.where((lane >= at) & (lane < at + 8), 0.0, x)
                for s in range(8):
                    low = columns[s] * scales[s]
                    for j in range(s + 1, 8):
                        columns[j] = columns[j] - low * wide(lows[s][j : j + 1, :])
                    y = y - low * tops[s]
                blocks[c] = y


def factor_kernel(ranks_ref, gram_ref, inv_ref):
    count, n, _ = inv_ref.shape
    lane = lax.broadcasted_iota(jnp.int32, (8, n), 1)
    sub = lax.broadcasted_iota(jnp.int32, (8, n), 0)
    work = []
    for m in range(count):
        free = jnp.where(lane < ranks_ref[m], 0.0, 1.0)
        blocks = []
        for b in range(n // 8):
            g = gram_ref[m, 8 * b : 8 * b + 8, :]
            blocks.append(jnp.where(lane == sub + 8 * b, g + free, g))
        work.append(blocks)
    cholesky_inverse(work, n)
    for m in range(count):
        for b in range(n // 8):
            inv_ref[m, 8 * b : 8 * b + 8, :] = jnp.where(lane <= sub + 8 * b, work[m][b], 0.0)


def factor(grams, ranks):
    return pl.pallas_call(
        factor_kernel,
        in_specs=[SMEM, VMEM],
        out_specs=VMEM,
        out_shape=jax.ShapeDtypeStruct(grams.shape, F32),
        compiler_params=pltpu.CompilerParams(vmem_limit_bytes=16 * MIB),
        name="factor",
    )(ranks, grams)


def factor_p_kernel(halved, inv_ref, *refs):
    *codes, out_ref, p3_ref, buf_ref, sems = refs
    n = inv_ref.shape[1]
    which = half_of(halved)
    copies = []
    for m in range(inv_ref.shape[0]):
        i_high, i_low = halves(inv_ref[m])
        i_both = jnp.concatenate([i_high, i_low], axis=0)
        for code, place in ((codes[2 * m], which), (codes[2 * m + 1], 1 - which)):
            p_high, p_low = halves(decode(code))
            rows = p_high.shape[0]
            part = pl.ds(pl.multiple_of(place * rows, rows), rows)
            both = mm_nt(p_high, i_both)
            result = both[:, :n] + both[:, n:] + mm_nt(p_low, i_high)
            buf_ref[m, part] = result
            high, low = halves(result)
            p3_ref[m, part] = jnp.concatenate([high, low, high], axis=1)
        copies.append(pltpu.make_async_copy(buf_ref.at[m], out_ref.at[m], sems.at[m]))
        copies[-1].start()
    for copy in copies:
        copy.wait()


def factor_p_of(halved, inverse, codes):
    count, rows, width = len(codes), 2 * (codes[0][0].shape[0] - GROUPS), codes[0][0].shape[1]
    return pl.pallas_call(
        functools.partial(factor_p_kernel, halved),
        in_specs=[VMEM] * (1 + 2 * count),
        out_specs=[pl.BlockSpec(memory_space=pltpu.HBM), VMEM],
        out_shape=[
            jax.ShapeDtypeStruct((count, rows, width), F32),
            in_vmem((count, rows, 3 * width), BF16),
        ],
        scratch_shapes=[pltpu.VMEM((count, rows, width), F32), pltpu.SemaphoreType.DMA((count,))],
        compiler_params=pltpu.CompilerParams(vmem_limit_bytes=16 * MIB),
        name="factor_p",
    )(inverse, *[code for pair in codes for code in pair])


def error_kernel(count, pieces, groups, p3_ref, inv_ref, *refs):
    codes, refs = refs[:pieces], refs[pieces:]
    full_refs, (err_ref, fq_ref, right_ref, q_ref, buf_ref, sems) = refs[:count], refs[count:]
    rows, width = p3_ref.shape[1], inv_ref.shape[1]
    tile = min(rows, LANES)
    share = right_ref.shape[1] // pieces
    me = lax.axis_index("fsdp") if pieces > 1 else 0
    copies = []
    for m in range(count):
        for r, code in enumerate(codes):
            place = (me ^ r) & 1 if pieces > 1 else 0
            for bit, members in groups:
                place = place * members + (((me ^ r) >> (bit.bit_length() - 1)) & (members - 1))
            at = pl.ds(pl.multiple_of(place * share, share), share)
            right_ref[m, at] = decode_part(code, m, count)
        i_high, i_low = halves(inv_ref[m])
        tiles = [right_ref[m, t : t + width] for t in range(0, right_ref.shape[1], width)]
        r_high, r_low = halves(jnp.concatenate(tiles, axis=1))
        both = mm(jnp.concatenate([i_high, i_low], axis=0), r_high)
        fq_t = both[:width] + both[width:] + mm(i_high, r_low)
        q_high, q_low = halves(fq_t)
        q3 = jnp.concatenate([q_high, q_high, q_low], axis=0)
        for start in range(0, rows, tile):
            part = pl.ds(start, tile)
            buf_ref[m, part] = full_refs[m][part] - mm(p3_ref[m, part], q3)
            copies.append(
                pltpu.make_async_copy(buf_ref.at[m, part], err_ref.at[m, 0, part], sems.at[len(copies)])
            )
            copies[-1].start()
        q_ref[m] = fq_t.T
        copies.append(pltpu.make_async_copy(q_ref.at[m], fq_ref.at[m], sems.at[len(copies)]))
        copies[-1].start()
    for copy in copies:
        copy.wait()


def error(full_grad, p3, inverse, codes):
    count, rows, _ = p3.shape
    width = inverse.shape[1]
    columns = full_grad[0].shape[1]
    out = pl.BlockSpec(memory_space=pltpu.HBM)
    groups = groups_of("fsdp") if len(codes) > 1 else []
    return pl.pallas_call(
        functools.partial(error_kernel, count, len(codes), groups),
        in_specs=[VMEM] * (2 + len(codes) + count),
        out_specs=[out, out],
        out_shape=[
            jax.ShapeDtypeStruct((count, 1, rows, columns), F32),
            jax.ShapeDtypeStruct((count, columns, width), F32),
        ],
        scratch_shapes=[
            pltpu.VMEM((count, columns * width // LANES, LANES), F32),
            pltpu.VMEM((count, columns, width), F32),
            pltpu.VMEM((count, rows, columns), F32),
            pltpu.SemaphoreType.DMA((count * (rows // min(rows, LANES) + 1),)),
        ],
        compiler_params=pltpu.CompilerParams(vmem_limit_bytes=24 * MIB),
        name="error",
    )(stay(p3), inverse, *codes, *[stay(x) for x in full_grad])


def power_of_two(n):
    return n & (n - 1) == 0


def across(x, axis, bit):
    size = lax.axis_size(axis)
    return lax.ppermute(x, axis, [(i, i ^ bit) for i in range(size)])


def bits_of(axis):
    size = lax.axis_size(axis)
    return [1 << b for b in range(size.bit_length() - 1)]


def groups_of(axis):
    bits = bits_of(axis)[1:]
    return [(bits[i], 1 << len(bits[i : i + 2])) for i in range(0, len(bits), 2)]


def gather_slow(x, axis):
    held = {0: x}
    for bit, members in groups_of(axis)[::-1]:
        for r in list(held):
            for k in range(1, members):
                held[r ^ (k * bit)] = across(held[r], axis, k * bit)
    return held


def gather_blocks(x, axis, beside=()):
    held = gather_slow(x, axis)
    order = list(held)
    held[order[-1]], *beside = tie(held[order[-1]], *beside)
    held.update({r ^ 1: across(held[r], axis, 1) for r in order})
    return [held[r] for r in range(len(held))], beside


def gather_cotangent(cotangent, beside):
    size = lax.axis_size("fsdp")
    width = cotangent.shape[2]
    if not (power_of_two(size) and size > 1 and width % 128 == 0):
        return [lax.all_gather(cotangent, "fsdp", axis=2, tiled=True)], [None], [], beside
    held = gather_slow(cotangent, "fsdp")
    *order, last = list(held)
    values = tie(*[held[r] for r in order], *beside)
    held.update(zip(order, values))
    beside = values[len(order) :]
    swapped = [across(held[r], "fsdp", 1) for r in order]
    held[last], *swapped = tie(held[last], *swapped)
    held.update({r ^ 1: x for r, x in zip(order, swapped)})
    begun = begin(held, order, beside[2])
    held[last ^ 1] = across(held[last], "fsdp", 1)
    return [held[r] for r in range(len(held))], [last], [begun], beside


def tie(*values):
    return lax.optimization_barrier(values)


def sums(halved, grams, pairs, p_codes, ranks):
    size = lax.axis_size("fsdp")
    replicas = lax.axis_size("dp")
    if not (power_of_two(size) and size > 1):
        inverse = factor(lax.psum(grams, "fsdp"), ranks)
        ordered = [jnp.stack(pair) for pair in pairs]
        odd = (lax.axis_index("fsdp") & 1) == 1
        whole = jnp.stack([jnp.where(odd, x[::-1], x).reshape(-1, x.shape[2]) for x in ordered])
        codes = [merge([list(lax.psum(whole, ("fsdp", "dp")))], [], "code")]
        return inverse, factor_p_of(halved, inverse, p_codes), codes
    groups = groups_of("fsdp")

    for bit in bits_of("fsdp"):
        grams = grams + across(grams, "fsdp", bit)

    terms = [[mine for mine, _ in pairs], [across(other, "fsdp", 1) for _, other in pairs]]
    codes = []
    for bit, members in groups:
        keep, others = merge(terms, codes, f"part_{bit}", members, bit)
        codes = [across(others[k - 1], "fsdp", k * bit) for k in range(1, members)]
        terms = [keep]
    code = merge(terms, codes, "code")
    if power_of_two(replicas) and replicas > 1:
        theirs = [across(code, "dp", k) for k in range(1, replicas)]
        inverse = factor(grams, ranks)
        *theirs, inverse = tie(*theirs, inverse)
        code = merge([], [code] + theirs, "code_sum")
    else:
        inverse = factor(grams, ranks)
        code = merge([[lax.psum(plain(code), "dp")]], [], "code_sum")
    code, inverse = tie(code, inverse)
    codes, made = gather_blocks(code, "fsdp", factor_p_of(halved, inverse, p_codes))
    return inverse, made, codes


def plain_kernel(code_ref, out_ref):
    out_ref[...] = decode(code_ref)


def plain(code):
    return pl.pallas_call(
        plain_kernel,
        in_specs=[VMEM],
        out_specs=VMEM,
        out_shape=jax.ShapeDtypeStruct((code.shape[0] - GROUPS, code.shape[1]), F32),
        name="plain",
    )(code)


def left_sums(halved, blocks, keys, begun, q2, inputs_t, held, fbq):
    count = fbq.shape[0]
    codes, full_grad, pairs, grams = [], [], [], []
    if not halved:
        pairs_of = [None] if keys == [None] else list(range(0, len(blocks), 2))
        p = lax.psum(jnp.stack([left(m, pairs_of, blocks, q2, inputs_t, fbq) for m in range(count)]), "dp")
        for m in range(count):
            full_grad.append(full(m, held, inputs_t, blocks))
            codes.append(halves_code(p[m]))
            total, part = own_half(m, halved, full_grad[m], codes[m][0])
            *pair, part = other_half(m, halved, full_grad[m], codes[m][1], total, part)
            pairs.append(pair)
            grams.append(part)
        return codes, full_grad, pairs, jnp.stack(grams)
    steps = bits_of("dp")[1:]
    mines = []
    late = blocks if keys == [None] else [blocks[r ^ k] for r in keys for k in range(2)]
    for m in range(count):
        mine, other = left_code(m, keys, begun, late, q2, inputs_t, fbq)
        mines.append(add_code(mine, across(other, "dp", 1)))
    own, late = {}, None
    for m in range(count)[::-1]:
        mine, in_t = tie(mines[m], inputs_t)
        grad = full(m, held, in_t, blocks)
        for bit in steps:
            if late is None:
                theirs, grad = tie(across(mine, "dp", bit), grad)
            else:
                theirs, grad, *own[late] = tie(across(mine, "dp", bit), grad, *own[late])
            mine = add_code(mine, theirs)
        mines[m] = mine
        full_grad.insert(0, grad)
        own[m] = list(own_half(m, halved, grad, mine))
        late = m
    for m in range(count):
        codes.append((mines[m], across(mines[m], "dp", 1)))
        *pair, part = other_half(m, halved, full_grad[m], codes[m][1], *own[m])
        pairs.append(pair)
        grams.append(part)
    return codes, full_grad, pairs, jnp.stack(grams)


def local(inputs, cotangent, feedback, q_init, factor_ranks):
    replicas = lax.axis_size("dp")
    halved = power_of_two(replicas) and replicas > 1
    beside = feedback_q(feedback, q_init, inputs, factor_ranks)
    blocks, keys, begun, (held, fbq, q2, inputs_t) = gather_cotangent(cotangent, beside)
    p_codes, full_grad, pairs, grams = left_sums(halved, blocks, keys, begun, q2, inputs_t, held, fbq)
    inverse, (factor_p, p3), codes = sums(halved, grams, pairs, p_codes, factor_ranks)
    new_error, factor_q = error(full_grad, p3, inverse, codes)
    return (factor_p, factor_q, new_error)


def solution(mesh):
    placed = (P("dp", "fsdp"), P(None, "dp", "fsdp"), P(None, "dp", "fsdp", None), P(), P())
    return jax.shard_map(
        local,
        mesh=mesh,
        in_specs=placed,
        out_specs=(P(None, "fsdp", None), P(), P(None, "dp", "fsdp", None)),
        check_vma=False,
    )
```

```python
import functools

import jax
import jax.numpy as jnp
from jax import lax
from jax.experimental import pallas as pl
from jax.experimental.pallas import tpu as pltpu
from jax.sharding import PartitionSpec as P

F32 = jnp.float32
BF16 = jnp.bfloat16
VMEM = pl.BlockSpec(memory_space=pltpu.VMEM)
SMEM = pl.BlockSpec(memory_space=pltpu.SMEM)
MIB = 1024 * 1024


def halves(x):
    high = x.astype(BF16)
    return high, (x - high.astype(F32)).astype(BF16)


def mm(a, b):
    return jnp.dot(a, b, preferred_element_type=F32)


def mm_nt(a, b):
    return lax.dot_general(a, b, (((1,), (1,)), ((), ())), preferred_element_type=F32)


def params(size, steps=1):
    return pltpu.CompilerParams(
        vmem_limit_bytes=size * MIB, dimension_semantics=("arbitrary",) * steps
    )


def tile_of(rows):
    return min(rows, 256)


def in_vmem(shape, dtype):
    return pltpu.VMEM(shape, dtype)


def stay(x):
    return pltpu.with_memory_space_constraint(x, pltpu.VMEM)


def masked_halves(q, rank):
    column = lax.broadcasted_iota(jnp.int32, q.shape, 1)
    return halves(jnp.where(column < rank, q, 0.0))


def feedback_q_kernel(
    ranks_ref, fb_ref, q_ref, in_ref, held_ref, out_ref, q2_ref, in_t_ref, ranks_own, q_own, in_own, sems, sem_q
):
    count, rows, _ = held_ref.shape
    width = q_ref.shape[2]
    tile = tile_of(rows)
    small = [
        pltpu.make_async_copy(ranks_ref, ranks_own, sem_q.at[0]),
        pltpu.make_async_copy(q_ref, q_own, sem_q.at[1]),
        pltpu.make_async_copy(in_ref, in_own, sem_q.at[2]),
    ]
    copies = []
    small[2].start()
    small[0].start()
    small[1].start()
    for m in range(count):
        for i in range(rows // tile):
            part = pl.ds(i * tile, tile)
            copies.append(
                pltpu.make_async_copy(fb_ref.at[m, 0, part], held_ref.at[m, part], sems.at[len(copies)])
            )
            copies[-1].start()
    small[2].wait()
    in_t_ref[...] = in_own[...].T
    small[0].wait()
    small[1].wait()
    for m in range(count):
        q_high, q_low = masked_halves(q_own[m], ranks_own[m])
        q2_ref[m, :, :width] = q_high
        q2_ref[m, :, width:] = q_low
    for m in range(count):
        for i in range(rows // tile):
            part = pl.ds(i * tile, tile)
            copies[m * (rows // tile) + i].wait()
            high, low = halves(held_ref[m, part])
            both = mm(high, q2_ref[m])
            out_ref[m, part] = both[:, :width] + both[:, width:] + mm(low, q2_ref[m, :, :width])


def feedback_q(feedback, q_init, inputs, ranks):
    count, _, rows, columns = feedback.shape
    width = q_init.shape[2]
    far = pl.BlockSpec(memory_space=pltpu.HBM)
    return pl.pallas_call(
        feedback_q_kernel,
        in_specs=[far] * 4,
        out_specs=[VMEM] * 4,
        out_shape=[
            in_vmem((count, rows, columns), F32),
            in_vmem((count, rows, width), F32),
            in_vmem((count, columns, 2 * width), BF16),
            in_vmem(inputs.shape[::-1], inputs.dtype),
        ],
        scratch_shapes=[
            pltpu.SMEM(ranks.shape, ranks.dtype),
            pltpu.VMEM(q_init.shape, q_init.dtype),
            pltpu.VMEM(inputs.shape, inputs.dtype),
            pltpu.SemaphoreType.DMA((count * (rows // tile_of(rows)),)),
            pltpu.SemaphoreType.DMA((3,)),
        ],
        compiler_params=pltpu.CompilerParams(vmem_limit_bytes=16 * MIB),
        name="feedback_q",
    )(*[pltpu.with_memory_space_constraint(x, pltpu.HBM) for x in (ranks, feedback, q_init, inputs)])


def fill_cotangent(blocks, at, whole_ref):
    if len(blocks) == 1:
        whole_ref[...] = blocks[0][at]
        return
    me = lax.axis_index("fsdp")
    for r, block in enumerate(blocks):
        width = block.shape[2]
        start = pl.multiple_of((me ^ r) * width, width)
        whole_ref[:, pl.ds(start, width)] = block[at]


def cotangent_q(q2_ref, m, pairs, at):
    terms = []
    for r, blocks in pairs:
        if r is None:
            terms.append(mm(blocks[0][at], q2_ref[m]))
            continue
        me = lax.axis_index("fsdp") ^ r
        width = blocks[0].shape[2]
        rows = [q2_ref[m, pl.ds(pl.multiple_of((me ^ k) * width, width), width)] for k in range(2)]
        pair = jnp.concatenate([block[at] for block in blocks], axis=1)
        terms.append(mm(pair, jnp.concatenate(rows, axis=0)))
    return sum(terms[1:], terms[0])


def paired(keys, refs):
    if keys == [None]:
        return [(None, refs)]
    return [(r, refs[2 * i : 2 * i + 2]) for i, r in enumerate(keys)]


def begin_kernel(keys, q2_ref, *refs):
    *blocks, out_ref = refs
    for m in range(out_ref.shape[0]):
        out_ref[m] = cotangent_q(q2_ref, m, paired(keys, blocks), m)


def begin(held, keys, q2):
    blocks = [held[r ^ k] for r in keys for k in range(2)]
    count, tokens, _ = blocks[0].shape
    return pl.pallas_call(
        functools.partial(begin_kernel, keys),
        in_specs=[VMEM] * (1 + len(blocks)),
        out_specs=VMEM,
        out_shape=jax.ShapeDtypeStruct((count, tokens, q2.shape[2]), F32),
        compiler_params=pltpu.CompilerParams(vmem_limit_bytes=16 * MIB),
        name="begin",
    )(q2, *blocks)


def gradient_q(both, inputs_t):
    width = both.shape[1] // 2
    c_high, c_low = halves(both[:, :width] + both[:, width:])
    both = mm(inputs_t, jnp.concatenate([c_high, c_low], axis=1))
    return both[:, :width] + both[:, width:]


def left_kernel(m, keys, q2_ref, in_ref, fbq_ref, *refs):
    *blocks, out_ref = refs
    out_ref[...] = fbq_ref[m] + gradient_q(cotangent_q(q2_ref, m, paired(keys, blocks), m), in_ref[...])


def left(m, keys, blocks, q2, inputs_t, fbq):
    _, rows, width = fbq.shape
    return pl.pallas_call(
        functools.partial(left_kernel, m, keys),
        in_specs=[VMEM] * (3 + len(blocks)),
        out_specs=VMEM,
        out_shape=jax.ShapeDtypeStruct((rows, width), F32),
        compiler_params=pltpu.CompilerParams(vmem_limit_bytes=16 * MIB),
        name=f"left_{m}",
    )(q2, inputs_t, fbq, *blocks)


GROUPS = 16
LANES = 128
NEAR = 3


def encode(x, out_ref):
    rows, width = x.shape
    grouped = x.reshape(GROUPS, rows // GROUPS, width)
    top = jnp.max(jnp.abs(grouped), axis=1)
    level = jnp.ceil(jnp.log(jnp.maximum(top, 1e-30)) * 32.0) + 1.0
    up = jnp.exp(level * (-1.0 / 32.0)) * 32767.0
    code = jnp.round(grouped * up[:, None, :]).reshape(rows, width)
    out_ref[:rows] = code.astype(jnp.int32).astype(jnp.int16)
    out_ref[rows:] = level.astype(jnp.int32).astype(jnp.int16)


def decode(ref):
    rows = ref.shape[0] - GROUPS
    width = ref.shape[1]
    level = ref[rows:].astype(jnp.int32).astype(F32)
    down = jnp.exp(level * (1.0 / 32.0)) * (1.0 / 32767.0)
    code = ref[:rows].astype(jnp.int32).astype(F32).reshape(GROUPS, rows // GROUPS, width)
    return (code * down[:, None, :]).reshape(rows, width)


def decode_part(ref, part, count):
    rows, width = ref.shape[0] - GROUPS, ref.shape[1]
    own, groups = rows // count, GROUPS // count
    level = ref[rows:].astype(jnp.int32).astype(F32)[part * groups : (part + 1) * groups]
    down = jnp.exp(level * (1.0 / 32.0)) * (1.0 / 32767.0)
    code = ref[part * own : (part + 1) * own].astype(jnp.int32).astype(F32)
    return (code.reshape(groups, own // groups, width) * down[:, None, :]).reshape(own, width)


def left_code_kernel(m, keys, q2_ref, in_ref, fbq_ref, *refs):
    *refs, mine_ref, code_ref, p_ref = refs
    if keys == [None]:
        both = cotangent_q(q2_ref, m, paired(keys, refs), m)
    else:
        both = refs[0][m] + cotangent_q(q2_ref, m, paired(keys, refs[1:]), m)
    p = fbq_ref[m] + gradient_q(both, in_ref[...])
    p_ref[...] = p.reshape(p_ref.shape)
    low = lax.axis_index("dp") & 1
    mine_ref[...] = p_ref[low]
    encode(p_ref[1 - low], code_ref)


def left_code(m, keys, begun, blocks, q2, inputs_t, fbq):
    _, rows, width = fbq.shape
    half = rows // 2
    return pl.pallas_call(
        functools.partial(left_code_kernel, m, keys),
        in_specs=[VMEM] * (3 + len(begun) + len(blocks)),
        out_specs=[VMEM] * 2,
        out_shape=[
            jax.ShapeDtypeStruct((half, width), F32),
            jax.ShapeDtypeStruct((half + GROUPS, width), jnp.int16),
        ],
        scratch_shapes=[pltpu.VMEM((2, half, width), F32)],
        compiler_params=pltpu.CompilerParams(vmem_limit_bytes=16 * MIB),
        name=f"left_code_{m}",
    )(q2, inputs_t, fbq, *begun, *blocks)


def add_kernel(mine_ref, theirs_ref, out_ref):
    mine = mine_ref[...] if mine_ref.dtype == F32 else decode(mine_ref)
    encode(mine + decode(theirs_ref), out_ref)


def add_code(mine, theirs):
    return pl.pallas_call(
        add_kernel,
        in_specs=[VMEM, VMEM],
        out_specs=VMEM,
        out_shape=jax.ShapeDtypeStruct(theirs.shape, jnp.int16),
        compiler_params=pltpu.CompilerParams(vmem_limit_bytes=16 * MIB),
        name="add_code",
    )(mine, theirs)


def halves_code_kernel(p_ref, first_ref, second_ref):
    half = p_ref.shape[0] // 2
    encode(p_ref[:half], first_ref)
    encode(p_ref[half:], second_ref)


def halves_code(p):
    code = jax.ShapeDtypeStruct((p.shape[0] // 2 + GROUPS, p.shape[1]), jnp.int16)
    return pl.pallas_call(
        halves_code_kernel,
        in_specs=[VMEM],
        out_specs=[VMEM, VMEM],
        out_shape=[code, code],
        compiler_params=pltpu.CompilerParams(vmem_limit_bytes=16 * MIB),
        name="halves_code",
    )(p)


def full_kernel(m, held_ref, in_ref, *refs):
    *blocks, out_ref, whole_ref = refs
    fill_cotangent(blocks, m, whole_ref)
    rows = out_ref.shape[0]
    tile = tile_of(rows)
    for i in range(rows // tile):
        part = pl.ds(i * tile, tile)
        out_ref[part] = held_ref[m, part] + mm(in_ref[part], whole_ref[...])


def full(m, held, inputs_t, blocks):
    _, rows, columns = held.shape
    return pl.pallas_call(
        functools.partial(full_kernel, m),
        in_specs=[VMEM] * (2 + len(blocks)),
        out_specs=VMEM,
        out_shape=in_vmem((rows, columns), F32),
        scratch_shapes=[pltpu.VMEM((inputs_t.shape[1], columns), BF16)],
        compiler_params=pltpu.CompilerParams(vmem_limit_bytes=16 * MIB),
        name=f"full_{m}",
    )(stay(held), inputs_t, *blocks)


def half_of(halved):
    return lax.axis_index("dp") & 1 if halved else 0


def half_products(full_ref, code_ref, which):
    half, width = code_ref.shape[0] - GROUPS, code_ref.shape[1]
    tile = tile_of(half)
    p = decode(code_ref)
    total = None
    for i in range(half // tile):
        p_high, p_low = halves(p[i * tile : (i + 1) * tile].T)
        start = pl.multiple_of(which * half + i * tile, tile)
        g_high, g_low = halves(full_ref[pl.ds(start, tile)])
        both = mm(jnp.concatenate([p_high, p_low], axis=0), g_high)
        term = both[:width] + both[width:] + mm(p_high, g_low)
        total = term if total is None else total + term
    return total, gram_of(p)


def own_half_kernel(halved, full_ref, code_ref, total_ref, gram_ref):
    total_ref[...], gram_ref[...] = half_products(full_ref, code_ref, half_of(halved))


def own_half(m, halved, full_grad, code):
    width = code.shape[1]
    return pl.pallas_call(
        functools.partial(own_half_kernel, halved),
        in_specs=[VMEM, VMEM],
        out_specs=[VMEM, VMEM],
        out_shape=[
            jax.ShapeDtypeStruct((width, full_grad.shape[1]), F32),
            jax.ShapeDtypeStruct((width, width), F32),
        ],
        compiler_params=pltpu.CompilerParams(vmem_limit_bytes=16 * MIB),
        name=f"own_half_{m}",
    )(stay(full_grad), code)


def other_half_kernel(halved, full_ref, code_ref, total_ref, part_ref, mine_ref, other_ref, gram_ref, both_ref):
    total, gram = half_products(full_ref, code_ref, 1 - half_of(halved))
    gram_ref[...] = part_ref[...] + gram
    total = total_ref[...] + total
    lanes = both_ref.shape[2]
    stacked = [total[:, t : t + lanes] for t in range(0, total.shape[1], lanes)]
    both_ref[...] = jnp.concatenate(stacked, axis=0).reshape(both_ref.shape)
    side = lax.axis_index("fsdp") & 1
    mine_ref[...] = both_ref[side]
    other_ref[...] = both_ref[1 - side]


def other_half(m, halved, full_grad, code, total, part):
    half = total.size // LANES // 2
    return pl.pallas_call(
        functools.partial(other_half_kernel, halved),
        in_specs=[VMEM] * 4,
        out_specs=[VMEM] * 3,
        out_shape=[jax.ShapeDtypeStruct((half, LANES), F32)] * 2 + [jax.ShapeDtypeStruct(part.shape, F32)],
        scratch_shapes=[pltpu.VMEM((2, half, LANES), F32)],
        compiler_params=pltpu.CompilerParams(vmem_limit_bytes=16 * MIB),
        name=f"other_half_{m}",
    )(stay(full_grad), code, total, part)


def tree(values):
    while len(values) > 1:
        values = [sum(values[i : i + 2][1:], values[i]) for i in range(0, len(values), 2)]
    return values[0]


def merge_kernel(count, plain, coded, parts, bit, *refs):
    terms, refs = refs[: plain * count], refs[plain * count :]
    codes, refs = refs[:coded], refs[coded:]
    decoded = [decode(code) for code in codes]
    rows = (decoded[0] if decoded else terms[0]).shape[0] // (count if decoded else 1)
    sums = []
    for m in range(count):
        values = [terms[t * count + m][...] for t in range(plain)]
        values += [value[m * rows : (m + 1) * rows] for value in decoded]
        sums.append(tree(values))
    if parts == 1:
        encode(jnp.concatenate(sums, axis=0), refs[0])
        return
    *outs, cut_ref = refs
    own = (lax.axis_index("fsdp") >> (bit.bit_length() - 1)) & (parts - 1)
    for m in range(count):
        cut_ref[m] = sums[m].reshape(cut_ref.shape[1:])
        outs[m][...] = cut_ref[m, own]
    for r in range(1, parts):
        encode(jnp.concatenate([cut_ref[m, own ^ r] for m in range(count)], axis=0), outs[count + r - 1])


def merge(terms, codes, name, parts=1, bit=1):
    count = len(terms[0]) if terms else 1
    if terms:
        rows = terms[0][0].shape[0]
        lanes = terms[0][0].shape[1]
    else:
        rows = codes[0].shape[0] - GROUPS
        lanes = codes[0].shape[1]
    share = rows // parts
    code = jax.ShapeDtypeStruct((count * share + GROUPS, lanes), jnp.int16)
    plain = [jax.ShapeDtypeStruct((share, lanes), F32)] * count if parts > 1 else []
    outs = plain + [code] * max(parts - 1, 1)
    flat = [x for term in terms for x in term]
    results = pl.pallas_call(
        functools.partial(merge_kernel, count, len(terms), len(codes), parts, bit),
        in_specs=[VMEM] * (len(flat) + len(codes)),
        out_specs=[VMEM] * len(outs),
        out_shape=outs,
        scratch_shapes=[pltpu.VMEM((count, parts, share, lanes), F32)] if parts > 1 else [],
        compiler_params=pltpu.CompilerParams(vmem_limit_bytes=16 * MIB),
        name=name,
    )(*flat, *codes)
    return (results[:count], results[count:]) if parts > 1 else results[0]


def gram_of(p):
    width = p.shape[1]
    high, low = halves(p)
    high_t, low_t = halves(p.T)
    both = mm(high_t, jnp.concatenate([high, low], axis=1))
    return both[:, :width] + both[:, width:] + mm(low_t, high)


def cholesky_inverse(work, n):
    lane = lax.broadcasted_iota(jnp.int32, (8, n), 1)
    sub = lax.broadcasted_iota(jnp.int32, (8, n), 0)
    last = n // 8

    def wide(x):
        return jnp.broadcast_to(x, (8, n))

    def columns_of(x, at):
        return [wide(x[:, at + j : at + j + 1]) for j in range(8)]

    carried = [columns_of(blocks[0], 0) for blocks in work]
    for b in range(last):
        at = 8 * b
        inside = (lane >= at) & (lane < at + 8)
        panels = []
        for columns, blocks in zip(carried, work):
            head = blocks[b]
            scales, lows, tops = [], [], []
            for s in range(8):
                scale = lax.rsqrt(wide(columns[s][s : s + 1, :]))
                low = columns[s] * scale
                for j in range(s + 1, 8):
                    columns[j] = columns[j] - low * wide(low[j : j + 1, :])
                row = jnp.where(lane == at + s, scale, wide(head[s : s + 1, :]) * scale)
                below = jnp.where(lane == at + s, 0.0, head) - low * row
                head = jnp.where(sub > s, below, jnp.where(sub == s, row, head))
                scales.append(scale)
                lows.append(low)
                tops.append(jnp.where((lane > at + s) & (lane < at + 8), 0.0, row))
            blocks[b] = head
            panels.append((scales, lows, tops))
        near = min(b + 1 + NEAR, last)
        for c in range(b + 1, near):
            for i, (blocks, (scales, lows, tops)) in enumerate(zip(work, panels)):
                x = blocks[c]
                columns = columns_of(x, at)
                following = columns_of(x, at + 8) if c == b + 1 else []
                y = jnp.where(inside, 0.0, x)
                for s in range(8):
                    low = columns[s] * scales[s]
                    for j in range(s + 1, 8):
                        columns[j] = columns[j] - low * wide(lows[s][j : j + 1, :])
                    y = y - low * tops[s]
                    following = [f - low * wide(low[j : j + 1, :]) for j, f in enumerate(following)]
                blocks[c] = y
                if following:
                    carried[i] = following
        if near < last:
            for blocks, (scales, lows, tops) in zip(work, panels):
                top = tops[0]
                for s in range(1, 8):
                    top = jnp.where(sub == s, tops[s], top)
                update = lax.dot_general(
                    blocks[b],
                    top,
                    (((0,), (0,)), ((), ())),
                    precision=lax.Precision.HIGHEST,
                    preferred_element_type=F32,
                )
                for c in range(near, last):
                    blocks[c] = jnp.where(inside, 0.0, blocks[c]) - update[8 * c : 8 * c + 8]


def factor_kernel(ranks_ref, gram_ref, inv_ref):
    count, n, _ = inv_ref.shape
    lane = lax.broadcasted_iota(jnp.int32, (8, n), 1)
    sub = lax.broadcasted_iota(jnp.int32, (8, n), 0)
    work = []
    for m in range(count):
        free = jnp.where(lane < ranks_ref[m], 0.0, 1.0)
        blocks = []
        for b in range(n // 8):
            g = gram_ref[m, 8 * b : 8 * b + 8, :]
            blocks.append(jnp.where(lane == sub + 8 * b, g + free, g))
        work.append(blocks)
    cholesky_inverse(work, n)
    for m in range(count):
        for b in range(n // 8):
            inv_ref[m, 8 * b : 8 * b + 8, :] = jnp.where(lane <= sub + 8 * b, work[m][b], 0.0)


def factor(grams, ranks):
    return pl.pallas_call(
        factor_kernel,
        in_specs=[SMEM, VMEM],
        out_specs=VMEM,
        out_shape=jax.ShapeDtypeStruct(grams.shape, F32),
        compiler_params=pltpu.CompilerParams(vmem_limit_bytes=16 * MIB),
        name="factor",
    )(ranks, grams)


def factor_p_kernel(halved, inv_ref, *refs):
    *codes, out_ref, p3_ref, buf_ref, sems = refs
    n = inv_ref.shape[1]
    which = half_of(halved)
    copies = []
    for m in range(inv_ref.shape[0]):
        i_high, i_low = halves(inv_ref[m])
        i_both = jnp.concatenate([i_high, i_low], axis=0)
        for code, place in ((codes[2 * m], which), (codes[2 * m + 1], 1 - which)):
            p_high, p_low = halves(decode(code))
            rows = p_high.shape[0]
            part = pl.ds(pl.multiple_of(place * rows, rows), rows)
            both = mm_nt(p_high, i_both)
            result = both[:, :n] + both[:, n:] + mm_nt(p_low, i_high)
            buf_ref[m, part] = result
            high, low = halves(result)
            p3_ref[m, part] = jnp.concatenate([high, low, high], axis=1)
        copies.append(pltpu.make_async_copy(buf_ref.at[m], out_ref.at[m], sems.at[m]))
        copies[-1].start()
    for copy in copies:
        copy.wait()


def factor_p_of(halved, inverse, codes):
    count, rows, width = len(codes), 2 * (codes[0][0].shape[0] - GROUPS), codes[0][0].shape[1]
    return pl.pallas_call(
        functools.partial(factor_p_kernel, halved),
        in_specs=[VMEM] * (1 + 2 * count),
        out_specs=[pl.BlockSpec(memory_space=pltpu.HBM), VMEM],
        out_shape=[
            jax.ShapeDtypeStruct((count, rows, width), F32),
            in_vmem((count, rows, 3 * width), BF16),
        ],
        scratch_shapes=[pltpu.VMEM((count, rows, width), F32), pltpu.SemaphoreType.DMA((count,))],
        compiler_params=pltpu.CompilerParams(vmem_limit_bytes=16 * MIB),
        name="factor_p",
    )(inverse, *[code for pair in codes for code in pair])


def error_kernel(count, pieces, groups, p3_ref, inv_ref, *refs):
    codes, refs = refs[:pieces], refs[pieces:]
    full_refs, (err_ref, fq_ref, right_ref, q_ref, buf_ref, sems) = refs[:count], refs[count:]
    rows, width = p3_ref.shape[1], inv_ref.shape[1]
    tile = min(rows, LANES)
    share = right_ref.shape[1] // pieces
    me = lax.axis_index("fsdp") if pieces > 1 else 0
    copies = []
    for m in range(count):
        for r, code in enumerate(codes):
            place = (me ^ r) & 1 if pieces > 1 else 0
            for bit, members in groups:
                place = place * members + (((me ^ r) >> (bit.bit_length() - 1)) & (members - 1))
            at = pl.ds(pl.multiple_of(place * share, share), share)
            right_ref[m, at] = decode_part(code, m, count)
        i_high, i_low = halves(inv_ref[m])
        tiles = [right_ref[m, t : t + width] for t in range(0, right_ref.shape[1], width)]
        r_high, r_low = halves(jnp.concatenate(tiles, axis=1))
        both = mm(jnp.concatenate([i_high, i_low], axis=0), r_high)
        fq_t = both[:width] + both[width:] + mm(i_high, r_low)
        q_high, q_low = halves(fq_t)
        q3 = jnp.concatenate([q_high, q_high, q_low], axis=0)
        for start in range(0, rows, tile):
            part = pl.ds(start, tile)
            buf_ref[m, part] = full_refs[m][part] - mm(p3_ref[m, part], q3)
            copies.append(
                pltpu.make_async_copy(buf_ref.at[m, part], err_ref.at[m, 0, part], sems.at[len(copies)])
            )
            copies[-1].start()
        q_ref[m] = fq_t.T
        copies.append(pltpu.make_async_copy(q_ref.at[m], fq_ref.at[m], sems.at[len(copies)]))
        copies[-1].start()
    for copy in copies:
        copy.wait()


def error(full_grad, p3, inverse, codes):
    count, rows, _ = p3.shape
    width = inverse.shape[1]
    columns = full_grad[0].shape[1]
    out = pl.BlockSpec(memory_space=pltpu.HBM)
    groups = groups_of("fsdp") if len(codes) > 1 else []
    return pl.pallas_call(
        functools.partial(error_kernel, count, len(codes), groups),
        in_specs=[VMEM] * (2 + len(codes) + count),
        out_specs=[out, out],
        out_shape=[
            jax.ShapeDtypeStruct((count, 1, rows, columns), F32),
            jax.ShapeDtypeStruct((count, columns, width), F32),
        ],
        scratch_shapes=[
            pltpu.VMEM((count, columns * width // LANES, LANES), F32),
            pltpu.VMEM((count, columns, width), F32),
            pltpu.VMEM((count, rows, columns), F32),
            pltpu.SemaphoreType.DMA((count * (rows // min(rows, LANES) + 1),)),
        ],
        compiler_params=pltpu.CompilerParams(vmem_limit_bytes=24 * MIB),
        name="error",
    )(stay(p3), inverse, *codes, *[stay(x) for x in full_grad])


def power_of_two(n):
    return n & (n - 1) == 0


def across(x, axis, bit):
    size = lax.axis_size(axis)
    return lax.ppermute(x, axis, [(i, i ^ bit) for i in range(size)])


def bits_of(axis):
    size = lax.axis_size(axis)
    return [1 << b for b in range(size.bit_length() - 1)]


def groups_of(axis):
    bits = bits_of(axis)[1:]
    return [(bits[i], 1 << len(bits[i : i + 2])) for i in range(0, len(bits), 2)]


def gather_slow(x, axis):
    held = {0: x}
    for bit, members in groups_of(axis)[::-1]:
        for r in list(held):
            for k in range(1, members):
                held[r ^ (k * bit)] = across(held[r], axis, k * bit)
    return held


def gather_blocks(x, axis, beside=()):
    held = gather_slow(x, axis)
    order = list(held)
    held[order[-1]], *beside = tie(held[order[-1]], *beside)
    held.update({r ^ 1: across(held[r], axis, 1) for r in order})
    return [held[r] for r in range(len(held))], beside


def gather_cotangent(cotangent, beside):
    size = lax.axis_size("fsdp")
    width = cotangent.shape[2]
    if not (power_of_two(size) and size > 1 and width % 128 == 0):
        return [lax.all_gather(cotangent, "fsdp", axis=2, tiled=True)], [None], [], beside
    held = gather_slow(cotangent, "fsdp")
    *order, last = list(held)
    values = tie(*[held[r] for r in order], *beside)
    held.update(zip(order, values))
    beside = values[len(order) :]
    swapped = [across(held[r], "fsdp", 1) for r in order]
    held[last], *swapped = tie(held[last], *swapped)
    held.update({r ^ 1: x for r, x in zip(order, swapped)})
    begun = begin(held, order, beside[2])
    held[last ^ 1] = across(held[last], "fsdp", 1)
    return [held[r] for r in range(len(held))], [last], [begun], beside


def tie(*values):
    return lax.optimization_barrier(values)


def sums(halved, grams, pairs, p_codes, ranks):
    size = lax.axis_size("fsdp")
    replicas = lax.axis_size("dp")
    if not (power_of_two(size) and size > 1):
        inverse = factor(lax.psum(grams, "fsdp"), ranks)
        ordered = [jnp.stack(pair) for pair in pairs]
        odd = (lax.axis_index("fsdp") & 1) == 1
        whole = jnp.stack([jnp.where(odd, x[::-1], x).reshape(-1, x.shape[2]) for x in ordered])
        codes = [merge([list(lax.psum(whole, ("fsdp", "dp")))], [], "code")]
        return inverse, factor_p_of(halved, inverse, p_codes), codes
    groups = groups_of("fsdp")

    for bit in bits_of("fsdp"):
        grams = grams + across(grams, "fsdp", bit)

    terms = [[mine for mine, _ in pairs], [across(other, "fsdp", 1) for _, other in pairs]]
    codes = []
    for bit, members in groups:
        keep, others = merge(terms, codes, f"part_{bit}", members, bit)
        codes = [across(others[k - 1], "fsdp", k * bit) for k in range(1, members)]
        terms = [keep]
    code = merge(terms, codes, "code")
    if power_of_two(replicas) and replicas > 1:
        theirs = [across(code, "dp", k) for k in range(1, replicas)]
        inverse = factor(grams, ranks)
        *theirs, inverse = tie(*theirs, inverse)
        code = merge([], [code] + theirs, "code_sum")
    else:
        inverse = factor(grams, ranks)
        code = merge([[lax.psum(plain(code), "dp")]], [], "code_sum")
    code, inverse = tie(code, inverse)
    codes, made = gather_blocks(code, "fsdp", factor_p_of(halved, inverse, p_codes))
    return inverse, made, codes


def plain_kernel(code_ref, out_ref):
    out_ref[...] = decode(code_ref)


def plain(code):
    return pl.pallas_call(
        plain_kernel,
        in_specs=[VMEM],
        out_specs=VMEM,
        out_shape=jax.ShapeDtypeStruct((code.shape[0] - GROUPS, code.shape[1]), F32),
        name="plain",
    )(code)


def left_sums(halved, blocks, keys, begun, q2, inputs_t, held, fbq):
    count = fbq.shape[0]
    codes, full_grad, pairs, grams = [], [], [], []
    if not halved:
        pairs_of = [None] if keys == [None] else list(range(0, len(blocks), 2))
        p = lax.psum(jnp.stack([left(m, pairs_of, blocks, q2, inputs_t, fbq) for m in range(count)]), "dp")
        for m in range(count):
            full_grad.append(full(m, held, inputs_t, blocks))
            codes.append(halves_code(p[m]))
            total, part = own_half(m, halved, full_grad[m], codes[m][0])
            *pair, part = other_half(m, halved, full_grad[m], codes[m][1], total, part)
            pairs.append(pair)
            grams.append(part)
        return codes, full_grad, pairs, jnp.stack(grams)
    steps = bits_of("dp")[1:]
    mines = []
    late = blocks if keys == [None] else [blocks[r ^ k] for r in keys for k in range(2)]
    for m in range(count):
        mine, other = left_code(m, keys, begun, late, q2, inputs_t, fbq)
        mines.append(add_code(mine, across(other, "dp", 1)))
    own, late = {}, None
    for m in range(count)[::-1]:
        mine, in_t = tie(mines[m], inputs_t)
        grad = full(m, held, in_t, blocks)
        for bit in steps:
            if late is None:
                theirs, grad = tie(across(mine, "dp", bit), grad)
            else:
                theirs, grad, *own[late] = tie(across(mine, "dp", bit), grad, *own[late])
            mine = add_code(mine, theirs)
        mines[m] = mine
        full_grad.insert(0, grad)
        own[m] = list(own_half(m, halved, grad, mine))
        late = m
    for m in range(count):
        codes.append((mines[m], across(mines[m], "dp", 1)))
        *pair, part = other_half(m, halved, full_grad[m], codes[m][1], *own[m])
        pairs.append(pair)
        grams.append(part)
    return codes, full_grad, pairs, jnp.stack(grams)


def local(inputs, cotangent, feedback, q_init, factor_ranks):
    replicas = lax.axis_size("dp")
    halved = power_of_two(replicas) and replicas > 1
    beside = feedback_q(feedback, q_init, inputs, factor_ranks)
    blocks, keys, begun, (held, fbq, q2, inputs_t) = gather_cotangent(cotangent, beside)
    p_codes, full_grad, pairs, grams = left_sums(halved, blocks, keys, begun, q2, inputs_t, held, fbq)
    inverse, (factor_p, p3), codes = sums(halved, grams, pairs, p_codes, factor_ranks)
    new_error, factor_q = error(full_grad, p3, inverse, codes)
    return (factor_p, factor_q, new_error)


def solution(mesh):
    placed = (P("dp", "fsdp"), P(None, "dp", "fsdp"), P(None, "dp", "fsdp", None), P(), P())
    return jax.shard_map(
        local,
        mesh=mesh,
        in_specs=placed,
        out_specs=(P(None, "fsdp", None), P(), P(None, "dp", "fsdp", None)),
        check_vma=False,
    )
```

```python
import functools

import jax
import jax.numpy as jnp
from jax import lax
from jax.experimental import pallas as pl
from jax.experimental.pallas import tpu as pltpu
from jax.sharding import PartitionSpec as P

F32 = jnp.float32
BF16 = jnp.bfloat16
VMEM = pl.BlockSpec(memory_space=pltpu.VMEM)
SMEM = pl.BlockSpec(memory_space=pltpu.SMEM)
MIB = 1024 * 1024


def halves(x):
    high = x.astype(BF16)
    return high, (x - high.astype(F32)).astype(BF16)


def mm(a, b):
    return jnp.dot(a, b, preferred_element_type=F32)


def mm_nt(a, b):
    return lax.dot_general(a, b, (((1,), (1,)), ((), ())), preferred_element_type=F32)


def params(size, steps=1):
    return pltpu.CompilerParams(
        vmem_limit_bytes=size * MIB, dimension_semantics=("arbitrary",) * steps
    )


def tile_of(rows):
    return min(rows, 256)


def in_vmem(shape, dtype):
    return pltpu.VMEM(shape, dtype)


def stay(x):
    return pltpu.with_memory_space_constraint(x, pltpu.VMEM)


def masked_halves(q, rank):
    column = lax.broadcasted_iota(jnp.int32, q.shape, 1)
    return halves(jnp.where(column < rank, q, 0.0))


def feedback_q_kernel(
    ranks_ref, fb_ref, q_ref, in_ref, held_ref, out_ref, q2_ref, in_t_ref, ranks_own, q_own, in_own, sems, sem_q
):
    count, rows, _ = held_ref.shape
    width = q_ref.shape[2]
    tile = tile_of(rows)
    small = [
        pltpu.make_async_copy(ranks_ref, ranks_own, sem_q.at[0]),
        pltpu.make_async_copy(q_ref, q_own, sem_q.at[1]),
        pltpu.make_async_copy(in_ref, in_own, sem_q.at[2]),
    ]
    copies = []
    small[2].start()
    small[0].start()
    small[1].start()
    for m in range(count):
        for i in range(rows // tile):
            part = pl.ds(i * tile, tile)
            copies.append(
                pltpu.make_async_copy(fb_ref.at[m, 0, part], held_ref.at[m, part], sems.at[len(copies)])
            )
            copies[-1].start()
    small[2].wait()
    in_t_ref[...] = in_own[...].T
    small[0].wait()
    small[1].wait()
    for m in range(count):
        q_high, q_low = masked_halves(q_own[m], ranks_own[m])
        q2_ref[m, :, :width] = q_high
        q2_ref[m, :, width:] = q_low
    for m in range(count):
        for i in range(rows // tile):
            part = pl.ds(i * tile, tile)
            copies[m * (rows // tile) + i].wait()
            high, low = halves(held_ref[m, part])
            both = mm(high, q2_ref[m])
            out_ref[m, part] = both[:, :width] + both[:, width:] + mm(low, q2_ref[m, :, :width])


def feedback_q(feedback, q_init, inputs, ranks):
    count, _, rows, columns = feedback.shape
    width = q_init.shape[2]
    far = pl.BlockSpec(memory_space=pltpu.HBM)
    return pl.pallas_call(
        feedback_q_kernel,
        in_specs=[far] * 4,
        out_specs=[VMEM] * 4,
        out_shape=[
            in_vmem((count, rows, columns), F32),
            in_vmem((count, rows, width), F32),
            in_vmem((count, columns, 2 * width), BF16),
            in_vmem(inputs.shape[::-1], inputs.dtype),
        ],
        scratch_shapes=[
            pltpu.SMEM(ranks.shape, ranks.dtype),
            pltpu.VMEM(q_init.shape, q_init.dtype),
            pltpu.VMEM(inputs.shape, inputs.dtype),
            pltpu.SemaphoreType.DMA((count * (rows // tile_of(rows)),)),
            pltpu.SemaphoreType.DMA((3,)),
        ],
        compiler_params=pltpu.CompilerParams(vmem_limit_bytes=16 * MIB),
        name="feedback_q",
    )(*[pltpu.with_memory_space_constraint(x, pltpu.HBM) for x in (ranks, feedback, q_init, inputs)])


def fill_cotangent(blocks, at, whole_ref):
    if len(blocks) == 1:
        whole_ref[...] = blocks[0][at]
        return
    me = lax.axis_index("fsdp")
    for r, block in enumerate(blocks):
        width = block.shape[2]
        start = pl.multiple_of((me ^ r) * width, width)
        whole_ref[:, pl.ds(start, width)] = block[at]


def cotangent_q(q2_ref, m, pairs, at):
    terms = []
    for r, blocks in pairs:
        if r is None:
            terms.append(mm(blocks[0][at], q2_ref[m]))
            continue
        me = lax.axis_index("fsdp") ^ r
        width = blocks[0].shape[2]
        rows = [q2_ref[m, pl.ds(pl.multiple_of((me ^ k) * width, width), width)] for k in range(2)]
        pair = jnp.concatenate([block[at] for block in blocks], axis=1)
        terms.append(mm(pair, jnp.concatenate(rows, axis=0)))
    return sum(terms[1:], terms[0])


def paired(keys, refs):
    if keys == [None]:
        return [(None, refs)]
    return [(r, refs[2 * i : 2 * i + 2]) for i, r in enumerate(keys)]


def begin_kernel(keys, q2_ref, *refs):
    *blocks, out_ref = refs
    for m in range(out_ref.shape[0]):
        out_ref[m] = cotangent_q(q2_ref, m, paired(keys, blocks), m)


def begin(held, keys, q2):
    blocks = [held[r ^ k] for r in keys for k in range(2)]
    count, tokens, _ = blocks[0].shape
    return pl.pallas_call(
        functools.partial(begin_kernel, keys),
        in_specs=[VMEM] * (1 + len(blocks)),
        out_specs=VMEM,
        out_shape=jax.ShapeDtypeStruct((count, tokens, q2.shape[2]), F32),
        compiler_params=pltpu.CompilerParams(vmem_limit_bytes=16 * MIB),
        name="begin",
    )(q2, *blocks)


def gradient_q(both, inputs_t):
    width = both.shape[1] // 2
    c_high, c_low = halves(both[:, :width] + both[:, width:])
    both = mm(inputs_t, jnp.concatenate([c_high, c_low], axis=1))
    return both[:, :width] + both[:, width:]


def left_kernel(m, keys, q2_ref, in_ref, fbq_ref, *refs):
    *blocks, out_ref = refs
    out_ref[...] = fbq_ref[m] + gradient_q(cotangent_q(q2_ref, m, paired(keys, blocks), m), in_ref[...])


def left(m, keys, blocks, q2, inputs_t, fbq):
    _, rows, width = fbq.shape
    return pl.pallas_call(
        functools.partial(left_kernel, m, keys),
        in_specs=[VMEM] * (3 + len(blocks)),
        out_specs=VMEM,
        out_shape=jax.ShapeDtypeStruct((rows, width), F32),
        compiler_params=pltpu.CompilerParams(vmem_limit_bytes=16 * MIB),
        name=f"left_{m}",
    )(q2, inputs_t, fbq, *blocks)


GROUPS = 16
LANES = 128
NEAR = 3


def encode(x, out_ref):
    rows, width = x.shape
    grouped = x.reshape(GROUPS, rows // GROUPS, width)
    top = jnp.max(jnp.abs(grouped), axis=1)
    level = jnp.ceil(jnp.log(jnp.maximum(top, 1e-30)) * 32.0) + 1.0
    up = jnp.exp(level * (-1.0 / 32.0)) * 32767.0
    code = jnp.round(grouped * up[:, None, :]).reshape(rows, width)
    out_ref[:rows] = code.astype(jnp.int32).astype(jnp.int16)
    out_ref[rows:] = level.astype(jnp.int32).astype(jnp.int16)


def decode(ref):
    rows = ref.shape[0] - GROUPS
    width = ref.shape[1]
    level = ref[rows:].astype(jnp.int32).astype(F32)
    down = jnp.exp(level * (1.0 / 32.0)) * (1.0 / 32767.0)
    code = ref[:rows].astype(jnp.int32).astype(F32).reshape(GROUPS, rows // GROUPS, width)
    return (code * down[:, None, :]).reshape(rows, width)


def decode_part(ref, part, count):
    rows, width = ref.shape[0] - GROUPS, ref.shape[1]
    own, groups = rows // count, GROUPS // count
    level = ref[rows:].astype(jnp.int32).astype(F32)[part * groups : (part + 1) * groups]
    down = jnp.exp(level * (1.0 / 32.0)) * (1.0 / 32767.0)
    code = ref[part * own : (part + 1) * own].astype(jnp.int32).astype(F32)
    return (code.reshape(groups, own // groups, width) * down[:, None, :]).reshape(own, width)


def left_code_kernel(m, keys, q2_ref, in_ref, fbq_ref, *refs):
    *refs, mine_ref, code_ref, p_ref = refs
    if keys == [None]:
        both = cotangent_q(q2_ref, m, paired(keys, refs), m)
    else:
        both = refs[0][m] + cotangent_q(q2_ref, m, paired(keys, refs[1:]), m)
    p = fbq_ref[m] + gradient_q(both, in_ref[...])
    p_ref[...] = p.reshape(p_ref.shape)
    low = lax.axis_index("dp") & 1
    mine_ref[...] = p_ref[low]
    encode(p_ref[1 - low], code_ref)


def left_code(m, keys, begun, blocks, q2, inputs_t, fbq):
    _, rows, width = fbq.shape
    half = rows // 2
    return pl.pallas_call(
        functools.partial(left_code_kernel, m, keys),
        in_specs=[VMEM] * (3 + len(begun) + len(blocks)),
        out_specs=[VMEM] * 2,
        out_shape=[
            jax.ShapeDtypeStruct((half, width), F32),
            jax.ShapeDtypeStruct((half + GROUPS, width), jnp.int16),
        ],
        scratch_shapes=[pltpu.VMEM((2, half, width), F32)],
        compiler_params=pltpu.CompilerParams(vmem_limit_bytes=16 * MIB),
        name=f"left_code_{m}",
    )(q2, inputs_t, fbq, *begun, *blocks)


def add_kernel(mine_ref, theirs_ref, out_ref):
    mine = mine_ref[...] if mine_ref.dtype == F32 else decode(mine_ref)
    encode(mine + decode(theirs_ref), out_ref)


def add_code(mine, theirs):
    return pl.pallas_call(
        add_kernel,
        in_specs=[VMEM, VMEM],
        out_specs=VMEM,
        out_shape=jax.ShapeDtypeStruct(theirs.shape, jnp.int16),
        compiler_params=pltpu.CompilerParams(vmem_limit_bytes=16 * MIB),
        name="add_code",
    )(mine, theirs)


def halves_code_kernel(p_ref, first_ref, second_ref):
    half = p_ref.shape[0] // 2
    encode(p_ref[:half], first_ref)
    encode(p_ref[half:], second_ref)


def halves_code(p):
    code = jax.ShapeDtypeStruct((p.shape[0] // 2 + GROUPS, p.shape[1]), jnp.int16)
    return pl.pallas_call(
        halves_code_kernel,
        in_specs=[VMEM],
        out_specs=[VMEM, VMEM],
        out_shape=[code, code],
        compiler_params=pltpu.CompilerParams(vmem_limit_bytes=16 * MIB),
        name="halves_code",
    )(p)


def full_kernel(m, held_ref, in_ref, *refs):
    *blocks, out_ref, whole_ref = refs
    fill_cotangent(blocks, m, whole_ref)
    rows = out_ref.shape[0]
    tile = tile_of(rows)
    for i in range(rows // tile):
        part = pl.ds(i * tile, tile)
        out_ref[part] = held_ref[m, part] + mm(in_ref[part], whole_ref[...])


def full(m, held, inputs_t, blocks):
    _, rows, columns = held.shape
    return pl.pallas_call(
        functools.partial(full_kernel, m),
        in_specs=[VMEM] * (2 + len(blocks)),
        out_specs=VMEM,
        out_shape=in_vmem((rows, columns), F32),
        scratch_shapes=[pltpu.VMEM((inputs_t.shape[1], columns), BF16)],
        compiler_params=pltpu.CompilerParams(vmem_limit_bytes=16 * MIB),
        name=f"full_{m}",
    )(stay(held), inputs_t, *blocks)


def half_of(halved):
    return lax.axis_index("dp") & 1 if halved else 0


def half_products(full_ref, code_ref, which):
    half, width = code_ref.shape[0] - GROUPS, code_ref.shape[1]
    tile = tile_of(half)
    p = decode(code_ref)
    total = None
    for i in range(half // tile):
        p_high, p_low = halves(p[i * tile : (i + 1) * tile].T)
        start = pl.multiple_of(which * half + i * tile, tile)
        g_high, g_low = halves(full_ref[pl.ds(start, tile)])
        both = mm(jnp.concatenate([p_high, p_low], axis=0), g_high)
        term = both[:width] + both[width:] + mm(p_high, g_low)
        total = term if total is None else total + term
    return total, gram_of(p)


def own_half_kernel(halved, full_ref, code_ref, total_ref, gram_ref):
    total_ref[...], gram_ref[...] = half_products(full_ref, code_ref, half_of(halved))


def own_half(m, halved, full_grad, code):
    width = code.shape[1]
    return pl.pallas_call(
        functools.partial(own_half_kernel, halved),
        in_specs=[VMEM, VMEM],
        out_specs=[VMEM, VMEM],
        out_shape=[
            jax.ShapeDtypeStruct((width, full_grad.shape[1]), F32),
            jax.ShapeDtypeStruct((width, width), F32),
        ],
        compiler_params=pltpu.CompilerParams(vmem_limit_bytes=16 * MIB),
        name=f"own_half_{m}",
    )(stay(full_grad), code)


def other_half_kernel(halved, full_ref, code_ref, total_ref, part_ref, mine_ref, other_ref, gram_ref, both_ref):
    total, gram = half_products(full_ref, code_ref, 1 - half_of(halved))
    gram_ref[...] = part_ref[...] + gram
    total = total_ref[...] + total
    lanes = both_ref.shape[2]
    stacked = [total[:, t : t + lanes] for t in range(0, total.shape[1], lanes)]
    both_ref[...] = jnp.concatenate(stacked, axis=0).reshape(both_ref.shape)
    side = lax.axis_index("fsdp") & 1
    mine_ref[...] = both_ref[side]
    other_ref[...] = both_ref[1 - side]


def other_half(m, halved, full_grad, code, total, part):
    half = total.size // LANES // 2
    return pl.pallas_call(
        functools.partial(other_half_kernel, halved),
        in_specs=[VMEM] * 4,
        out_specs=[VMEM] * 3,
        out_shape=[jax.ShapeDtypeStruct((half, LANES), F32)] * 2 + [jax.ShapeDtypeStruct(part.shape, F32)],
        scratch_shapes=[pltpu.VMEM((2, half, LANES), F32)],
        compiler_params=pltpu.CompilerParams(vmem_limit_bytes=16 * MIB),
        name=f"other_half_{m}",
    )(stay(full_grad), code, total, part)


def tree(values):
    while len(values) > 1:
        values = [sum(values[i : i + 2][1:], values[i]) for i in range(0, len(values), 2)]
    return values[0]


def merge_kernel(count, plain, coded, parts, bit, *refs):
    terms, refs = refs[: plain * count], refs[plain * count :]
    codes, refs = refs[:coded], refs[coded:]
    decoded = [decode(code) for code in codes]
    rows = (decoded[0] if decoded else terms[0]).shape[0] // (count if decoded else 1)
    sums = []
    for m in range(count):
        values = [terms[t * count + m][...] for t in range(plain)]
        values += [value[m * rows : (m + 1) * rows] for value in decoded]
        sums.append(tree(values))
    if parts == 1:
        encode(jnp.concatenate(sums, axis=0), refs[0])
        return
    *outs, cut_ref = refs
    own = (lax.axis_index("fsdp") >> (bit.bit_length() - 1)) & (parts - 1)
    for m in range(count):
        cut_ref[m] = sums[m].reshape(cut_ref.shape[1:])
        outs[m][...] = cut_ref[m, own]
    for r in range(1, parts):
        encode(jnp.concatenate([cut_ref[m, own ^ r] for m in range(count)], axis=0), outs[count + r - 1])


def merge(terms, codes, name, parts=1, bit=1):
    count = len(terms[0]) if terms else 1
    if terms:
        rows = terms[0][0].shape[0]
        lanes = terms[0][0].shape[1]
    else:
        rows = codes[0].shape[0] - GROUPS
        lanes = codes[0].shape[1]
    share = rows // parts
    code = jax.ShapeDtypeStruct((count * share + GROUPS, lanes), jnp.int16)
    plain = [jax.ShapeDtypeStruct((share, lanes), F32)] * count if parts > 1 else []
    outs = plain + [code] * max(parts - 1, 1)
    flat = [x for term in terms for x in term]
    results = pl.pallas_call(
        functools.partial(merge_kernel, count, len(terms), len(codes), parts, bit),
        in_specs=[VMEM] * (len(flat) + len(codes)),
        out_specs=[VMEM] * len(outs),
        out_shape=outs,
        scratch_shapes=[pltpu.VMEM((count, parts, share, lanes), F32)] if parts > 1 else [],
        compiler_params=pltpu.CompilerParams(vmem_limit_bytes=16 * MIB),
        name=name,
    )(*flat, *codes)
    return (results[:count], results[count:]) if parts > 1 else results[0]


def gram_of(p):
    width = p.shape[1]
    high, low = halves(p)
    high_t, low_t = halves(p.T)
    both = mm(high_t, jnp.concatenate([high, low], axis=1))
    return both[:, :width] + both[:, width:] + mm(low_t, high)


def cholesky_inverse(work, n):
    lane = lax.broadcasted_iota(jnp.int32, (8, n), 1)
    sub = lax.broadcasted_iota(jnp.int32, (8, n), 0)
    last = n // 8

    def wide(x):
        return jnp.broadcast_to(x, (8, n))

    def columns_of(x, at):
        return [wide(x[:, at + j : at + j + 1]) for j in range(8)]

    carried = [columns_of(blocks[0], 0) for blocks in work]
    for b in range(last):
        at = 8 * b
        inside = (lane >= at) & (lane < at + 8)
        panels = []
        for columns, blocks in zip(carried, work):
            head = blocks[b]
            scales, lows, tops = [], [], []
            for s in range(8):
                scale = lax.rsqrt(wide(columns[s][s : s + 1, :]))
                low = columns[s] * scale
                for j in range(s + 1, 8):
                    columns[j] = columns[j] - low * wide(low[j : j + 1, :])
                row = jnp.where(lane == at + s, scale, wide(head[s : s + 1, :]) * scale)
                below = jnp.where(lane == at + s, 0.0, head) - low * row
                head = jnp.where(sub > s, below, jnp.where(sub == s, row, head))
                scales.append(scale)
                lows.append(low)
                tops.append(jnp.where((lane > at + s) & (lane < at + 8), 0.0, row))
            blocks[b] = head
            panels.append((scales, lows, tops))
        near = min(b + 1 + NEAR, last)
        for c in range(b + 1, near):
            for i, (blocks, (scales, lows, tops)) in enumerate(zip(work, panels)):
                x = blocks[c]
                columns = columns_of(x, at)
                following = columns_of(x, at + 8) if c == b + 1 else []
                y = jnp.where(inside, 0.0, x)
                for s in range(8):
                    low = columns[s] * scales[s]
                    for j in range(s + 1, 8):
                        columns[j] = columns[j] - low * wide(lows[s][j : j + 1, :])
                    y = y - low * tops[s]
                    following = [f - low * wide(low[j : j + 1, :]) for j, f in enumerate(following)]
                blocks[c] = y
                if following:
                    carried[i] = following
        if near < last:
            for blocks, (scales, lows, tops) in zip(work, panels):
                top = tops[0]
                for s in range(1, 8):
                    top = jnp.where(sub == s, tops[s], top)
                update = lax.dot_general(
                    blocks[b],
                    top,
                    (((0,), (0,)), ((), ())),
                    precision=lax.Precision.HIGHEST,
                    preferred_element_type=F32,
                )
                for c in range(near, last):
                    blocks[c] = jnp.where(inside, 0.0, blocks[c]) - update[8 * c : 8 * c + 8]


def factor_kernel(ranks_ref, gram_ref, inv_ref):
    count, n, _ = inv_ref.shape
    lane = lax.broadcasted_iota(jnp.int32, (8, n), 1)
    sub = lax.broadcasted_iota(jnp.int32, (8, n), 0)
    work = []
    for m in range(count):
        free = jnp.where(lane < ranks_ref[m], 0.0, 1.0)
        blocks = []
        for b in range(n // 8):
            g = gram_ref[m, 8 * b : 8 * b + 8, :]
            blocks.append(jnp.where(lane == sub + 8 * b, g + free, g))
        work.append(blocks)
    cholesky_inverse(work, n)
    for m in range(count):
        for b in range(n // 8):
            inv_ref[m, 8 * b : 8 * b + 8, :] = jnp.where(lane <= sub + 8 * b, work[m][b], 0.0)


def factor(grams, ranks):
    return pl.pallas_call(
        factor_kernel,
        in_specs=[SMEM, VMEM],
        out_specs=VMEM,
        out_shape=jax.ShapeDtypeStruct(grams.shape, F32),
        compiler_params=pltpu.CompilerParams(vmem_limit_bytes=16 * MIB),
        name="factor",
    )(ranks, grams)


def factor_p_kernel(halved, inv_ref, *refs):
    *codes, out_ref, p3_ref, buf_ref, sems = refs
    n = inv_ref.shape[1]
    which = half_of(halved)
    copies = []
    for m in range(inv_ref.shape[0]):
        i_high, i_low = halves(inv_ref[m])
        i_both = jnp.concatenate([i_high, i_low], axis=0)
        for code, place in ((codes[2 * m], which), (codes[2 * m + 1], 1 - which)):
            p_high, p_low = halves(decode(code))
            rows = p_high.shape[0]
            part = pl.ds(pl.multiple_of(place * rows, rows), rows)
            both = mm_nt(p_high, i_both)
            result = both[:, :n] + both[:, n:] + mm_nt(p_low, i_high)
            buf_ref[m, part] = result
            high, low = halves(result)
            p3_ref[m, part] = jnp.concatenate([high, low, high], axis=1)
        copies.append(pltpu.make_async_copy(buf_ref.at[m], out_ref.at[m], sems.at[m]))
        copies[-1].start()
    for copy in copies:
        copy.wait()


def factor_p_of(halved, inverse, codes):
    count, rows, width = len(codes), 2 * (codes[0][0].shape[0] - GROUPS), codes[0][0].shape[1]
    return pl.pallas_call(
        functools.partial(factor_p_kernel, halved),
        in_specs=[VMEM] * (1 + 2 * count),
        out_specs=[pl.BlockSpec(memory_space=pltpu.HBM), VMEM],
        out_shape=[
            jax.ShapeDtypeStruct((count, rows, width), F32),
            in_vmem((count, rows, 3 * width), BF16),
        ],
        scratch_shapes=[pltpu.VMEM((count, rows, width), F32), pltpu.SemaphoreType.DMA((count,))],
        compiler_params=pltpu.CompilerParams(vmem_limit_bytes=16 * MIB),
        name="factor_p",
    )(inverse, *[code for pair in codes for code in pair])


def error_kernel(count, pieces, groups, p3_ref, inv_ref, *refs):
    codes, refs = refs[:pieces], refs[pieces:]
    full_refs, (err_ref, fq_ref, right_ref, q_ref, buf_ref, sems) = refs[:count], refs[count:]
    rows, width = p3_ref.shape[1], inv_ref.shape[1]
    tile = min(rows, LANES)
    share = right_ref.shape[1] // pieces
    me = lax.axis_index("fsdp") if pieces > 1 else 0
    copies = []

    def send_right(m, fq_t):
        q_ref[m] = fq_t.T
        copies.append(pltpu.make_async_copy(q_ref.at[m], fq_ref.at[m], sems.at[len(copies)]))
        copies[-1].start()

    for m in range(count):
        for r, code in enumerate(codes):
            place = (me ^ r) & 1 if pieces > 1 else 0
            for bit, members in groups:
                place = place * members + (((me ^ r) >> (bit.bit_length() - 1)) & (members - 1))
            at = pl.ds(pl.multiple_of(place * share, share), share)
            right_ref[m, at] = decode_part(code, m, count)
        i_high, i_low = halves(inv_ref[m])
        tiles = [right_ref[m, t : t + width] for t in range(0, right_ref.shape[1], width)]
        r_high, r_low = halves(jnp.concatenate(tiles, axis=1))
        both = mm(jnp.concatenate([i_high, i_low], axis=0), r_high)
        fq_t = both[:width] + both[width:] + mm(i_high, r_low)
        q_high, q_low = halves(fq_t)
        q3 = jnp.concatenate([q_high, q_high, q_low], axis=0)
        if m > 0:
            send_right(m, fq_t)
        for start in range(0, rows, tile):
            part = pl.ds(start, tile)
            buf_ref[m, part] = full_refs[m][part] - mm(p3_ref[m, part], q3)
            copies.append(
                pltpu.make_async_copy(buf_ref.at[m, part], err_ref.at[m, 0, part], sems.at[len(copies)])
            )
            copies[-1].start()
        if m == 0:
            send_right(m, fq_t)
    for copy in copies:
        copy.wait()


def error(full_grad, p3, inverse, codes):
    count, rows, _ = p3.shape
    width = inverse.shape[1]
    columns = full_grad[0].shape[1]
    out = pl.BlockSpec(memory_space=pltpu.HBM)
    groups = groups_of("fsdp") if len(codes) > 1 else []
    return pl.pallas_call(
        functools.partial(error_kernel, count, len(codes), groups),
        in_specs=[VMEM] * (2 + len(codes) + count),
        out_specs=[out, out],
        out_shape=[
            jax.ShapeDtypeStruct((count, 1, rows, columns), F32),
            jax.ShapeDtypeStruct((count, columns, width), F32),
        ],
        scratch_shapes=[
            pltpu.VMEM((count, columns * width // LANES, LANES), F32),
            pltpu.VMEM((count, columns, width), F32),
            pltpu.VMEM((count, rows, columns), F32),
            pltpu.SemaphoreType.DMA((count * (rows // min(rows, LANES) + 1),)),
        ],
        compiler_params=pltpu.CompilerParams(vmem_limit_bytes=24 * MIB),
        name="error",
    )(stay(p3), inverse, *codes, *[stay(x) for x in full_grad])


def power_of_two(n):
    return n & (n - 1) == 0


def across(x, axis, bit):
    size = lax.axis_size(axis)
    return lax.ppermute(x, axis, [(i, i ^ bit) for i in range(size)])


def bits_of(axis):
    size = lax.axis_size(axis)
    return [1 << b for b in range(size.bit_length() - 1)]


def groups_of(axis):
    bits = bits_of(axis)[1:]
    return [(bits[i], 1 << len(bits[i : i + 2])) for i in range(0, len(bits), 2)]


def gather_slow(x, axis):
    held = {0: x}
    for bit, members in groups_of(axis)[::-1]:
        for r in list(held):
            for k in range(1, members):
                held[r ^ (k * bit)] = across(held[r], axis, k * bit)
    return held


def gather_blocks(x, axis, beside=()):
    held = gather_slow(x, axis)
    order = list(held)
    held[order[-1]], *beside = tie(held[order[-1]], *beside)
    held.update({r ^ 1: across(held[r], axis, 1) for r in order})
    return [held[r] for r in range(len(held))], beside


def gather_cotangent(cotangent, beside):
    size = lax.axis_size("fsdp")
    width = cotangent.shape[2]
    if not (power_of_two(size) and size > 1 and width % 128 == 0):
        return [lax.all_gather(cotangent, "fsdp", axis=2, tiled=True)], [None], [], beside
    held = gather_slow(cotangent, "fsdp")
    *order, last = list(held)
    values = tie(*[held[r] for r in order], *beside)
    held.update(zip(order, values))
    beside = values[len(order) :]
    swapped = [across(held[r], "fsdp", 1) for r in order]
    held[last], *swapped = tie(held[last], *swapped)
    held.update({r ^ 1: x for r, x in zip(order, swapped)})
    begun = begin(held, order, beside[2])
    held[last ^ 1] = across(held[last], "fsdp", 1)
    return [held[r] for r in range(len(held))], [last], [begun], beside


def tie(*values):
    return lax.optimization_barrier(values)


def sums(halved, grams, pairs, p_codes, ranks):
    size = lax.axis_size("fsdp")
    replicas = lax.axis_size("dp")
    if not (power_of_two(size) and size > 1):
        inverse = factor(lax.psum(grams, "fsdp"), ranks)
        ordered = [jnp.stack(pair) for pair in pairs]
        odd = (lax.axis_index("fsdp") & 1) == 1
        whole = jnp.stack([jnp.where(odd, x[::-1], x).reshape(-1, x.shape[2]) for x in ordered])
        codes = [merge([list(lax.psum(whole, ("fsdp", "dp")))], [], "code")]
        return inverse, factor_p_of(halved, inverse, p_codes), codes
    groups = groups_of("fsdp")

    for bit in bits_of("fsdp"):
        grams = grams + across(grams, "fsdp", bit)

    terms = [[mine for mine, _ in pairs], [across(other, "fsdp", 1) for _, other in pairs]]
    codes = []
    for bit, members in groups:
        keep, others = merge(terms, codes, f"part_{bit}", members, bit)
        codes = [across(others[k - 1], "fsdp", k * bit) for k in range(1, members)]
        terms = [keep]
    code = merge(terms, codes, "code")
    if power_of_two(replicas) and replicas > 1:
        theirs = [across(code, "dp", k) for k in range(1, replicas)]
        inverse = factor(grams, ranks)
        *theirs, inverse = tie(*theirs, inverse)
        code = merge([], [code] + theirs, "code_sum")
    else:
        inverse = factor(grams, ranks)
        code = merge([[lax.psum(plain(code), "dp")]], [], "code_sum")
    code, inverse = tie(code, inverse)
    codes, made = gather_blocks(code, "fsdp", factor_p_of(halved, inverse, p_codes))
    return inverse, made, codes


def plain_kernel(code_ref, out_ref):
    out_ref[...] = decode(code_ref)


def plain(code):
    return pl.pallas_call(
        plain_kernel,
        in_specs=[VMEM],
        out_specs=VMEM,
        out_shape=jax.ShapeDtypeStruct((code.shape[0] - GROUPS, code.shape[1]), F32),
        name="plain",
    )(code)


def left_sums(halved, blocks, keys, begun, q2, inputs_t, held, fbq):
    count = fbq.shape[0]
    codes, full_grad, pairs, grams = [], [], [], []
    if not halved:
        pairs_of = [None] if keys == [None] else list(range(0, len(blocks), 2))
        p = lax.psum(jnp.stack([left(m, pairs_of, blocks, q2, inputs_t, fbq) for m in range(count)]), "dp")
        for m in range(count):
            full_grad.append(full(m, held, inputs_t, blocks))
            codes.append(halves_code(p[m]))
            total, part = own_half(m, halved, full_grad[m], codes[m][0])
            *pair, part = other_half(m, halved, full_grad[m], codes[m][1], total, part)
            pairs.append(pair)
            grams.append(part)
        return codes, full_grad, pairs, jnp.stack(grams)
    steps = bits_of("dp")[1:]
    mines = []
    late = blocks if keys == [None] else [blocks[r ^ k] for r in keys for k in range(2)]
    for m in range(count):
        mine, other = left_code(m, keys, begun, late, q2, inputs_t, fbq)
        mines.append(add_code(mine, across(other, "dp", 1)))
    own, late = {}, None
    for m in range(count)[::-1]:
        mine, in_t = tie(mines[m], inputs_t)
        grad = full(m, held, in_t, blocks)
        for bit in steps:
            if late is None:
                theirs, grad = tie(across(mine, "dp", bit), grad)
            else:
                theirs, grad, *own[late] = tie(across(mine, "dp", bit), grad, *own[late])
            mine = add_code(mine, theirs)
        mines[m] = mine
        full_grad.insert(0, grad)
        own[m] = list(own_half(m, halved, grad, mine))
        late = m
    for m in range(count):
        codes.append((mines[m], across(mines[m], "dp", 1)))
        *pair, part = other_half(m, halved, full_grad[m], codes[m][1], *own[m])
        pairs.append(pair)
        grams.append(part)
    return codes, full_grad, pairs, jnp.stack(grams)


def local(inputs, cotangent, feedback, q_init, factor_ranks):
    replicas = lax.axis_size("dp")
    halved = power_of_two(replicas) and replicas > 1
    beside = feedback_q(feedback, q_init, inputs, factor_ranks)
    blocks, keys, begun, (held, fbq, q2, inputs_t) = gather_cotangent(cotangent, beside)
    p_codes, full_grad, pairs, grams = left_sums(halved, blocks, keys, begun, q2, inputs_t, held, fbq)
    inverse, (factor_p, p3), codes = sums(halved, grams, pairs, p_codes, factor_ranks)
    new_error, factor_q = error(full_grad, p3, inverse, codes)
    return (factor_p, factor_q, new_error)


def solution(mesh):
    placed = (P("dp", "fsdp"), P(None, "dp", "fsdp"), P(None, "dp", "fsdp", None), P(), P())
    return jax.shard_map(
        local,
        mesh=mesh,
        in_specs=placed,
        out_specs=(P(None, "fsdp", None), P(), P(None, "dp", "fsdp", None)),
        check_vma=False,
    )
```
